128 devices in a mesh: wall: 8 (over z, core), depth: 16 (over y, x).
Axes of the slice: x: 4, y: 4, z: 4, core: 2. Of those that a mesh axis runs over, the one named last changes fastest.
Arguments:
- pressure: float32 [8, 256, 1024], P(None, 'depth', 'wall'), may hold values from 0.5 to 2
- layer: int32 [8, 256, 1024], P(None, 'depth', 'wall'), may hold values from 0 to 7
- permeability: float32 [2, 8], replicated, may hold values from 1 to 3
- loading: float32 [8, 256, 1024], P(None, 'depth', 'wall'), may hold values from -6 to 6
- spring: float32 [1024], P('wall'), may hold values from -4 to 4
- contact: int32 [64], P('wall'), may hold values 0 or 1
Outputs:
- pressure_out: float32 [8, 256, 1024], P(None, 'depth', 'wall')
- spring_out: float32 [1024], P('wall')
The draws below stay inside these ranges and needn't reach their ends.
All inputs are finite; a program needn't handle non-finite values. No bound on the sum of `contact` on one device may be relied on, other than what follows from the above.
Results may differ from the reference program's by a relative error of at most 0.0017.
Values sent between devices are 32-bit elements; how exact they have to be, the bound alone decides.
A program may use at most 64 MiB of HBM per device.

```python
import math
import jax
import jax.numpy as jnp
from jax import lax

CROSS = 8
LAYERS = 8
BLOCK = 16
SUBSTEPS = 3
OUTER = 2
NX = 1024
NZ = 256
NBLOCK = 64
VNUM = 512


def with_ends(values, key, least, top_value):
    longest = values.shape.index(max(values.shape))
    spots = []
    for shift in (0, 1):
        where = [jax.random.randint(jax.random.fold_in(key, axis), (), 0, length) for axis, length in enumerate(values.shape)]
        where[longest] = (where[longest] + shift) % values.shape[longest]
        spots.append(tuple(where))
    return values.at[spots[0]].set(least).at[spots[1]].set(top_value)


def level_of(rng, dims, cuts, low, high):
    loudness = 1.0
    for dim, shards_of in cuts:
        steps = jax.random.uniform(jax.random.fold_in(jax.random.fold_in(rng, 6), dim), (shards_of,), jnp.float32, low / len(cuts), high / len(cuts))
        loudness = loudness * jnp.repeat(jnp.exp(steps), dims[dim] // shards_of).reshape((-1,) + (1,) * (len(dims) - 1 - dim))
    return loudness


def bell_draw(rng, shape, deviation, reach, pieces=(), held_as=jnp.bfloat16):
    entries = deviation * jax.random.normal(rng, shape, jnp.float32)
    if pieces:
        entries = entries * level_of(rng, shape, pieces, -0.22, 0.18)
    return jnp.clip(entries, -reach, reach).astype(held_as)


def setup_inputs(seed: int = 0) -> dict:
    key_of = jax.random.split(jax.random.key(seed), 7)
    pressure = jnp.clip(0.5 + 1.5 * jax.random.uniform(key_of[0], (CROSS, NZ, NX), jnp.float32) ** level_of(key_of[0], (CROSS, NZ, NX), ((1, 16), (2, 8)), -0.2, 0.2), 0.5, 2.0)
    layer = with_ends(jax.random.randint(key_of[1], (CROSS, NZ, NX), 0, LAYERS), jax.random.fold_in(key_of[1], 1), 0, LAYERS - 1).astype(jnp.int32)
    permeability = jnp.clip(jnp.exp(jax.random.uniform(key_of[2], (2, LAYERS), jnp.float32, math.log(1.0), math.log(3.0))), 1.0, 3.0)
    loading = bell_draw(key_of[3], (CROSS, NZ, NX), 1.0, 6.0, ((1, 16), (2, 8)), jnp.float32)
    spring = bell_draw(key_of[4], (NX,), 1.0, 4.0, ((0, 8),), jnp.float32)
    contact = with_ends((jax.random.randint(key_of[5], (NBLOCK,), 0, 2) < 1).astype(jnp.int32), jax.random.fold_in(key_of[5], 1), 0, 1)
    return dict(pressure=pressure, layer=layer, permeability=permeability, loading=loading, spring=spring, contact=contact)


ALONG_RATE = 0.1
ACROSS_RATE = 0.06
WALL_GAIN = 1.0
SOURCE_RATE = 1.0
SPRING_KEEP = 0.5
SPRING_DRIVE = 2.0


def lookup(layer, table_row):
    totals = jnp.zeros(layer.shape, jnp.float32)
    for soil_level in range(LAYERS):
        totals = totals + jnp.where(layer == soil_level, table_row[soil_level], jnp.float32(0.0))
    return totals


def harmonic(upper_perm, lower_perm):
    return 2.0 * upper_perm * lower_perm / (upper_perm + lower_perm)


def face_numbers(vertical_perm):
    padded = jnp.pad(vertical_perm, ((0, 0), (1, 1), (0, 0)))
    upward = VNUM * harmonic(padded[:, :-2], padded[:, 1:-1])
    downward = VNUM * harmonic(padded[:, 1:-1], padded[:, 2:])
    first_row = (jnp.arange(vertical_perm.shape[1]) == 0)[None, :, None]
    upward = jnp.where(first_row, VNUM * vertical_perm, upward)
    return upward, downward


def horizontal(field, leftward, rightward, lateral_perm, wall_value, contact_share):
    along = ALONG_RATE * lateral_perm * (leftward + rightward - 2.0 * field)
    change = field[1:] - field[:-1]
    blank = jnp.zeros_like(field[:1])
    across = jnp.concatenate([change, blank], 0) - jnp.concatenate([blank, change], 0)
    wall_flux = contact_share[None, :] * (wall_value[None, :] - field[0])
    wall_term = jnp.concatenate([wall_flux[None], jnp.zeros_like(field[1:])], 0)
    return along + ACROSS_RATE * lateral_perm * (across + wall_term)


def thomas(upward, downward, right_side):
    diagonal = 1.0 + upward + downward

    def forward(carried, column_item):
        slope_prev, offset_prev = carried
        up_coef, down_coef, middle, solved_side = column_item
        pivot_value = middle + up_coef * slope_prev
        slope_now = -down_coef / pivot_value
        offset_now = (solved_side + up_coef * offset_prev) / pivot_value
        return (slope_now, offset_now), (slope_now, offset_now)

    moved = tuple(jnp.moveaxis(field, 1, 0) for field in (upward, downward, diagonal, right_side))
    blank = jnp.zeros(moved[0].shape[1:], jnp.float32)
    _, (slopes, offsets) = lax.scan(forward, (blank, blank), moved)

    def backward(beneath, column_item):
        slope_now, offset_now = column_item
        solved = offset_now - slope_now * beneath
        return solved, solved

    _, values = lax.scan(backward, blank, (slopes, offsets), reverse=True)
    return jnp.moveaxis(values, 0, 1)


def reference(pressure, layer, permeability, loading, spring, contact):
    vertical_perm = lookup(layer, permeability[0])
    lateral_perm = lookup(layer, permeability[1])
    upward, downward = face_numbers(vertical_perm)
    contact_share = jnp.repeat(contact.astype(jnp.float32), BLOCK)
    weights = (jnp.arange(NZ).astype(jnp.float32) + 0.5) / NZ
    field = pressure
    for outer_step in range(OUTER):
        wall_value = WALL_GAIN * spring
        for substep in range(SUBSTEPS):
            blank = jnp.zeros_like(field[..., :1])
            leftward = jnp.concatenate([blank, field[..., :-1]], 2)
            rightward = jnp.concatenate([field[..., 1:], blank], 2)
            right_side = field + horizontal(field, leftward, rightward, lateral_perm, wall_value, contact_share) + SOURCE_RATE * loading
            field = thomas(upward, downward, right_side)
        moment = jnp.sum(weights[:, None] * field[0], axis=0) / NZ
        spring = SPRING_KEEP * spring + SPRING_DRIVE * contact_share * moment
    return field, spring
```

```python
import jax
import jax.numpy as jnp
from jax import lax
from jax.experimental import pallas as pl
from jax.experimental.pallas import tpu as pltpu
from jax.sharding import PartitionSpec as P

MESH = pl.DeviceIdType.MESH
F32 = jnp.float32

SOILS = 8
PANEL = 16
SUBSTEPS = 3
OUTER = 2
VNUM = 512.0
ALONG_RATE = 0.1
ACROSS_RATE = 0.06
SPRING_KEEP = 0.5
SPRING_DRIVE = 2.0

CROSS = 8
ROWS = 16
BLOCKS = 16
OWN = 8
WIDE = 3 * OWN
GROUPS = 3
LANES = 128
LAST = ROWS - 1
MIDDLE = 7
LAYER, PRESSURE, LOADING = 0, 1, 2


def lane_roll(x, shift):
    return pltpu.roll(x, shift % LANES, x.ndim - 1)


def cross_roll(x, shift):
    return pltpu.roll(x, shift % CROSS, x.ndim - 2)


def harmonic(a, b):
    return (2.0 * VNUM) * a * b / (a + b)


def pick(level, table, row):
    value = jnp.full(level.shape, table[row, 0], F32)
    for soil in range(1, SOILS):
        value = jnp.where(level == float(soil), table[row, soil], value)
    return value


def kernel(
    table, contact, pressure, layer, loading, spring,
    pressure_out, spring_out,
    packed, landed, nothing, wall_mine, wall_beside,
    field, source, keep, along, back, ahead, chain, outward, from_prev, from_last,
    reduce_up, reduce_down, reduced_inv, sep_up, sep_down, springs,
    result, returned, spring_row, spring_rows,
    send_sem, land_sem, wall_sem, wall_send, return_send, return_sem, row_send, row_sem,
):
    wall, me = lax.axis_index("wall"), lax.axis_index("depth")
    walls = lax.axis_size("wall")
    has_left, has_right = wall > 0, wall < walls - 1
    first, last = me == 0, me == BLOCKS - 1

    barrier = pltpu.get_barrier_semaphore()

    def greet(k, _):
        pl.semaphore_signal(
            barrier, inc=1, device_id=(wall, lax.rem(me + k, BLOCKS)), device_id_type=MESH
        )
        return 0

    lax.fori_loop(1, BLOCKS, greet, 0)

    @pl.when(first & has_left)
    def _():
        def call(k, _):
            pl.semaphore_signal(barrier, inc=1, device_id=(wall - 1, k), device_id_type=MESH)
            return 0

        lax.fori_loop(0, BLOCKS, call, 0)

    @pl.when(last & has_right)
    def _():
        def call(k, _):
            pl.semaphore_signal(barrier, inc=1, device_id=(wall + 1, k), device_id_type=MESH)
            return 0

        lax.fori_loop(0, BLOCKS, call, 0)

    for which, ref in ((LAYER, layer), (PRESSURE, pressure), (LOADING, loading)):
        flat = ref.reshape(CROSS * ROWS, LANES)
        planes = [flat[pl.ds(z, CROSS, stride=ROWS), :] for z in range(ROWS)]
        packed[which] = jnp.concatenate(planes, 0).astype(F32).T

    lane = lax.broadcasted_iota(jnp.int32, (8, LANES), 1)
    sub = lax.broadcasted_iota(jnp.int32, (8, LANES), 0)
    share = jnp.zeros((8, LANES), F32)
    for panel in range(LANES // PANEL):
        share = jnp.where(lane // PANEL == panel, contact[panel].astype(F32), share)
    own_spring = jnp.broadcast_to(spring[...].reshape(1, LANES), (8, LANES))
    wall_mine[...] = jnp.where(sub == 0, own_spring, share)

    sides = has_left.astype(jnp.int32) + has_right.astype(jnp.int32)
    pl.semaphore_wait(barrier, BLOCKS - 1 + sides)

    def to_peer(which, to, start, size, at, slot):
        return pltpu.make_async_remote_copy(
            src_ref=packed.at[which, pl.ds(start, size)],
            dst_ref=landed.at[which, me, pl.ds(at, size)],
            send_sem=send_sem.at[which, slot],
            recv_sem=land_sem.at[which],
            device_id=to,
            device_id_type=MESH,
        )

    def to_self(which, start, size, at):
        return pltpu.make_async_copy(
            packed.at[which, pl.ds(start, size)],
            landed.at[which, me, pl.ds(at, size)],
            land_sem.at[which],
        )

    def no_column(which, at):
        return pltpu.make_async_copy(
            nothing, landed.at[which, :, pl.ds(at, OWN)], land_sem.at[which]
        )

    def for_each_copy(which, act):
        def deal(k, _):
            to = lax.rem(me + k, BLOCKS)

            @pl.when(to == 0)
            def _():
                act(to_peer(which, (wall, to), 0, 2 * OWN, OWN, k))

            @pl.when(to == BLOCKS - 1)
            def _():
                act(to_peer(which, (wall, to), LANES - 2 * OWN, 2 * OWN, 0, k))

            @pl.when((to > 0) & (to < BLOCKS - 1))
            def _():
                start = pl.multiple_of((to - 1) * OWN, OWN)
                act(to_peer(which, (wall, to), start, WIDE, 0, k))

            return 0

        lax.fori_loop(1, BLOCKS, deal, 0)

        @pl.when(has_right)
        def _():
            act(to_peer(which, (wall + 1, 0), LANES - OWN, OWN, 0, BLOCKS))

        @pl.when(has_left)
        def _():
            act(to_peer(which, (wall - 1, BLOCKS - 1), 0, OWN, 2 * OWN, 0))

    to_right = pltpu.make_async_remote_copy(
        src_ref=wall_mine, dst_ref=wall_beside, send_sem=wall_send.at[0], recv_sem=wall_sem.at[0],
        device_id=(wall + 1, 0), device_id_type=MESH,
    )
    to_left = pltpu.make_async_remote_copy(
        src_ref=wall_mine, dst_ref=wall_beside, send_sem=wall_send.at[1], recv_sem=wall_sem.at[0],
        device_id=(wall - 1, BLOCKS - 1), device_id_type=MESH,
    )
    nothing[...] = jnp.zeros_like(nothing)
    for which in (LAYER, PRESSURE, LOADING):
        for_each_copy(which, lambda copy: copy.start())

        @pl.when(first)
        def _():
            to_self(which, 0, 2 * OWN, OWN).start()

        @pl.when(last)
        def _():
            to_self(which, LANES - 2 * OWN, 2 * OWN, 0).start()

        @pl.when(jnp.logical_not(first | last))
        def _():
            to_self(which, pl.multiple_of((me - 1) * OWN, OWN), WIDE, 0).start()

        @pl.when(first & jnp.logical_not(has_left))
        def _():
            no_column(which, 0).start()

        @pl.when(last & jnp.logical_not(has_right))
        def _():
            no_column(which, 2 * OWN).start()

    @pl.when(first & has_right)
    def _():
        to_right.start()

    @pl.when(last & has_left)
    def _():
        to_left.start()

    wide = (GROUPS, CROSS, LANES)
    lanes = lax.broadcasted_iota(jnp.int32, wide, 2)
    block = lanes // OWN
    column = 3 * (lanes % OWN) + lax.broadcasted_iota(jnp.int32, wide, 0)
    cross = lax.broadcasted_iota(jnp.int32, wide, 1)
    place = wall * LANES + me * OWN - OWN + column
    inside = (place >= 0) & (place < walls * LANES)
    top, bottom = block == 0, block == BLOCKS - 1

    def arrived(which):
        pltpu.make_async_copy(landed.at[which], landed.at[which], land_sem.at[which]).wait()
        for g in range(GROUPS):
            rows = [landed[which, s, pl.ds(g, OWN, stride=GROUPS), :] for s in range(BLOCKS)]
            turned = jnp.concatenate(rows, 0).T.reshape(ROWS, CROSS, LANES)
            field_or = source if which == LOADING else field
            field_or[:, g] = turned

    arrived(LAYER)
    perm = [pick(field[z], table, 0) for z in range(ROWS)]
    up = [None] * ROWS
    for z in range(1, ROWS):
        up[z] = harmonic(perm[z - 1], perm[z])
    up[0] = jnp.where(top, VNUM * perm[0], harmonic(lane_roll(perm[LAST], OWN), perm[0]))
    down = up[1:] + [jnp.where(bottom, 0.0, lane_roll(up[0], -OWN))]
    diagonal = [1.0 + up[z] + down[z] for z in range(ROWS)]

    inverse, toward = [None] * ROWS, [None] * ROWS
    chained = [None] * ROWS
    for z in range(MIDDLE):
        pivot = diagonal[z] if z == 0 else diagonal[z] - up[z] * toward[z - 1]
        inverse[z] = 1.0 / pivot
        toward[z] = down[z] * inverse[z]
        chained[z] = up[z] * inverse[z]
    for z in range(LAST - 1, MIDDLE, -1):
        pivot = diagonal[z] if z == LAST - 1 else diagonal[z] - down[z] * toward[z + 1]
        inverse[z] = 1.0 / pivot
        toward[z] = up[z] * inverse[z]
        chained[z] = down[z] * inverse[z]
    inverse[MIDDLE] = 1.0 / (
        diagonal[MIDDLE] - up[MIDDLE] * toward[MIDDLE - 1] - down[MIDDLE] * toward[MIDDLE + 1]
    )
    chained[MIDDLE] = up[MIDDLE] * inverse[MIDDLE]
    toward[MIDDLE] = down[MIDDLE] * inverse[MIDDLE]
    inverse[LAST] = jnp.ones(wide, F32)

    upper, lower = [None] * LAST, [None] * LAST
    upper[0] = jnp.where(top, 0.0, chained[0])
    for z in range(1, MIDDLE):
        upper[z] = chained[z] * upper[z - 1]
    upper[MIDDLE] = chained[MIDDLE] * upper[MIDDLE - 1]
    for z in range(MIDDLE - 1, -1, -1):
        upper[z] = upper[z] + toward[z] * upper[z + 1]
    for z in range(MIDDLE + 1, LAST):
        upper[z] = toward[z] * upper[z - 1]
    lower[LAST - 1] = chained[LAST - 1]
    for z in range(LAST - 2, MIDDLE, -1):
        lower[z] = chained[z] * lower[z + 1]
    lower[MIDDLE] = toward[MIDDLE] * lower[MIDDLE + 1]
    for z in range(MIDDLE + 1, LAST):
        lower[z] = lower[z] + toward[z] * lower[z - 1]
    for z in range(MIDDLE - 1, -1, -1):
        lower[z] = toward[z] * lower[z + 1]
    for z in range(LAST):
        chain[z], outward[z] = chained[z], toward[z]
        from_prev[z], from_last[z] = upper[z], lower[z]

    a_coef = up[LAST] * upper[LAST - 1]
    c_coef = down[LAST] * lane_roll(lower[0], -OWN)
    b_coef = diagonal[LAST] - up[LAST] * lower[LAST - 1] - down[LAST] * lane_roll(upper[0], -OWN)
    sep_up[...], sep_down[...] = up[LAST], down[LAST]
    for level in range(4):
        hop = OWN << level
        b_inv = 1.0 / b_coef
        alpha = a_coef * lane_roll(b_inv, hop)
        gamma = c_coef * lane_roll(b_inv, -hop)
        reduce_up[level], reduce_down[level] = alpha, gamma
        b_coef = b_coef - alpha * lane_roll(c_coef, hop) - gamma * lane_roll(a_coef, -hop)
        a_coef, c_coef = alpha * lane_roll(a_coef, hop), gamma * lane_roll(c_coef, -hop)
    reduced_inv[...] = 1.0 / b_coef

    @pl.when((first & has_left) | (last & has_right))
    def _():
        pltpu.make_async_copy(wall_beside, wall_beside, wall_sem.at[0]).wait()

    @pl.when(jnp.logical_not((first & has_left) | (last & has_right)))
    def _():
        wall_beside[...] = jnp.zeros_like(wall_beside)

    beside = (first & (lane >= LANES - OWN)) | (last & (lane < OWN))
    window = jnp.where(beside, wall_beside[...], wall_mine[...])
    window = lane_roll_by(window, lax.rem(LANES + OWN - me * OWN, LANES))
    touching = []
    for g in range(GROUPS):
        spread = jnp.take_along_axis(window, 3 * (lane % OWN) + g, axis=1)
        springs[g] = jnp.broadcast_to(spread[0:1], (CROSS, LANES))
        touching.append(jnp.broadcast_to(spread[1:2], (CROSS, LANES)))
    touching = jnp.stack(touching)

    ahead_mask = (cross < CROSS - 1).astype(F32)
    back_mask = jnp.where(cross > 0, 1.0, touching)
    for z in range(ROWS):
        lateral = jnp.where(inside, pick(field[z], table, 1), 0.0)
        a1 = ALONG_RATE * lateral
        a2 = ACROSS_RATE * lateral
        a2b, a2a = a2 * back_mask, a2 * ahead_mask
        keep[z] = (1.0 - 2.0 * a1 - a2b - a2a) * inverse[z]
        along[z], back[z], ahead[z] = a1 * inverse[z], a2b * inverse[z], a2a * inverse[z]
    arrived(LOADING)
    for z in range(ROWS):
        source[z] = source[z] * inverse[z]
    arrived(PRESSURE)

    def solve(_, carry):
        spring_now = springs[...]
        scaled = []
        for z in range(ROWS):
            now = field[z]
            left = jnp.stack([lane_roll(now[2], 1), now[0], now[1]])
            right = jnp.stack([now[1], now[2], lane_roll(now[0], -1)])
            behind = jnp.where(cross == 0, spring_now, cross_roll(now, 1))
            scaled.append(
                source[z] + keep[z] * now + along[z] * (left + right)
                + back[z] * behind + ahead[z] * cross_roll(now, -1)
            )
        for z in range(1, MIDDLE):
            scaled[z] = scaled[z] + chain[z] * scaled[z - 1]
        for z in range(LAST - 2, MIDDLE, -1):
            scaled[z] = scaled[z] + chain[z] * scaled[z + 1]
        scaled[MIDDLE] = (
            scaled[MIDDLE] + chain[MIDDLE] * scaled[MIDDLE - 1] + outward[MIDDLE] * scaled[MIDDLE + 1]
        )
        for z in range(MIDDLE - 1, -1, -1):
            scaled[z] = scaled[z] + outward[z] * scaled[z + 1]
        for z in range(MIDDLE + 1, LAST):
            scaled[z] = scaled[z] + outward[z] * scaled[z - 1]
        ends = (
            scaled[LAST] + sep_up[...] * scaled[LAST - 1]
            + sep_down[...] * lane_roll(scaled[0], -OWN)
        )
        for level in range(4):
            hop = OWN << level
            ends = (
                ends + reduce_up[level] * lane_roll(ends, hop)
                + reduce_down[level] * lane_roll(ends, -hop)
            )
        ends = ends * reduced_inv[...]
        above = lane_roll(ends, OWN)
        for z in range(LAST):
            field[z] = scaled[z] + from_prev[z] * above + from_last[z] * ends
        field[LAST] = ends
        return carry

    def outer_step(_, carry):
        lax.fori_loop(0, SUBSTEPS, solve, 0)
        base = ROWS * block.astype(F32) + 0.5
        moment = jnp.zeros(wide, F32)
        for z in range(ROWS):
            moment = moment + (base + float(z)) * field[z]
        for level in range(4):
            moment = moment + lane_roll(moment, OWN << level)
        moment = moment * (1.0 / (ROWS * BLOCKS) ** 2)
        springs[...] = SPRING_KEEP * springs[...] + SPRING_DRIVE * touching * moment
        return carry

    lax.fori_loop(0, OUTER, outer_step, 0)

    spot = lane % OWN

    def own_columns(planes):
        out = jnp.zeros((8, LANES), F32)
        for place_here in range(OWN):
            at, g = divmod(OWN + place_here, GROUPS)
            out = jnp.where(spot == place_here, lane_roll(planes[g], place_here - at), out)
        return out

    mine = jnp.concatenate([own_columns(field[z]) for z in range(ROWS)], 0)
    result[...] = mine.T.reshape(BLOCKS, OWN, LANES)
    spring_row[...] = own_columns(springs[...])[0:1]

    def give_back(k):
        to = lax.rem(me + k, BLOCKS)
        planes = pltpu.make_async_remote_copy(
            src_ref=result.at[to], dst_ref=returned.at[me],
            send_sem=return_send.at[k], recv_sem=return_sem.at[0],
            device_id=(wall, to), device_id_type=MESH,
        )
        row = pltpu.make_async_remote_copy(
            src_ref=spring_row, dst_ref=spring_rows.at[me],
            send_sem=row_send.at[k], recv_sem=row_sem.at[0],
            device_id=(wall, to), device_id_type=MESH,
        )
        return planes, row

    def start_back(k, _):
        planes, row = give_back(k)
        planes.start()
        row.start()
        return 0

    lax.fori_loop(1, BLOCKS, start_back, 0)
    pltpu.make_async_copy(result.at[me], returned.at[me], return_sem.at[0]).start()
    pltpu.make_async_copy(spring_row, spring_rows.at[me], row_sem.at[0]).start()

    for which in (LAYER, PRESSURE, LOADING):
        for_each_copy(which, lambda copy: copy.wait_send())

    @pl.when(first & has_right)
    def _():
        to_right.wait_send()

    @pl.when(last & has_left)
    def _():
        to_left.wait_send()

    pltpu.make_async_copy(returned, returned, return_sem.at[0]).wait()
    final = returned[...].reshape(LANES, LANES).T
    flat_out = pressure_out.reshape(CROSS * ROWS, LANES)
    for z in range(ROWS):
        flat_out[pl.ds(z, CROSS, stride=ROWS), :] = final[z * CROSS:(z + 1) * CROSS]

    pltpu.make_async_copy(spring_rows, spring_rows, row_sem.at[0]).wait()
    total = jnp.zeros((1, LANES), F32)
    for d in range(BLOCKS):
        total = jnp.where(lane[0:1] // OWN == d, spring_rows[d], total)
    spring_out[...] = total.reshape(spring_out.shape)

    def finish_back(k, _):
        planes, row = give_back(k)
        planes.wait_send()
        row.wait_send()
        return 0

    lax.fori_loop(1, BLOCKS, finish_back, 0)


def lane_roll_by(x, shift):
    return pltpu.roll(x, shift, x.ndim - 1)


def on_device(pressure, layer, permeability, loading, spring, contact):
    vmem = pl.BlockSpec(memory_space=pltpu.VMEM)
    smem = pl.BlockSpec(memory_space=pltpu.SMEM)
    planes = pltpu.VMEM((ROWS, GROUPS, CROSS, LANES), F32)
    plane = pltpu.VMEM((GROUPS, CROSS, LANES), F32)
    steps = pltpu.VMEM((4, GROUPS, CROSS, LANES), F32)
    tile = pltpu.VMEM((8, LANES), F32)
    return pl.pallas_call(
        kernel,
        out_shape=(
            jax.ShapeDtypeStruct(pressure.shape, F32),
            jax.ShapeDtypeStruct(spring.shape, F32),
        ),
        in_specs=[smem, smem, vmem, vmem, vmem, vmem],
        out_specs=(vmem, vmem),
        scratch_shapes=[
            pltpu.VMEM((3, LANES, LANES), F32),
            pltpu.VMEM((3, BLOCKS, WIDE, LANES), F32),
            pltpu.VMEM((BLOCKS, OWN, LANES), F32),
            tile, tile,
            planes, planes, planes, planes, planes, planes,
            planes, planes, planes, planes,
            steps, steps, plane, plane, plane, plane,
            pltpu.VMEM((BLOCKS, OWN, LANES), F32),
            pltpu.VMEM((BLOCKS, OWN, LANES), F32),
            pltpu.VMEM((1, LANES), F32),
            pltpu.VMEM((BLOCKS, 1, LANES), F32),
            pltpu.SemaphoreType.DMA((3, BLOCKS + 1)),
            pltpu.SemaphoreType.DMA((3,)),
            pltpu.SemaphoreType.DMA((1,)),
            pltpu.SemaphoreType.DMA((2,)),
            pltpu.SemaphoreType.DMA((BLOCKS,)),
            pltpu.SemaphoreType.DMA((1,)),
            pltpu.SemaphoreType.DMA((BLOCKS,)),
            pltpu.SemaphoreType.DMA((1,)),
        ],
        compiler_params=pltpu.CompilerParams(
            collective_id=0, has_side_effects=True, vmem_limit_bytes=24 << 20
        ),
    )(permeability, contact, pressure, layer, loading, spring)


def solution(mesh):
    cells = P(None, "depth", "wall")
    return jax.shard_map(
        on_device,
        mesh=mesh,
        in_specs=(cells, cells, P(), cells, P("wall"), P("wall")),
        out_specs=(cells, P("wall")),
        check_vma=False,
    )
```

```python
import jax
import jax.numpy as jnp
from jax import lax
from jax.experimental import pallas as pl
from jax.experimental.pallas import tpu as pltpu
from jax.sharding import PartitionSpec as P

MESH = pl.DeviceIdType.MESH
F32 = jnp.float32

SOILS = 8
PANEL = 16
SUBSTEPS = 3
OUTER = 2
VNUM = 512.0
ALONG_RATE = 0.1
ACROSS_RATE = 0.06
SPRING_KEEP = 0.5
SPRING_DRIVE = 2.0

CROSS = 8
ROWS = 16
BLOCKS = 16
OWN = 8
WIDE = 3 * OWN
GROUPS = 3
LANES = 128
LAST = ROWS - 1
MIDDLE = 7
LAYER, PRESSURE, LOADING = 0, 1, 2
HALO = (5, 6, 5)
SENT = OWN + 1


def lane_roll(x, shift):
    return pltpu.roll(x, shift % LANES, x.ndim - 1)


def cross_roll(x, shift):
    return pltpu.roll(x, shift % CROSS, x.ndim - 2)


def harmonic(a, b):
    return (2.0 * VNUM) * a * b / (a + b)


def pick(level, table, row):
    value = jnp.full(level.shape, table[row, 0], F32)
    for soil in range(1, SOILS):
        value = jnp.where(level == float(soil), table[row, soil], value)
    return value


def kernel(
    table_in, contact_in, pressure_in, layer_in, loading_in, spring_in,
    returned,
    table, contact, pressure, layer, loading, spring, in_sem,
    packed, landed, nothing, wall_mine, wall_beside,
    field, source, keep, along, back, ahead, chain, outward, from_prev, from_last,
    reduce_up, reduce_down, reduced_inv, sep_up, sep_down, springs,
    result,
    send_sem, land_sem, wall_sem, wall_send, return_send, return_sem,
):
    wall, me = lax.axis_index("wall"), lax.axis_index("depth")
    walls = lax.axis_size("wall")
    has_left, has_right = wall > 0, wall < walls - 1
    first, last = me == 0, me == BLOCKS - 1

    inputs = [
        pltpu.make_async_copy(source_ref, here, in_sem.at[at])
        for at, (source_ref, here) in enumerate((
            (layer_in, layer), (pressure_in, pressure), (loading_in, loading),
            (spring_in, spring), (contact_in, contact), (table_in, table),
        ))
    ]
    for copy in inputs:
        copy.start()

    barrier = pltpu.get_barrier_semaphore()

    def greet(k, _):
        pl.semaphore_signal(
            barrier, inc=1, device_id=(wall, lax.rem(me + k, BLOCKS)), device_id_type=MESH
        )
        return 0

    lax.fori_loop(1, BLOCKS, greet, 0)

    @pl.when(first & has_left)
    def _():
        def call(k, _):
            pl.semaphore_signal(barrier, inc=1, device_id=(wall - 1, k), device_id_type=MESH)
            return 0

        lax.fori_loop(0, BLOCKS, call, 0)

    @pl.when(last & has_right)
    def _():
        def call(k, _):
            pl.semaphore_signal(barrier, inc=1, device_id=(wall + 1, k), device_id_type=MESH)
            return 0

        lax.fori_loop(0, BLOCKS, call, 0)

    def pack(which, ref):
        inputs[which].wait()
        flat = ref.reshape(CROSS * ROWS, LANES)
        planes = [flat[pl.ds(z, CROSS, stride=ROWS), :] for z in range(ROWS)]
        packed[which] = jnp.concatenate(planes, 0).astype(F32).T

    def to_peer(which, to, start, size, at, slot):
        return pltpu.make_async_remote_copy(
            src_ref=packed.at[which, pl.ds(start, size)],
            dst_ref=landed.at[which, me, pl.ds(at, size)],
            send_sem=send_sem.at[which, slot],
            recv_sem=land_sem.at[which],
            device_id=to,
            device_id_type=MESH,
        )

    def to_self(which, start, size, at):
        return pltpu.make_async_copy(
            packed.at[which, pl.ds(start, size)],
            landed.at[which, me, pl.ds(at, size)],
            land_sem.at[which],
        )

    def no_column(which, size, at):
        return pltpu.make_async_copy(
            nothing.at[:, pl.ds(0, size)], landed.at[which, :, pl.ds(at, size)], land_sem.at[which]
        )

    def for_each_copy(which, act):
        halo = HALO[which]

        def deal(k, _):
            to = lax.rem(me + k, BLOCKS)

            @pl.when(to == 0)
            def _():
                act(to_peer(which, (wall, to), 0, OWN + halo, OWN, k))

            @pl.when(to == BLOCKS - 1)
            def _():
                act(to_peer(which, (wall, to), LANES - OWN - halo, OWN + halo, OWN - halo, k))

            @pl.when((to > 0) & (to < BLOCKS - 1))
            def _():
                act(to_peer(which, (wall, to), to * OWN - halo, OWN + 2 * halo, OWN - halo, k))

            return 0

        lax.fori_loop(1, BLOCKS, deal, 0)

        @pl.when(has_right)
        def _():
            act(to_peer(which, (wall + 1, 0), LANES - halo, halo, OWN - halo, BLOCKS))

        @pl.when(has_left)
        def _():
            act(to_peer(which, (wall - 1, BLOCKS - 1), 0, halo, 2 * OWN, 0))

    def deal_out(which):
        halo = HALO[which]
        for_each_copy(which, lambda copy: copy.start())

        @pl.when(first)
        def _():
            to_self(which, 0, OWN + halo, OWN).start()

        @pl.when(last)
        def _():
            to_self(which, LANES - OWN - halo, OWN + halo, OWN - halo).start()

        @pl.when(jnp.logical_not(first | last))
        def _():
            to_self(which, me * OWN - halo, OWN + 2 * halo, OWN - halo).start()

        @pl.when(first & jnp.logical_not(has_left))
        def _():
            no_column(which, halo, OWN - halo).start()

        @pl.when(last & jnp.logical_not(has_right))
        def _():
            no_column(which, halo, 2 * OWN).start()

    pack(LAYER, layer)
    nothing[...] = jnp.zeros_like(nothing)
    sides = has_left.astype(jnp.int32) + has_right.astype(jnp.int32)
    pl.semaphore_wait(barrier, BLOCKS - 1 + sides)
    deal_out(LAYER)
    pack(PRESSURE, pressure)
    deal_out(PRESSURE)
    pack(LOADING, loading)
    deal_out(LOADING)

    for copy in inputs[LOADING + 1:]:
        copy.wait()
    lane = lax.broadcasted_iota(jnp.int32, (8, LANES), 1)
    sub = lax.broadcasted_iota(jnp.int32, (8, LANES), 0)
    share = jnp.zeros((8, LANES), F32)
    for panel in range(LANES // PANEL):
        share = jnp.where(lane // PANEL == panel, contact[panel].astype(F32), share)
    own_spring = jnp.broadcast_to(spring[...].reshape(1, LANES), (8, LANES))
    wall_mine[...] = jnp.where(sub == 0, own_spring, share)
    to_right = pltpu.make_async_remote_copy(
        src_ref=wall_mine, dst_ref=wall_beside, send_sem=wall_send.at[0], recv_sem=wall_sem.at[0],
        device_id=(wall + 1, 0), device_id_type=MESH,
    )
    to_left = pltpu.make_async_remote_copy(
        src_ref=wall_mine, dst_ref=wall_beside, send_sem=wall_send.at[1], recv_sem=wall_sem.at[0],
        device_id=(wall - 1, BLOCKS - 1), device_id_type=MESH,
    )

    @pl.when(first & has_right)
    def _():
        to_right.start()

    @pl.when(last & has_left)
    def _():
        to_left.start()

    wide = (GROUPS, CROSS, LANES)
    lanes = lax.broadcasted_iota(jnp.int32, wide, 2)
    block = lanes // OWN
    column = 3 * (lanes % OWN) + lax.broadcasted_iota(jnp.int32, wide, 0)
    cross = lax.broadcasted_iota(jnp.int32, wide, 1)
    place = wall * LANES + me * OWN - OWN + column
    inside = (place >= 0) & (place < walls * LANES)
    top, bottom = block == 0, block == BLOCKS - 1

    def arrived(which):
        valid = landed.at[which, :, pl.ds(OWN - HALO[which], OWN + 2 * HALO[which])]
        pltpu.make_async_copy(valid, valid, land_sem.at[which]).wait()
        for g in range(GROUPS):
            rows = [landed[which, s, pl.ds(g, OWN, stride=GROUPS), :] for s in range(BLOCKS)]
            turned = jnp.concatenate(rows, 0).T.reshape(ROWS, CROSS, LANES)
            field_or = source if which == LOADING else field
            field_or[:, g] = turned

    arrived(LAYER)
    perm = [pick(field[z], table, 0) for z in range(ROWS)]
    up = [None] * ROWS
    for z in range(1, ROWS):
        up[z] = harmonic(perm[z - 1], perm[z])
    up[0] = jnp.where(top, VNUM * perm[0], harmonic(lane_roll(perm[LAST], OWN), perm[0]))
    down = up[1:] + [jnp.where(bottom, 0.0, lane_roll(up[0], -OWN))]
    diagonal = [1.0 + up[z] + down[z] for z in range(ROWS)]

    inverse, toward = [None] * ROWS, [None] * ROWS
    chained = [None] * ROWS
    for z in range(MIDDLE):
        pivot = diagonal[z] if z == 0 else diagonal[z] - up[z] * toward[z - 1]
        inverse[z] = 1.0 / pivot
        toward[z] = down[z] * inverse[z]
        chained[z] = up[z] * inverse[z]
    for z in range(LAST - 1, MIDDLE, -1):
        pivot = diagonal[z] if z == LAST - 1 else diagonal[z] - down[z] * toward[z + 1]
        inverse[z] = 1.0 / pivot
        toward[z] = up[z] * inverse[z]
        chained[z] = down[z] * inverse[z]
    inverse[MIDDLE] = 1.0 / (
        diagonal[MIDDLE] - up[MIDDLE] * toward[MIDDLE - 1] - down[MIDDLE] * toward[MIDDLE + 1]
    )
    chained[MIDDLE] = up[MIDDLE] * inverse[MIDDLE]
    toward[MIDDLE] = down[MIDDLE] * inverse[MIDDLE]
    inverse[LAST] = jnp.ones(wide, F32)

    upper, lower = [None] * LAST, [None] * LAST
    upper[0] = jnp.where(top, 0.0, chained[0])
    for z in range(1, MIDDLE):
        upper[z] = chained[z] * upper[z - 1]
    upper[MIDDLE] = chained[MIDDLE] * upper[MIDDLE - 1]
    for z in range(MIDDLE - 1, -1, -1):
        upper[z] = upper[z] + toward[z] * upper[z + 1]
    for z in range(MIDDLE + 1, LAST):
        upper[z] = toward[z] * upper[z - 1]
    lower[LAST - 1] = chained[LAST - 1]
    for z in range(LAST - 2, MIDDLE, -1):
        lower[z] = chained[z] * lower[z + 1]
    lower[MIDDLE] = toward[MIDDLE] * lower[MIDDLE + 1]
    for z in range(MIDDLE + 1, LAST):
        lower[z] = lower[z] + toward[z] * lower[z - 1]
    for z in range(MIDDLE - 1, -1, -1):
        lower[z] = toward[z] * lower[z + 1]
    for z in range(LAST):
        chain[z], outward[z] = chained[z], toward[z]
        from_prev[z], from_last[z] = upper[z], lower[z]

    a_coef = up[LAST] * upper[LAST - 1]
    c_coef = down[LAST] * lane_roll(lower[0], -OWN)
    b_coef = diagonal[LAST] - up[LAST] * lower[LAST - 1] - down[LAST] * lane_roll(upper[0], -OWN)
    sep_up[...], sep_down[...] = up[LAST], down[LAST]
    for level in range(4):
        hop = OWN << level
        b_inv = 1.0 / b_coef
        alpha = a_coef * lane_roll(b_inv, hop)
        gamma = c_coef * lane_roll(b_inv, -hop)
        reduce_up[level], reduce_down[level] = alpha, gamma
        b_coef = b_coef - alpha * lane_roll(c_coef, hop) - gamma * lane_roll(a_coef, -hop)
        a_coef, c_coef = alpha * lane_roll(a_coef, hop), gamma * lane_roll(c_coef, -hop)
    reduced_inv[...] = 1.0 / b_coef

    @pl.when((first & has_left) | (last & has_right))
    def _():
        pltpu.make_async_copy(wall_beside, wall_beside, wall_sem.at[0]).wait()

    @pl.when(jnp.logical_not((first & has_left) | (last & has_right)))
    def _():
        wall_beside[...] = jnp.zeros_like(wall_beside)

    beside = (first & (lane >= LANES - OWN)) | (last & (lane < OWN))
    window = jnp.where(beside, wall_beside[...], wall_mine[...])
    window = lane_roll_by(window, lax.rem(LANES + OWN - me * OWN, LANES))
    touching = []
    for g in range(GROUPS):
        spread = jnp.take_along_axis(window, 3 * (lane % OWN) + g, axis=1)
        springs[g] = jnp.broadcast_to(spread[0:1], (CROSS, LANES))
        touching.append(jnp.broadcast_to(spread[1:2], (CROSS, LANES)))
    touching = jnp.stack(touching)

    ahead_mask = (cross < CROSS - 1).astype(F32)
    back_mask = jnp.where(cross > 0, 1.0, touching)
    for z in range(ROWS):
        lateral = jnp.where(inside, pick(field[z], table, 1), 0.0)
        a1 = ALONG_RATE * lateral
        a2 = ACROSS_RATE * lateral
        a2b, a2a = a2 * back_mask, a2 * ahead_mask
        keep[z] = (1.0 - 2.0 * a1 - a2b - a2a) * inverse[z]
        along[z], back[z], ahead[z] = a1 * inverse[z], a2b * inverse[z], a2a * inverse[z]
    arrived(LOADING)
    for z in range(ROWS):
        source[z] = source[z] * inverse[z]
    arrived(PRESSURE)

    def solve(_, carry):
        spring_now = springs[...]
        scaled = []
        for z in range(ROWS):
            now = field[z]
            left = jnp.stack([lane_roll(now[2], 1), now[0], now[1]])
            right = jnp.stack([now[1], now[2], lane_roll(now[0], -1)])
            behind = jnp.where(cross == 0, spring_now, cross_roll(now, 1))
            scaled.append(
                source[z] + keep[z] * now + along[z] * (left + right)
                + back[z] * behind + ahead[z] * cross_roll(now, -1)
            )
        for z in range(1, MIDDLE):
            scaled[z] = scaled[z] + chain[z] * scaled[z - 1]
        for z in range(LAST - 2, MIDDLE, -1):
            scaled[z] = scaled[z] + chain[z] * scaled[z + 1]
        scaled[MIDDLE] = (
            scaled[MIDDLE] + chain[MIDDLE] * scaled[MIDDLE - 1] + outward[MIDDLE] * scaled[MIDDLE + 1]
        )
        for z in range(MIDDLE - 1, -1, -1):
            scaled[z] = scaled[z] + outward[z] * scaled[z + 1]
        for z in range(MIDDLE + 1, LAST):
            scaled[z] = scaled[z] + outward[z] * scaled[z - 1]
        ends = (
            scaled[LAST] + sep_up[...] * scaled[LAST - 1]
            + sep_down[...] * lane_roll(scaled[0], -OWN)
        )
        for level in range(4):
            hop = OWN << level
            ends = (
                ends + reduce_up[level] * lane_roll(ends, hop)
                + reduce_down[level] * lane_roll(ends, -hop)
            )
        ends = ends * reduced_inv[...]
        above = lane_roll(ends, OWN)
        for z in range(LAST):
            field[z] = scaled[z] + from_prev[z] * above + from_last[z] * ends
        field[LAST] = ends
        return carry

    def outer_step(_, carry):
        lax.fori_loop(0, SUBSTEPS, solve, 0)
        base = ROWS * block.astype(F32) + 0.5
        moment = jnp.zeros(wide, F32)
        for z in range(ROWS):
            moment = moment + (base + float(z)) * field[z]
        for level in range(4):
            moment = moment + lane_roll(moment, OWN << level)
        moment = moment * (1.0 / (ROWS * BLOCKS) ** 2)
        springs[...] = SPRING_KEEP * springs[...] + SPRING_DRIVE * touching * moment
        return carry

    lax.fori_loop(0, OUTER, outer_step, 0)

    spot = lane % OWN

    def own_columns(planes):
        out = jnp.zeros((8, LANES), F32)
        for place_here in range(OWN):
            at, g = divmod(OWN + place_here, GROUPS)
            out = jnp.where(spot == place_here, lane_roll(planes[g], place_here - at), out)
        return out

    mine = jnp.concatenate([own_columns(field[z]) for z in range(ROWS)], 0)
    result[:, 0:OWN] = mine.T.reshape(BLOCKS, OWN, LANES)
    result[:, OWN:] = jnp.broadcast_to(own_columns(springs[...])[None], (BLOCKS, 8, LANES))

    def give_back(k):
        to = lax.rem(me + k, BLOCKS)
        return pltpu.make_async_remote_copy(
            src_ref=result.at[to, pl.ds(0, SENT)], dst_ref=returned.at[me, pl.ds(0, SENT)],
            send_sem=return_send.at[k], recv_sem=return_sem.at[0],
            device_id=(wall, to), device_id_type=MESH,
        )

    def start_back(k, _):
        give_back(k).start()
        return 0

    lax.fori_loop(1, BLOCKS, start_back, 0)
    pltpu.make_async_copy(
        result.at[me, pl.ds(0, SENT)], returned.at[me, pl.ds(0, SENT)], return_sem.at[0]
    ).start()

    for which in (LAYER, PRESSURE, LOADING):
        for_each_copy(which, lambda copy: copy.wait_send())

    @pl.when(first & has_right)
    def _():
        to_right.wait_send()

    @pl.when(last & has_left)
    def _():
        to_left.wait_send()

    def finish_back(k, _):
        give_back(k).wait_send()
        return 0

    lax.fori_loop(1, BLOCKS, finish_back, 0)
    back_here = returned.at[:, pl.ds(0, SENT)]
    pltpu.make_async_copy(back_here, back_here, return_sem.at[0]).wait()


def place_rows(returned, pressure_out, spring_out):
    planes = returned[:, 0:OWN].reshape(LANES, LANES).T
    flat = pressure_out.reshape(CROSS * ROWS, LANES)
    for z in range(ROWS):
        flat[pl.ds(z, CROSS, stride=ROWS), :] = planes[z * CROSS:(z + 1) * CROSS]
    owner = lax.broadcasted_iota(jnp.int32, (1, LANES), 1) // OWN
    total = jnp.zeros((1, LANES), F32)
    for d in range(BLOCKS):
        total = jnp.where(owner == d, returned[d, OWN:OWN + 1], total)
    spring_out[...] = total.reshape(spring_out.shape)


def lane_roll_by(x, shift):
    return pltpu.roll(x, shift, x.ndim - 1)


def on_device(pressure, layer, permeability, loading, spring, contact):
    vmem = pl.BlockSpec(memory_space=pltpu.VMEM)
    hbm = pl.BlockSpec(memory_space=pltpu.MemorySpace.HBM)
    planes = pltpu.VMEM((ROWS, GROUPS, CROSS, LANES), F32)
    plane = pltpu.VMEM((GROUPS, CROSS, LANES), F32)
    steps = pltpu.VMEM((4, GROUPS, CROSS, LANES), F32)
    tile = pltpu.VMEM((8, LANES), F32)
    returned = pl.pallas_call(
        kernel,
        out_shape=jax.ShapeDtypeStruct((BLOCKS, 2 * OWN, LANES), F32),
        in_specs=[hbm] * 6,
        out_specs=hbm,
        scratch_shapes=[
            pltpu.SMEM(permeability.shape, F32),
            pltpu.SMEM(contact.shape, jnp.int32),
            pltpu.VMEM(pressure.shape, F32),
            pltpu.VMEM(layer.shape, jnp.int32),
            pltpu.VMEM(loading.shape, F32),
            pltpu.VMEM(spring.shape, F32),
            pltpu.SemaphoreType.DMA((6,)),
            pltpu.VMEM((3, LANES, LANES), F32),
            pltpu.VMEM((3, BLOCKS, WIDE, LANES), F32),
            pltpu.VMEM((BLOCKS, OWN, LANES), F32),
            tile, tile,
            planes, planes, planes, planes, planes, planes,
            planes, planes, planes, planes,
            steps, steps, plane, plane, plane, plane,
            pltpu.VMEM((BLOCKS, 2 * OWN, LANES), F32),
            pltpu.SemaphoreType.DMA((3, BLOCKS + 1)),
            pltpu.SemaphoreType.DMA((3,)),
            pltpu.SemaphoreType.DMA((1,)),
            pltpu.SemaphoreType.DMA((2,)),
            pltpu.SemaphoreType.DMA((BLOCKS,)),
            pltpu.SemaphoreType.DMA((1,)),
        ],
        compiler_params=pltpu.CompilerParams(
            collective_id=0, has_side_effects=True, vmem_limit_bytes=60 << 20
        ),
    )(permeability, contact, pressure, layer, loading, spring)
    return pl.pallas_call(
        place_rows,
        out_shape=(
            jax.ShapeDtypeStruct(pressure.shape, F32),
            jax.ShapeDtypeStruct(spring.shape, F32),
        ),
        in_specs=[vmem],
        out_specs=(vmem, vmem),
    )(returned)


def solution(mesh):
    cells = P(None, "depth", "wall")
    return jax.shard_map(
        on_device,
        mesh=mesh,
        in_specs=(cells, cells, P(), cells, P("wall"), P("wall")),
        out_specs=(cells, P("wall")),
        check_vma=False,
    )
```

```python
import jax
import jax.numpy as jnp
from jax import lax
from jax.experimental import pallas as pl
from jax.experimental.pallas import tpu as pltpu
from jax.sharding import PartitionSpec as P

MESH = pl.DeviceIdType.MESH
F32 = jnp.float32

SOILS = 8
PANEL = 16
SUBSTEPS = 3
OUTER = 2
VNUM = 512.0
ALONG_RATE = 0.1
ACROSS_RATE = 0.06
SPRING_KEEP = 0.5
SPRING_DRIVE = 2.0

CROSS = 8
ROWS = 16
BLOCKS = 16
OWN = 8
WIDE = 3 * OWN
GROUPS = 3
LANES = 128
LAST = ROWS - 1
MIDDLE = 7
LAYER, PRESSURE, LOADING = 0, 1, 2
HALO = (5, 6, 5)
SENT = OWN + 1


def lane_roll(x, shift):
    return pltpu.roll(x, shift % LANES, x.ndim - 1)


def cross_roll(x, shift):
    return pltpu.roll(x, shift % CROSS, x.ndim - 2)


def harmonic(a, b):
    return (2.0 * VNUM) * a * b / (a + b)


def pick(level, table, row):
    value = jnp.full(level.shape, table[row, 0], F32)
    for soil in range(1, SOILS):
        value = jnp.where(level == float(soil), table[row, soil], value)
    return value


def kernel(
    table_in, contact_in, pressure_in, layer_in, loading_in, spring_in,
    returned,
    table, contact, pressure, layer, loading, spring, in_sem,
    packed, landed, nothing, wall_mine, wall_beside,
    field, source, keep, along, back, ahead, chain, outward, from_prev, from_last,
    reduce_up, reduce_down, reduced_inv, sep_up, sep_down, springs,
    result,
    send_sem, land_sem, wall_sem, wall_send, return_send, return_sem,
):
    wall, me = lax.axis_index("wall"), lax.axis_index("depth")
    walls = lax.axis_size("wall")
    has_left, has_right = wall > 0, wall < walls - 1
    first, last = me == 0, me == BLOCKS - 1

    inputs = [
        pltpu.make_async_copy(source_ref, here, in_sem.at[at])
        for at, (source_ref, here) in enumerate((
            (layer_in, layer), (pressure_in, pressure), (loading_in, loading),
            (spring_in, spring), (contact_in, contact), (table_in, table),
        ))
    ]
    for copy in inputs:
        copy.start()

    barrier = pltpu.get_barrier_semaphore()

    def greet(k, _):
        pl.semaphore_signal(
            barrier, inc=1, device_id=(wall, lax.rem(me + k, BLOCKS)), device_id_type=MESH
        )
        return 0

    lax.fori_loop(1, BLOCKS, greet, 0)

    @pl.when(first & has_left)
    def _():
        def call(k, _):
            pl.semaphore_signal(barrier, inc=1, device_id=(wall - 1, k), device_id_type=MESH)
            return 0

        lax.fori_loop(0, BLOCKS, call, 0)

    @pl.when(last & has_right)
    def _():
        def call(k, _):
            pl.semaphore_signal(barrier, inc=1, device_id=(wall + 1, k), device_id_type=MESH)
            return 0

        lax.fori_loop(0, BLOCKS, call, 0)

    def pack(which, ref):
        inputs[which].wait()
        flat = ref.reshape(CROSS * ROWS, LANES)
        planes = [flat[pl.ds(z, CROSS, stride=ROWS), :] for z in range(ROWS)]
        packed[which] = jnp.concatenate(planes, 0).astype(F32).T

    def to_peer(which, to, start, size, at, slot):
        return pltpu.make_async_remote_copy(
            src_ref=packed.at[which, pl.ds(start, size)],
            dst_ref=landed.at[which, me, pl.ds(at, size)],
            send_sem=send_sem.at[which, slot],
            recv_sem=land_sem.at[which],
            device_id=to,
            device_id_type=MESH,
        )

    def to_self(which, start, size, at):
        return pltpu.make_async_copy(
            packed.at[which, pl.ds(start, size)],
            landed.at[which, me, pl.ds(at, size)],
            land_sem.at[which],
        )

    def no_column(which, size, at):
        return pltpu.make_async_copy(
            nothing.at[:, pl.ds(0, size)], landed.at[which, :, pl.ds(at, size)], land_sem.at[which]
        )

    def for_each_copy(which, act):
        halo = HALO[which]

        def deal(k, _):
            to = lax.rem(me + k, BLOCKS)

            @pl.when(to == 0)
            def _():
                act(to_peer(which, (wall, to), 0, OWN + halo, OWN, k))

            @pl.when(to == BLOCKS - 1)
            def _():
                act(to_peer(which, (wall, to), LANES - OWN - halo, OWN + halo, OWN - halo, k))

            @pl.when((to > 0) & (to < BLOCKS - 1))
            def _():
                act(to_peer(which, (wall, to), to * OWN - halo, OWN + 2 * halo, OWN - halo, k))

            return 0

        lax.fori_loop(1, BLOCKS, deal, 0)

    def for_each_side(which, act):
        halo = HALO[which]

        @pl.when(has_right)
        def _():
            act(to_peer(which, (wall + 1, 0), LANES - halo, halo, OWN - halo, BLOCKS))

        @pl.when(has_left)
        def _():
            act(to_peer(which, (wall - 1, BLOCKS - 1), 0, halo, 2 * OWN, 0))

    def deal_out(which):
        halo = HALO[which]
        for_each_copy(which, lambda copy: copy.start())

        @pl.when(first)
        def _():
            to_self(which, 0, OWN + halo, OWN).start()

        @pl.when(last)
        def _():
            to_self(which, LANES - OWN - halo, OWN + halo, OWN - halo).start()

        @pl.when(jnp.logical_not(first | last))
        def _():
            to_self(which, me * OWN - halo, OWN + 2 * halo, OWN - halo).start()

        @pl.when(first & jnp.logical_not(has_left))
        def _():
            no_column(which, halo, OWN - halo).start()

        @pl.when(last & jnp.logical_not(has_right))
        def _():
            no_column(which, halo, 2 * OWN).start()

    pack(LAYER, layer)
    pack(PRESSURE, pressure)
    pack(LOADING, loading)
    nothing[...] = jnp.zeros_like(nothing)
    sides = has_left.astype(jnp.int32) + has_right.astype(jnp.int32)
    pl.semaphore_wait(barrier, BLOCKS - 1 + sides)
    for which in (LAYER, PRESSURE, LOADING):
        for_each_side(which, lambda copy: copy.start())
    for which in (LAYER, PRESSURE, LOADING):
        deal_out(which)

    for copy in inputs[LOADING + 1:]:
        copy.wait()
    lane = lax.broadcasted_iota(jnp.int32, (8, LANES), 1)
    sub = lax.broadcasted_iota(jnp.int32, (8, LANES), 0)
    share = jnp.zeros((8, LANES), F32)
    for panel in range(LANES // PANEL):
        share = jnp.where(lane // PANEL == panel, contact[panel].astype(F32), share)
    own_spring = jnp.broadcast_to(spring[...].reshape(1, LANES), (8, LANES))
    wall_mine[...] = jnp.where(sub == 0, own_spring, share)
    to_right = pltpu.make_async_remote_copy(
        src_ref=wall_mine, dst_ref=wall_beside, send_sem=wall_send.at[0], recv_sem=wall_sem.at[0],
        device_id=(wall + 1, 0), device_id_type=MESH,
    )
    to_left = pltpu.make_async_remote_copy(
        src_ref=wall_mine, dst_ref=wall_beside, send_sem=wall_send.at[1], recv_sem=wall_sem.at[0],
        device_id=(wall - 1, BLOCKS - 1), device_id_type=MESH,
    )

    @pl.when(first & has_right)
    def _():
        to_right.start()

    @pl.when(last & has_left)
    def _():
        to_left.start()

    wide = (GROUPS, CROSS, LANES)
    lanes = lax.broadcasted_iota(jnp.int32, wide, 2)
    block = lanes // OWN
    column = 3 * (lanes % OWN) + lax.broadcasted_iota(jnp.int32, wide, 0)
    cross = lax.broadcasted_iota(jnp.int32, wide, 1)
    place = wall * LANES + me * OWN - OWN + column
    inside = (place >= 0) & (place < walls * LANES)
    top, bottom = block == 0, block == BLOCKS - 1

    def arrived(which):
        valid = landed.at[which, :, pl.ds(OWN - HALO[which], OWN + 2 * HALO[which])]
        pltpu.make_async_copy(valid, valid, land_sem.at[which]).wait()
        for g in range(GROUPS):
            rows = [landed[which, s, pl.ds(g, OWN, stride=GROUPS), :] for s in range(BLOCKS)]
            turned = jnp.concatenate(rows, 0).T.reshape(ROWS, CROSS, LANES)
            field_or = source if which == LOADING else field
            field_or[:, g] = turned

    arrived(LAYER)
    perm = [pick(field[z], table, 0) for z in range(ROWS)]
    up = [None] * ROWS
    for z in range(1, ROWS):
        up[z] = harmonic(perm[z - 1], perm[z])
    up[0] = jnp.where(top, VNUM * perm[0], harmonic(lane_roll(perm[LAST], OWN), perm[0]))
    down = up[1:] + [jnp.where(bottom, 0.0, lane_roll(up[0], -OWN))]
    diagonal = [1.0 + up[z] + down[z] for z in range(ROWS)]

    inverse, toward = [None] * ROWS, [None] * ROWS
    chained = [None] * ROWS
    for z in range(MIDDLE):
        pivot = diagonal[z] if z == 0 else diagonal[z] - up[z] * toward[z - 1]
        inverse[z] = 1.0 / pivot
        toward[z] = down[z] * inverse[z]
        chained[z] = up[z] * inverse[z]
    for z in range(LAST - 1, MIDDLE, -1):
        pivot = diagonal[z] if z == LAST - 1 else diagonal[z] - down[z] * toward[z + 1]
        inverse[z] = 1.0 / pivot
        toward[z] = up[z] * inverse[z]
        chained[z] = down[z] * inverse[z]
    inverse[MIDDLE] = 1.0 / (
        diagonal[MIDDLE] - up[MIDDLE] * toward[MIDDLE - 1] - down[MIDDLE] * toward[MIDDLE + 1]
    )
    chained[MIDDLE] = up[MIDDLE] * inverse[MIDDLE]
    toward[MIDDLE] = down[MIDDLE] * inverse[MIDDLE]
    inverse[LAST] = jnp.ones(wide, F32)

    upper, lower = [None] * LAST, [None] * LAST
    upper[0] = jnp.where(top, 0.0, chained[0])
    for z in range(1, MIDDLE):
        upper[z] = chained[z] * upper[z - 1]
    upper[MIDDLE] = chained[MIDDLE] * upper[MIDDLE - 1]
    for z in range(MIDDLE - 1, -1, -1):
        upper[z] = upper[z] + toward[z] * upper[z + 1]
    for z in range(MIDDLE + 1, LAST):
        upper[z] = toward[z] * upper[z - 1]
    lower[LAST - 1] = chained[LAST - 1]
    for z in range(LAST - 2, MIDDLE, -1):
        lower[z] = chained[z] * lower[z + 1]
    lower[MIDDLE] = toward[MIDDLE] * lower[MIDDLE + 1]
    for z in range(MIDDLE + 1, LAST):
        lower[z] = lower[z] + toward[z] * lower[z - 1]
    for z in range(MIDDLE - 1, -1, -1):
        lower[z] = toward[z] * lower[z + 1]
    for z in range(LAST):
        chain[z], outward[z] = chained[z], toward[z]
        from_prev[z], from_last[z] = upper[z], lower[z]

    a_coef = up[LAST] * upper[LAST - 1]
    c_coef = down[LAST] * lane_roll(lower[0], -OWN)
    b_coef = diagonal[LAST] - up[LAST] * lower[LAST - 1] - down[LAST] * lane_roll(upper[0], -OWN)
    sep_up[...], sep_down[...] = up[LAST], down[LAST]
    for level in range(4):
        hop = OWN << level
        b_inv = 1.0 / b_coef
        alpha = a_coef * lane_roll(b_inv, hop)
        gamma = c_coef * lane_roll(b_inv, -hop)
        reduce_up[level], reduce_down[level] = alpha, gamma
        b_coef = b_coef - alpha * lane_roll(c_coef, hop) - gamma * lane_roll(a_coef, -hop)
        a_coef, c_coef = alpha * lane_roll(a_coef, hop), gamma * lane_roll(c_coef, -hop)
    reduced_inv[...] = 1.0 / b_coef

    @pl.when((first & has_left) | (last & has_right))
    def _():
        pltpu.make_async_copy(wall_beside, wall_beside, wall_sem.at[0]).wait()

    @pl.when(jnp.logical_not((first & has_left) | (last & has_right)))
    def _():
        wall_beside[...] = jnp.zeros_like(wall_beside)

    beside = (first & (lane >= LANES - OWN)) | (last & (lane < OWN))
    window = jnp.where(beside, wall_beside[...], wall_mine[...])
    window = lane_roll_by(window, lax.rem(LANES + OWN - me * OWN, LANES))
    touching = []
    for g in range(GROUPS):
        spread = jnp.take_along_axis(window, 3 * (lane % OWN) + g, axis=1)
        springs[g] = jnp.broadcast_to(spread[0:1], (CROSS, LANES))
        touching.append(jnp.broadcast_to(spread[1:2], (CROSS, LANES)))
    touching = jnp.stack(touching)

    ahead_mask = (cross < CROSS - 1).astype(F32)
    back_mask = jnp.where(cross > 0, 1.0, touching)
    for z in range(ROWS):
        lateral = jnp.where(inside, pick(field[z], table, 1), 0.0)
        a1 = ALONG_RATE * lateral
        a2 = ACROSS_RATE * lateral
        a2b, a2a = a2 * back_mask, a2 * ahead_mask
        keep[z] = (1.0 - 2.0 * a1 - a2b - a2a) * inverse[z]
        along[z], back[z], ahead[z] = a1 * inverse[z], a2b * inverse[z], a2a * inverse[z]
    arrived(LOADING)
    for z in range(ROWS):
        source[z] = source[z] * inverse[z]
    arrived(PRESSURE)

    def solve(_, carry):
        spring_now = springs[...]
        scaled = []
        for z in range(ROWS):
            now = field[z]
            left = jnp.stack([lane_roll(now[2], 1), now[0], now[1]])
            right = jnp.stack([now[1], now[2], lane_roll(now[0], -1)])
            behind = jnp.where(cross == 0, spring_now, cross_roll(now, 1))
            scaled.append(
                source[z] + keep[z] * now + along[z] * (left + right)
                + back[z] * behind + ahead[z] * cross_roll(now, -1)
            )
        for z in range(1, MIDDLE):
            scaled[z] = scaled[z] + chain[z] * scaled[z - 1]
        for z in range(LAST - 2, MIDDLE, -1):
            scaled[z] = scaled[z] + chain[z] * scaled[z + 1]
        scaled[MIDDLE] = (
            scaled[MIDDLE] + chain[MIDDLE] * scaled[MIDDLE - 1] + outward[MIDDLE] * scaled[MIDDLE + 1]
        )
        for z in range(MIDDLE - 1, -1, -1):
            scaled[z] = scaled[z] + outward[z] * scaled[z + 1]
        for z in range(MIDDLE + 1, LAST):
            scaled[z] = scaled[z] + outward[z] * scaled[z - 1]
        ends = (
            scaled[LAST] + sep_up[...] * scaled[LAST - 1]
            + sep_down[...] * lane_roll(scaled[0], -OWN)
        )
        for level in range(4):
            hop = OWN << level
            ends = (
                ends + reduce_up[level] * lane_roll(ends, hop)
                + reduce_down[level] * lane_roll(ends, -hop)
            )
        ends = ends * reduced_inv[...]
        above = lane_roll(ends, OWN)
        for z in range(LAST):
            field[z] = scaled[z] + from_prev[z] * above + from_last[z] * ends
        field[LAST] = ends
        return carry

    def outer_step(_, carry):
        lax.fori_loop(0, SUBSTEPS, solve, 0)
        base = ROWS * block.astype(F32) + 0.5
        moment = jnp.zeros(wide, F32)
        for z in range(ROWS):
            moment = moment + (base + float(z)) * field[z]
        for level in range(4):
            moment = moment + lane_roll(moment, OWN << level)
        moment = moment * (1.0 / (ROWS * BLOCKS) ** 2)
        springs[...] = SPRING_KEEP * springs[...] + SPRING_DRIVE * touching * moment
        return carry

    lax.fori_loop(0, OUTER, outer_step, 0)

    spot = lane % OWN

    def own_columns(planes):
        out = jnp.zeros((8, LANES), F32)
        for place_here in range(OWN):
            at, g = divmod(OWN + place_here, GROUPS)
            out = jnp.where(spot == place_here, lane_roll(planes[g], place_here - at), out)
        return out

    mine = jnp.concatenate([own_columns(field[z]) for z in range(ROWS)], 0)
    result[:, 0:OWN] = mine.T.reshape(BLOCKS, OWN, LANES)
    result[:, OWN:] = jnp.broadcast_to(own_columns(springs[...])[None], (BLOCKS, 8, LANES))

    def give_back(k):
        to = lax.rem(me + k, BLOCKS)
        return pltpu.make_async_remote_copy(
            src_ref=result.at[to, pl.ds(0, SENT)], dst_ref=returned.at[me, pl.ds(0, SENT)],
            send_sem=return_send.at[k], recv_sem=return_sem.at[0],
            device_id=(wall, to), device_id_type=MESH,
        )

    def start_back(k, _):
        give_back(k).start()
        return 0

    lax.fori_loop(1, BLOCKS, start_back, 0)
    pltpu.make_async_copy(
        result.at[me, pl.ds(0, SENT)], returned.at[me, pl.ds(0, SENT)], return_sem.at[0]
    ).start()

    for which in (LAYER, PRESSURE, LOADING):
        for_each_side(which, lambda copy: copy.wait_send())
        for_each_copy(which, lambda copy: copy.wait_send())

    @pl.when(first & has_right)
    def _():
        to_right.wait_send()

    @pl.when(last & has_left)
    def _():
        to_left.wait_send()

    def finish_back(k, _):
        give_back(k).wait_send()
        return 0

    lax.fori_loop(1, BLOCKS, finish_back, 0)
    back_here = returned.at[:, pl.ds(0, SENT)]
    pltpu.make_async_copy(back_here, back_here, return_sem.at[0]).wait()


def place_rows(returned, pressure_out, spring_out):
    planes = returned[:, 0:OWN].reshape(LANES, LANES).T
    flat = pressure_out.reshape(CROSS * ROWS, LANES)
    for z in range(ROWS):
        flat[pl.ds(z, CROSS, stride=ROWS), :] = planes[z * CROSS:(z + 1) * CROSS]
    owner = lax.broadcasted_iota(jnp.int32, (1, LANES), 1) // OWN
    total = jnp.zeros((1, LANES), F32)
    for d in range(BLOCKS):
        total = jnp.where(owner == d, returned[d, OWN:OWN + 1], total)
    spring_out[...] = total.reshape(spring_out.shape)


def lane_roll_by(x, shift):
    return pltpu.roll(x, shift, x.ndim - 1)


def on_device(pressure, layer, permeability, loading, spring, contact):
    vmem = pl.BlockSpec(memory_space=pltpu.VMEM)
    hbm = pl.BlockSpec(memory_space=pltpu.MemorySpace.HBM)
    planes = pltpu.VMEM((ROWS, GROUPS, CROSS, LANES), F32)
    plane = pltpu.VMEM((GROUPS, CROSS, LANES), F32)
    steps = pltpu.VMEM((4, GROUPS, CROSS, LANES), F32)
    tile = pltpu.VMEM((8, LANES), F32)
    returned = pl.pallas_call(
        kernel,
        out_shape=jax.ShapeDtypeStruct((BLOCKS, 2 * OWN, LANES), F32),
        in_specs=[hbm] * 6,
        out_specs=hbm,
        scratch_shapes=[
            pltpu.SMEM(permeability.shape, F32),
            pltpu.SMEM(contact.shape, jnp.int32),
            pltpu.VMEM(pressure.shape, F32),
            pltpu.VMEM(layer.shape, jnp.int32),
            pltpu.VMEM(loading.shape, F32),
            pltpu.VMEM(spring.shape, F32),
            pltpu.SemaphoreType.DMA((6,)),
            pltpu.VMEM((3, LANES, LANES), F32),
            pltpu.VMEM((3, BLOCKS, WIDE, LANES), F32),
            pltpu.VMEM((BLOCKS, OWN, LANES), F32),
            tile, tile,
            planes, planes, planes, planes, planes, planes,
            planes, planes, planes, planes,
            steps, steps, plane, plane, plane, plane,
            pltpu.VMEM((BLOCKS, 2 * OWN, LANES), F32),
            pltpu.SemaphoreType.DMA((3, BLOCKS + 1)),
            pltpu.SemaphoreType.DMA((3,)),
            pltpu.SemaphoreType.DMA((1,)),
            pltpu.SemaphoreType.DMA((2,)),
            pltpu.SemaphoreType.DMA((BLOCKS,)),
            pltpu.SemaphoreType.DMA((1,)),
        ],
        compiler_params=pltpu.CompilerParams(
            collective_id=0, has_side_effects=True, vmem_limit_bytes=60 << 20
        ),
    )(permeability, contact, pressure, layer, loading, spring)
    return pl.pallas_call(
        place_rows,
        out_shape=(
            jax.ShapeDtypeStruct(pressure.shape, F32),
            jax.ShapeDtypeStruct(spring.shape, F32),
        ),
        in_specs=[vmem],
        out_specs=(vmem, vmem),
    )(returned)


def solution(mesh):
    cells = P(None, "depth", "wall")
    return jax.shard_map(
        on_device,
        mesh=mesh,
        in_specs=(cells, cells, P(), cells, P("wall"), P("wall")),
        out_specs=(cells, P("wall")),
        check_vma=False,
    )
```

```python
import jax
import jax.numpy as jnp
from jax import lax
from jax.experimental import pallas as pl
from jax.experimental.pallas import tpu as pltpu
from jax.sharding import PartitionSpec as P

MESH = pl.DeviceIdType.MESH
F32 = jnp.float32

SOILS = 8
PANEL = 16
SUBSTEPS = 3
OUTER = 2
VNUM = 512.0
ALONG_RATE = 0.1
ACROSS_RATE = 0.06
SPRING_KEEP = 0.5
SPRING_DRIVE = 2.0

CROSS = 8
ROWS = 16
BLOCKS = 16
OWN = 8
WIDE = 3 * OWN
GROUPS = 3
LANES = 128
LAST = ROWS - 1
MIDDLE = 7
LAYER, PRESSURE, LOADING = 0, 1, 2
HALO = (5, 6, 5)
WIDTHS = tuple(OWN + 2 * halo for halo in HALO)
SIDE = 4
FAR_FIRST = sorted(
    ((dy, dx) for dy in range(SIDE) for dx in range(SIDE) if dy or dx),
    key=lambda at: -sum(min(step, SIDE - step) for step in at),
)
SENT = OWN + 1


def lane_roll(x, shift):
    return pltpu.roll(x, shift % LANES, x.ndim - 1)


def cross_roll(x, shift):
    return pltpu.roll(x, shift % CROSS, x.ndim - 2)


def harmonic(a, b):
    return (2.0 * VNUM) * a * b / (a + b)


def pick(level, table, row):
    value = jnp.full(level.shape, table[row, 0], F32)
    for soil in range(1, SOILS):
        value = jnp.where(level == float(soil), table[row, soil], value)
    return value


def kernel(
    table_in, contact_in, pressure_in, layer_in, loading_in, spring_in,
    returned,
    table, contact, pressure, layer, loading, spring, in_sem,
    packed, landed, beyond, wall_mine, wall_beside,
    field, source, keep, along, back, ahead, chain, outward, from_prev, from_last,
    reduce_up, reduce_down, reduced_inv, sep_up, sep_down, springs,
    result,
    send_sem, land_sem, side_send, side_sem, wall_sem, wall_send, return_send, return_sem,
):
    wall, me = lax.axis_index("wall"), lax.axis_index("depth")
    walls = lax.axis_size("wall")
    has_left, has_right = wall > 0, wall < walls - 1
    first, last = me == 0, me == BLOCKS - 1

    inputs = [
        pltpu.make_async_copy(source_ref, here, in_sem.at[at])
        for at, (source_ref, here) in enumerate((
            (layer_in, layer), (pressure_in, pressure), (loading_in, loading),
            (spring_in, spring), (contact_in, contact), (table_in, table),
        ))
    ]
    for copy in inputs:
        copy.start()

    peers = [
        lax.rem(me // SIDE + dy, SIDE) * SIDE + lax.rem(me % SIDE + dx, SIDE) for dy, dx in FAR_FIRST
    ]

    barrier = pltpu.get_barrier_semaphore()
    for peer in peers:
        pl.semaphore_signal(barrier, inc=1, device_id=(wall, peer), device_id_type=MESH)

    @pl.when(first & has_left)
    def _():
        def call(k, _):
            pl.semaphore_signal(barrier, inc=1, device_id=(wall - 1, k), device_id_type=MESH)
            return 0

        lax.fori_loop(0, BLOCKS, call, 0)

    @pl.when(last & has_right)
    def _():
        def call(k, _):
            pl.semaphore_signal(barrier, inc=1, device_id=(wall + 1, k), device_id_type=MESH)
            return 0

        lax.fori_loop(0, BLOCKS, call, 0)

    def pack(which, ref):
        inputs[which].wait()
        flat = ref.reshape(CROSS * ROWS, LANES)
        planes = [flat[pl.ds(z, CROSS, stride=ROWS), :] for z in range(ROWS)]
        packed[which, OWN:OWN + LANES] = jnp.concatenate(planes, 0).astype(F32).T

    def to_peer(which, peer):
        width = OWN + 2 * HALO[which]
        return pltpu.make_async_remote_copy(
            src_ref=packed.at[which, pl.ds(peer * OWN + OWN - HALO[which], width)],
            dst_ref=landed.at[which, me, pl.ds(OWN - HALO[which], width)],
            send_sem=send_sem.at[0], recv_sem=land_sem.at[which],
            device_id=(wall, peer), device_id_type=MESH,
        )

    def to_self(which):
        width = OWN + 2 * HALO[which]
        return pltpu.make_async_copy(
            packed.at[which, pl.ds(me * OWN + OWN - HALO[which], width)],
            landed.at[which, me, pl.ds(OWN - HALO[which], width)],
            land_sem.at[which],
        )

    def to_right(which):
        return pltpu.make_async_remote_copy(
            src_ref=packed.at[which, pl.ds(OWN + LANES - HALO[which], HALO[which])],
            dst_ref=beyond.at[which, me, pl.ds(OWN - HALO[which], HALO[which])],
            send_sem=side_send.at[0, which], recv_sem=side_sem.at[which],
            device_id=(wall + 1, 0), device_id_type=MESH,
        )

    def to_left(which):
        return pltpu.make_async_remote_copy(
            src_ref=packed.at[which, pl.ds(OWN, HALO[which])],
            dst_ref=beyond.at[which, me, pl.ds(0, HALO[which])],
            send_sem=side_send.at[1, which], recv_sem=side_sem.at[which],
            device_id=(wall - 1, BLOCKS - 1), device_id_type=MESH,
        )

    for which in (LAYER, PRESSURE, LOADING):
        packed[which, 0:OWN] = jnp.zeros((OWN, LANES), F32)
        packed[which, OWN + LANES:] = jnp.zeros((OWN, LANES), F32)
    pack(LAYER, layer)
    pack(PRESSURE, pressure)
    pack(LOADING, loading)
    sides = has_left.astype(jnp.int32) + has_right.astype(jnp.int32)
    pl.semaphore_wait(barrier, BLOCKS - 1 + sides)

    @pl.when(has_right)
    def _():
        for which in (LAYER, PRESSURE, LOADING):
            to_right(which).start()

    @pl.when(has_left)
    def _():
        for which in (LAYER, PRESSURE, LOADING):
            to_left(which).start()

    for peer in peers:
        to_peer(LAYER, peer).start()
    for peer in peers:
        to_peer(PRESSURE, peer).start()
        to_peer(LOADING, peer).start()
    for which in (LAYER, PRESSURE, LOADING):
        to_self(which).start()

    for copy in inputs[LOADING + 1:]:
        copy.wait()
    lane = lax.broadcasted_iota(jnp.int32, (8, LANES), 1)
    sub = lax.broadcasted_iota(jnp.int32, (8, LANES), 0)
    share = jnp.zeros((8, LANES), F32)
    for panel in range(LANES // PANEL):
        share = jnp.where(lane // PANEL == panel, contact[panel].astype(F32), share)
    own_spring = jnp.broadcast_to(spring[...].reshape(1, LANES), (8, LANES))
    wall_mine[...] = jnp.where(sub == 0, own_spring, share)
    wall_right = pltpu.make_async_remote_copy(
        src_ref=wall_mine, dst_ref=wall_beside, send_sem=wall_send.at[0], recv_sem=wall_sem.at[0],
        device_id=(wall + 1, 0), device_id_type=MESH,
    )
    wall_left = pltpu.make_async_remote_copy(
        src_ref=wall_mine, dst_ref=wall_beside, send_sem=wall_send.at[1], recv_sem=wall_sem.at[0],
        device_id=(wall - 1, BLOCKS - 1), device_id_type=MESH,
    )

    @pl.when(first & has_right)
    def _():
        wall_right.start()

    @pl.when(last & has_left)
    def _():
        wall_left.start()

    wide = (GROUPS, CROSS, LANES)
    lanes = lax.broadcasted_iota(jnp.int32, wide, 2)
    block = lanes // OWN
    column = 3 * (lanes % OWN) + lax.broadcasted_iota(jnp.int32, wide, 0)
    cross = lax.broadcasted_iota(jnp.int32, wide, 1)
    place = wall * LANES + me * OWN - OWN + column
    inside = (place >= 0) & (place < walls * LANES)
    top, bottom = block == 0, block == BLOCKS - 1

    def arrived(which):
        valid = landed.at[which, :, pl.ds(OWN - HALO[which], OWN + 2 * HALO[which])]
        pltpu.make_async_copy(valid, valid, land_sem.at[which]).wait()

        @pl.when((first & has_left) | (last & has_right))
        def _():
            strip = beyond.at[which, :, pl.ds(0, HALO[which])]
            pltpu.make_async_copy(strip, strip, side_sem.at[which]).wait()

        @pl.when(first)
        def _():
            landed[which, :, 0:OWN] = jnp.where(has_left, beyond[which], 0.0)

        @pl.when(last)
        def _():
            landed[which, :, 2 * OWN:] = jnp.where(has_right, beyond[which], 0.0)

        for g in range(GROUPS):
            rows = [landed[which, s, pl.ds(g, OWN, stride=GROUPS), :] for s in range(BLOCKS)]
            turned = jnp.concatenate(rows, 0).T.reshape(ROWS, CROSS, LANES)
            field_or = source if which == LOADING else field
            field_or[:, g] = turned

    arrived(LAYER)
    perm = [pick(field[z], table, 0) for z in range(ROWS)]
    up = [None] * ROWS
    for z in range(1, ROWS):
        up[z] = harmonic(perm[z - 1], perm[z])
    up[0] = jnp.where(top, VNUM * perm[0], harmonic(lane_roll(perm[LAST], OWN), perm[0]))
    down = up[1:] + [jnp.where(bottom, 0.0, lane_roll(up[0], -OWN))]
    diagonal = [1.0 + up[z] + down[z] for z in range(ROWS)]

    inverse, toward = [None] * ROWS, [None] * ROWS
    chained = [None] * ROWS
    for z in range(MIDDLE):
        pivot = diagonal[z] if z == 0 else diagonal[z] - up[z] * toward[z - 1]
        inverse[z] = 1.0 / pivot
        toward[z] = down[z] * inverse[z]
        chained[z] = up[z] * inverse[z]
    for z in range(LAST - 1, MIDDLE, -1):
        pivot = diagonal[z] if z == LAST - 1 else diagonal[z] - down[z] * toward[z + 1]
        inverse[z] = 1.0 / pivot
        toward[z] = up[z] * inverse[z]
        chained[z] = down[z] * inverse[z]
    inverse[MIDDLE] = 1.0 / (
        diagonal[MIDDLE] - up[MIDDLE] * toward[MIDDLE - 1] - down[MIDDLE] * toward[MIDDLE + 1]
    )
    chained[MIDDLE] = up[MIDDLE] * inverse[MIDDLE]
    toward[MIDDLE] = down[MIDDLE] * inverse[MIDDLE]
    inverse[LAST] = jnp.ones(wide, F32)

    upper, lower = [None] * LAST, [None] * LAST
    upper[0] = jnp.where(top, 0.0, chained[0])
    for z in range(1, MIDDLE):
        upper[z] = chained[z] * upper[z - 1]
    upper[MIDDLE] = chained[MIDDLE] * upper[MIDDLE - 1]
    for z in range(MIDDLE - 1, -1, -1):
        upper[z] = upper[z] + toward[z] * upper[z + 1]
    for z in range(MIDDLE + 1, LAST):
        upper[z] = toward[z] * upper[z - 1]
    lower[LAST - 1] = chained[LAST - 1]
    for z in range(LAST - 2, MIDDLE, -1):
        lower[z] = chained[z] * lower[z + 1]
    lower[MIDDLE] = toward[MIDDLE] * lower[MIDDLE + 1]
    for z in range(MIDDLE + 1, LAST):
        lower[z] = lower[z] + toward[z] * lower[z - 1]
    for z in range(MIDDLE - 1, -1, -1):
        lower[z] = toward[z] * lower[z + 1]
    for z in range(LAST):
        chain[z], outward[z] = chained[z], toward[z]
        from_prev[z], from_last[z] = upper[z], lower[z]

    a_coef = up[LAST] * upper[LAST - 1]
    c_coef = down[LAST] * lane_roll(lower[0], -OWN)
    b_coef = diagonal[LAST] - up[LAST] * lower[LAST - 1] - down[LAST] * lane_roll(upper[0], -OWN)
    sep_up[...], sep_down[...] = up[LAST], down[LAST]
    for level in range(4):
        hop = OWN << level
        b_inv = 1.0 / b_coef
        alpha = a_coef * lane_roll(b_inv, hop)
        gamma = c_coef * lane_roll(b_inv, -hop)
        reduce_up[level], reduce_down[level] = alpha, gamma
        b_coef = b_coef - alpha * lane_roll(c_coef, hop) - gamma * lane_roll(a_coef, -hop)
        a_coef, c_coef = alpha * lane_roll(a_coef, hop), gamma * lane_roll(c_coef, -hop)
    reduced_inv[...] = 1.0 / b_coef

    @pl.when((first & has_left) | (last & has_right))
    def _():
        pltpu.make_async_copy(wall_beside, wall_beside, wall_sem.at[0]).wait()

    @pl.when(jnp.logical_not((first & has_left) | (last & has_right)))
    def _():
        wall_beside[...] = jnp.zeros_like(wall_beside)

    beside = (first & (lane >= LANES - OWN)) | (last & (lane < OWN))
    window = jnp.where(beside, wall_beside[...], wall_mine[...])
    window = lane_roll_by(window, lax.rem(LANES + OWN - me * OWN, LANES))
    touching = []
    for g in range(GROUPS):
        spread = jnp.take_along_axis(window, 3 * (lane % OWN) + g, axis=1)
        springs[g] = jnp.broadcast_to(spread[0:1], (CROSS, LANES))
        touching.append(jnp.broadcast_to(spread[1:2], (CROSS, LANES)))
    touching = jnp.stack(touching)

    ahead_mask = (cross < CROSS - 1).astype(F32)
    back_mask = jnp.where(cross > 0, 1.0, touching)
    for z in range(ROWS):
        lateral = jnp.where(inside, pick(field[z], table, 1), 0.0)
        a1 = ALONG_RATE * lateral
        a2 = ACROSS_RATE * lateral
        a2b, a2a = a2 * back_mask, a2 * ahead_mask
        keep[z] = (1.0 - 2.0 * a1 - a2b - a2a) * inverse[z]
        along[z], back[z], ahead[z] = a1 * inverse[z], a2b * inverse[z], a2a * inverse[z]
    arrived(LOADING)
    for z in range(ROWS):
        source[z] = source[z] * inverse[z]
    arrived(PRESSURE)

    def solve(_, carry):
        spring_now = springs[...]
        scaled = []
        for z in range(ROWS):
            now = field[z]
            left = jnp.stack([lane_roll(now[2], 1), now[0], now[1]])
            right = jnp.stack([now[1], now[2], lane_roll(now[0], -1)])
            behind = jnp.where(cross == 0, spring_now, cross_roll(now, 1))
            scaled.append(
                source[z] + keep[z] * now + along[z] * (left + right)
                + back[z] * behind + ahead[z] * cross_roll(now, -1)
            )
        for z in range(1, MIDDLE):
            scaled[z] = scaled[z] + chain[z] * scaled[z - 1]
        for z in range(LAST - 2, MIDDLE, -1):
            scaled[z] = scaled[z] + chain[z] * scaled[z + 1]
        scaled[MIDDLE] = (
            scaled[MIDDLE] + chain[MIDDLE] * scaled[MIDDLE - 1] + outward[MIDDLE] * scaled[MIDDLE + 1]
        )
        for z in range(MIDDLE - 1, -1, -1):
            scaled[z] = scaled[z] + outward[z] * scaled[z + 1]
        for z in range(MIDDLE + 1, LAST):
            scaled[z] = scaled[z] + outward[z] * scaled[z - 1]
        ends = (
            scaled[LAST] + sep_up[...] * scaled[LAST - 1]
            + sep_down[...] * lane_roll(scaled[0], -OWN)
        )
        for level in range(4):
            hop = OWN << level
            ends = (
                ends + reduce_up[level] * lane_roll(ends, hop)
                + reduce_down[level] * lane_roll(ends, -hop)
            )
        ends = ends * reduced_inv[...]
        above = lane_roll(ends, OWN)
        for z in range(LAST):
            field[z] = scaled[z] + from_prev[z] * above + from_last[z] * ends
        field[LAST] = ends
        return carry

    def outer_step(_, carry):
        lax.fori_loop(0, SUBSTEPS, solve, 0)
        base = ROWS * block.astype(F32) + 0.5
        moment = jnp.zeros(wide, F32)
        for z in range(ROWS):
            moment = moment + (base + float(z)) * field[z]
        for level in range(4):
            moment = moment + lane_roll(moment, OWN << level)
        moment = moment * (1.0 / (ROWS * BLOCKS) ** 2)
        springs[...] = SPRING_KEEP * springs[...] + SPRING_DRIVE * touching * moment
        return carry

    lax.fori_loop(0, OUTER, outer_step, 0)

    spot = lane % OWN

    def own_columns(planes):
        out = jnp.zeros((8, LANES), F32)
        for place_here in range(OWN):
            at, g = divmod(OWN + place_here, GROUPS)
            out = jnp.where(spot == place_here, lane_roll(planes[g], place_here - at), out)
        return out

    mine = jnp.concatenate([own_columns(field[z]) for z in range(ROWS)], 0)
    result[:, 0:OWN] = mine.T.reshape(BLOCKS, OWN, LANES)
    result[:, OWN:] = jnp.broadcast_to(own_columns(springs[...])[None], (BLOCKS, 8, LANES))

    for peer in peers:
        pltpu.make_async_remote_copy(
            src_ref=result.at[peer, pl.ds(0, SENT)], dst_ref=returned.at[me, pl.ds(0, SENT)],
            send_sem=return_send.at[0], recv_sem=return_sem.at[0],
            device_id=(wall, peer), device_id_type=MESH,
        ).start()
    pltpu.make_async_copy(
        result.at[me, pl.ds(0, SENT)], returned.at[me, pl.ds(0, SENT)], return_sem.at[0]
    ).start()

    sent = landed.reshape(3 * BLOCKS * WIDE, LANES).at[pl.ds(0, (BLOCKS - 1) * sum(WIDTHS))]
    pltpu.make_async_copy(sent, sent, send_sem.at[0]).wait()

    @pl.when(has_right)
    def _():
        for which in (LAYER, PRESSURE, LOADING):
            to_right(which).wait_send()

    @pl.when(has_left)
    def _():
        for which in (LAYER, PRESSURE, LOADING):
            to_left(which).wait_send()

    @pl.when(first & has_right)
    def _():
        wall_right.wait_send()

    @pl.when(last & has_left)
    def _():
        wall_left.wait_send()

    given = result.at[pl.ds(0, BLOCKS - 1), pl.ds(0, SENT)]
    pltpu.make_async_copy(given, given, return_send.at[0]).wait()
    back_here = returned.at[:, pl.ds(0, SENT)]
    pltpu.make_async_copy(back_here, back_here, return_sem.at[0]).wait()


def place_rows(returned, pressure_out, spring_out):
    planes = returned[:, 0:OWN].reshape(LANES, LANES).T
    flat = pressure_out.reshape(CROSS * ROWS, LANES)
    for z in range(ROWS):
        flat[pl.ds(z, CROSS, stride=ROWS), :] = planes[z * CROSS:(z + 1) * CROSS]
    owner = lax.broadcasted_iota(jnp.int32, (1, LANES), 1) // OWN
    total = jnp.zeros((1, LANES), F32)
    for d in range(BLOCKS):
        total = jnp.where(owner == d, returned[d, OWN:OWN + 1], total)
    spring_out[...] = total.reshape(spring_out.shape)


def lane_roll_by(x, shift):
    return pltpu.roll(x, shift, x.ndim - 1)


def on_device(pressure, layer, permeability, loading, spring, contact):
    vmem = pl.BlockSpec(memory_space=pltpu.VMEM)
    hbm = pl.BlockSpec(memory_space=pltpu.MemorySpace.HBM)
    planes = pltpu.VMEM((ROWS, GROUPS, CROSS, LANES), F32)
    plane = pltpu.VMEM((GROUPS, CROSS, LANES), F32)
    steps = pltpu.VMEM((4, GROUPS, CROSS, LANES), F32)
    tile = pltpu.VMEM((8, LANES), F32)
    returned = pl.pallas_call(
        kernel,
        out_shape=jax.ShapeDtypeStruct((BLOCKS, 2 * OWN, LANES), F32),
        in_specs=[hbm] * 6,
        out_specs=hbm,
        scratch_shapes=[
            pltpu.SMEM(permeability.shape, F32),
            pltpu.SMEM(contact.shape, jnp.int32),
            pltpu.VMEM(pressure.shape, F32),
            pltpu.VMEM(layer.shape, jnp.int32),
            pltpu.VMEM(loading.shape, F32),
            pltpu.VMEM(spring.shape, F32),
            pltpu.SemaphoreType.DMA((6,)),
            pltpu.VMEM((3, LANES + 2 * OWN, LANES), F32),
            pltpu.VMEM((3, BLOCKS, WIDE, LANES), F32),
            pltpu.VMEM((3, BLOCKS, OWN, LANES), F32),
            tile, tile,
            planes, planes, planes, planes, planes, planes,
            planes, planes, planes, planes,
            steps, steps, plane, plane, plane, plane,
            pltpu.VMEM((BLOCKS, 2 * OWN, LANES), F32),
            pltpu.SemaphoreType.DMA((1,)),
            pltpu.SemaphoreType.DMA((3,)),
            pltpu.SemaphoreType.DMA((2, 3)),
            pltpu.SemaphoreType.DMA((3,)),
            pltpu.SemaphoreType.DMA((1,)),
            pltpu.SemaphoreType.DMA((2,)),
            pltpu.SemaphoreType.DMA((1,)),
            pltpu.SemaphoreType.DMA((1,)),
        ],
        compiler_params=pltpu.CompilerParams(
            collective_id=0, has_side_effects=True, vmem_limit_bytes=60 << 20
        ),
    )(permeability, contact, pressure, layer, loading, spring)
    return pl.pallas_call(
        place_rows,
        out_shape=(
            jax.ShapeDtypeStruct(pressure.shape, F32),
            jax.ShapeDtypeStruct(spring.shape, F32),
        ),
        in_specs=[vmem],
        out_specs=(vmem, vmem),
    )(returned)


def solution(mesh):
    cells = P(None, "depth", "wall")
    return jax.shard_map(
        on_device,
        mesh=mesh,
        in_specs=(cells, cells, P(), cells, P("wall"), P("wall")),
        out_specs=(cells, P("wall")),
        check_vma=False,
    )
```

```python
import jax
import jax.numpy as jnp
from jax import lax
from jax.experimental import pallas as pl
from jax.experimental.pallas import tpu as pltpu
from jax.sharding import PartitionSpec as P

MESH = pl.DeviceIdType.MESH
F32 = jnp.float32

SOILS = 8
PANEL = 16
SUBSTEPS = 3
OUTER = 2
VNUM = 512.0
ALONG_RATE = 0.1
ACROSS_RATE = 0.06
SPRING_KEEP = 0.5
SPRING_DRIVE = 2.0

CROSS = 8
ROWS = 16
BLOCKS = 16
OWN = 8
WIDE = 3 * OWN
GROUPS = 3
LANES = 128
LAST = ROWS - 1
MIDDLE = 7
LAYER, PRESSURE, LOADING = 0, 1, 2
HALO = (5, 6, 5)
WIDTHS = tuple(OWN + 2 * halo for halo in HALO)
SIDE = 4
FAR_FIRST = sorted(
    ((dy, dx) for dy in range(SIDE) for dx in range(SIDE) if dy or dx),
    key=lambda at: -sum(min(step, SIDE - step) for step in at),
)
SENT = OWN + 1


def lane_roll(x, shift):
    return pltpu.roll(x, shift % LANES, x.ndim - 1)


def cross_roll(x, shift):
    return pltpu.roll(x, shift % CROSS, x.ndim - 2)


def harmonic(a, b):
    return (2.0 * VNUM) * a * b / (a + b)


def pick(level, table, row):
    value = jnp.full(level.shape, table[row, 0], F32)
    for soil in range(1, SOILS):
        value = jnp.where(level == float(soil), table[row, soil], value)
    return value


def kernel(
    table_in, contact_in, pressure_in, layer_in, loading_in, spring_in,
    returned,
    table, contact, pressure, layer, loading, spring, in_sem,
    packed, landed, beyond, wall_mine, wall_beside,
    field, source, keep, along, back, ahead, chain, outward, from_prev, from_last,
    last_end, last_start, prev_end, prev_start, sep_up, springs,
    result,
    send_sem, land_sem, side_send, side_sem, wall_sem, wall_send, return_send, return_sem,
):
    wall, me = lax.axis_index("wall"), lax.axis_index("depth")
    walls = lax.axis_size("wall")
    has_left, has_right = wall > 0, wall < walls - 1
    first, last = me == 0, me == BLOCKS - 1

    inputs = [
        pltpu.make_async_copy(source_ref, here, in_sem.at[at])
        for at, (source_ref, here) in enumerate((
            (layer_in, layer), (pressure_in, pressure), (loading_in, loading),
            (spring_in, spring), (contact_in, contact), (table_in, table),
        ))
    ]
    for copy in inputs:
        copy.start()

    peers = [
        lax.rem(me // SIDE + dy, SIDE) * SIDE + lax.rem(me % SIDE + dx, SIDE) for dy, dx in FAR_FIRST
    ]

    barrier = pltpu.get_barrier_semaphore()
    for peer in peers:
        pl.semaphore_signal(barrier, inc=1, device_id=(wall, peer), device_id_type=MESH)

    @pl.when(first & has_left)
    def _():
        def call(k, _):
            pl.semaphore_signal(barrier, inc=1, device_id=(wall - 1, k), device_id_type=MESH)
            return 0

        lax.fori_loop(0, BLOCKS, call, 0)

    @pl.when(last & has_right)
    def _():
        def call(k, _):
            pl.semaphore_signal(barrier, inc=1, device_id=(wall + 1, k), device_id_type=MESH)
            return 0

        lax.fori_loop(0, BLOCKS, call, 0)

    def pack(which, ref):
        inputs[which].wait()
        flat = ref.reshape(CROSS * ROWS, LANES)
        planes = [flat[pl.ds(z, CROSS, stride=ROWS), :] for z in range(ROWS)]
        packed[which, OWN:OWN + LANES] = jnp.concatenate(planes, 0).astype(F32).T

    def to_peer(which, peer):
        width = OWN + 2 * HALO[which]
        return pltpu.make_async_remote_copy(
            src_ref=packed.at[which, pl.ds(peer * OWN + OWN - HALO[which], width)],
            dst_ref=landed.at[which, me, pl.ds(OWN - HALO[which], width)],
            send_sem=send_sem.at[0], recv_sem=land_sem.at[which],
            device_id=(wall, peer), device_id_type=MESH,
        )

    def to_self(which):
        width = OWN + 2 * HALO[which]
        return pltpu.make_async_copy(
            packed.at[which, pl.ds(me * OWN + OWN - HALO[which], width)],
            landed.at[which, me, pl.ds(OWN - HALO[which], width)],
            land_sem.at[which],
        )

    def to_right(which):
        return pltpu.make_async_remote_copy(
            src_ref=packed.at[which, pl.ds(OWN + LANES - HALO[which], HALO[which])],
            dst_ref=beyond.at[which, me, pl.ds(OWN - HALO[which], HALO[which])],
            send_sem=side_send.at[0, which], recv_sem=side_sem.at[which],
            device_id=(wall + 1, 0), device_id_type=MESH,
        )

    def to_left(which):
        return pltpu.make_async_remote_copy(
            src_ref=packed.at[which, pl.ds(OWN, HALO[which])],
            dst_ref=beyond.at[which, me, pl.ds(0, HALO[which])],
            send_sem=side_send.at[1, which], recv_sem=side_sem.at[which],
            device_id=(wall - 1, BLOCKS - 1), device_id_type=MESH,
        )

    for which in (LAYER, PRESSURE, LOADING):
        packed[which, 0:OWN] = jnp.zeros((OWN, LANES), F32)
        packed[which, OWN + LANES:] = jnp.zeros((OWN, LANES), F32)
    pack(LAYER, layer)
    pack(PRESSURE, pressure)
    pack(LOADING, loading)
    for copy in inputs[LOADING + 1:]:
        copy.wait()
    lane = lax.broadcasted_iota(jnp.int32, (8, LANES), 1)
    sub = lax.broadcasted_iota(jnp.int32, (8, LANES), 0)
    share = jnp.zeros((8, LANES), F32)
    for panel in range(LANES // PANEL):
        share = jnp.where(lane // PANEL == panel, contact[panel].astype(F32), share)
    own_spring = jnp.broadcast_to(spring[...].reshape(1, LANES), (8, LANES))
    wall_mine[...] = jnp.where(sub == 0, own_spring, share)
    wall_right = pltpu.make_async_remote_copy(
        src_ref=wall_mine, dst_ref=wall_beside, send_sem=wall_send.at[0], recv_sem=wall_sem.at[0],
        device_id=(wall + 1, 0), device_id_type=MESH,
    )
    wall_left = pltpu.make_async_remote_copy(
        src_ref=wall_mine, dst_ref=wall_beside, send_sem=wall_send.at[1], recv_sem=wall_sem.at[0],
        device_id=(wall - 1, BLOCKS - 1), device_id_type=MESH,
    )

    sides = has_left.astype(jnp.int32) + has_right.astype(jnp.int32)
    pl.semaphore_wait(barrier, BLOCKS - 1 + sides)

    @pl.when(first & has_right)
    def _():
        wall_right.start()

    @pl.when(last & has_left)
    def _():
        wall_left.start()

    @pl.when(has_right)
    def _():
        for which in (LAYER, PRESSURE, LOADING):
            to_right(which).start()

    @pl.when(has_left)
    def _():
        for which in (LAYER, PRESSURE, LOADING):
            to_left(which).start()

    for peer in peers:
        to_peer(LAYER, peer).start()
    for peer in peers:
        to_peer(PRESSURE, peer).start()
        to_peer(LOADING, peer).start()
    for which in (LAYER, PRESSURE, LOADING):
        to_self(which).start()

    wide = (GROUPS, CROSS, LANES)
    lanes = lax.broadcasted_iota(jnp.int32, wide, 2)
    block = lanes // OWN
    column = 3 * (lanes % OWN) + lax.broadcasted_iota(jnp.int32, wide, 0)
    cross = lax.broadcasted_iota(jnp.int32, wide, 1)
    place = wall * LANES + me * OWN - OWN + column
    inside = (place >= 0) & (place < walls * LANES)
    top, bottom = block == 0, block == BLOCKS - 1

    def arrived(which):
        valid = landed.at[which, :, pl.ds(OWN - HALO[which], OWN + 2 * HALO[which])]
        pltpu.make_async_copy(valid, valid, land_sem.at[which]).wait()

        @pl.when((first & has_left) | (last & has_right))
        def _():
            strip = beyond.at[which, :, pl.ds(0, HALO[which])]
            pltpu.make_async_copy(strip, strip, side_sem.at[which]).wait()

        @pl.when(first)
        def _():
            landed[which, :, 0:OWN] = jnp.where(has_left, beyond[which], 0.0)

        @pl.when(last)
        def _():
            landed[which, :, 2 * OWN:] = jnp.where(has_right, beyond[which], 0.0)

        for g in range(GROUPS):
            rows = [landed[which, s, pl.ds(g, OWN, stride=GROUPS), :] for s in range(BLOCKS)]
            turned = jnp.concatenate(rows, 0).T.reshape(ROWS, CROSS, LANES)
            field_or = source if which == LOADING else field
            field_or[:, g] = turned

    arrived(LAYER)
    perm = [pick(field[z], table, 0) for z in range(ROWS)]
    up = [None] * ROWS
    for z in range(1, ROWS):
        up[z] = harmonic(perm[z - 1], perm[z])
    up[0] = jnp.where(top, VNUM * perm[0], harmonic(lane_roll(perm[LAST], OWN), perm[0]))
    down = up[1:] + [jnp.where(bottom, 0.0, lane_roll(up[0], -OWN))]
    diagonal = [1.0 + up[z] + down[z] for z in range(ROWS)]

    inverse, toward = [None] * ROWS, [None] * ROWS
    chained = [None] * ROWS
    for z in range(MIDDLE):
        pivot = diagonal[z] if z == 0 else diagonal[z] - up[z] * toward[z - 1]
        inverse[z] = 1.0 / pivot
        toward[z] = down[z] * inverse[z]
        chained[z] = up[z] * inverse[z]
    for z in range(LAST - 1, MIDDLE, -1):
        pivot = diagonal[z] if z == LAST - 1 else diagonal[z] - down[z] * toward[z + 1]
        inverse[z] = 1.0 / pivot
        toward[z] = up[z] * inverse[z]
        chained[z] = down[z] * inverse[z]
    inverse[MIDDLE] = 1.0 / (
        diagonal[MIDDLE] - up[MIDDLE] * toward[MIDDLE - 1] - down[MIDDLE] * toward[MIDDLE + 1]
    )
    chained[MIDDLE] = up[MIDDLE] * inverse[MIDDLE]
    toward[MIDDLE] = down[MIDDLE] * inverse[MIDDLE]
    inverse[LAST] = jnp.ones(wide, F32)

    upper, lower = [None] * LAST, [None] * LAST
    upper[0] = jnp.where(top, 0.0, chained[0])
    for z in range(1, MIDDLE):
        upper[z] = chained[z] * upper[z - 1]
    upper[MIDDLE] = chained[MIDDLE] * upper[MIDDLE - 1]
    for z in range(MIDDLE - 1, -1, -1):
        upper[z] = upper[z] + toward[z] * upper[z + 1]
    for z in range(MIDDLE + 1, LAST):
        upper[z] = toward[z] * upper[z - 1]
    lower[LAST - 1] = chained[LAST - 1]
    for z in range(LAST - 2, MIDDLE, -1):
        lower[z] = chained[z] * lower[z + 1]
    lower[MIDDLE] = toward[MIDDLE] * lower[MIDDLE + 1]
    for z in range(MIDDLE + 1, LAST):
        lower[z] = lower[z] + toward[z] * lower[z - 1]
    for z in range(MIDDLE - 1, -1, -1):
        lower[z] = toward[z] * lower[z + 1]
    for z in range(LAST):
        chain[z], outward[z] = chained[z], toward[z]
        from_prev[z], from_last[z] = upper[z], lower[z]

    a_coef = up[LAST] * upper[LAST - 1]
    c_coef = down[LAST] * lane_roll(lower[0], -OWN)
    b_coef = diagonal[LAST] - up[LAST] * lower[LAST - 1] - down[LAST] * lane_roll(upper[0], -OWN)
    sep_up[...] = up[LAST]
    coefs = {0: jnp.ones(wide, F32)}
    for level in range(4):
        step = 1 << level
        hop = OWN * step
        b_inv = 1.0 / b_coef
        alpha = a_coef * lane_roll(b_inv, hop)
        gamma = c_coef * lane_roll(b_inv, -hop)
        b_coef = b_coef - alpha * lane_roll(c_coef, hop) - gamma * lane_roll(a_coef, -hop)
        a_coef, c_coef = alpha * lane_roll(a_coef, hop), gamma * lane_roll(c_coef, -hop)
        longer = dict(coefs)
        for j, coef in coefs.items():
            if 2 * step == BLOCKS:
                moved = [((j + step) % BLOCKS, (alpha + gamma) * lane_roll(coef, hop))]
            else:
                moved = [
                    ((j + step) % BLOCKS, alpha * lane_roll(coef, hop)),
                    ((j - step) % BLOCKS, gamma * lane_roll(coef, -hop)),
                ]
            for at, term in moved:
                longer[at] = longer[at] + term if at in longer else term
        coefs = longer
    b_inv = 1.0 / b_coef
    for j in range(BLOCKS):
        by_end = coefs[j] * b_inv
        by_start = by_end * lane_roll(down[LAST], OWN * j)
        last_end[j], last_start[(j - 1) % BLOCKS] = by_end, by_start
        prev_end[(j + 1) % BLOCKS], prev_start[j] = lane_roll(by_end, OWN), lane_roll(by_start, OWN)

    @pl.when((first & has_left) | (last & has_right))
    def _():
        pltpu.make_async_copy(wall_beside, wall_beside, wall_sem.at[0]).wait()

    @pl.when(jnp.logical_not((first & has_left) | (last & has_right)))
    def _():
        wall_beside[...] = jnp.zeros_like(wall_beside)

    beside = (first & (lane >= LANES - OWN)) | (last & (lane < OWN))
    window = jnp.where(beside, wall_beside[...], wall_mine[...])
    window = lane_roll_by(window, lax.rem(LANES + OWN - me * OWN, LANES))
    touching = []
    for g in range(GROUPS):
        spread = jnp.take_along_axis(window, 3 * (lane % OWN) + g, axis=1)
        springs[g] = jnp.broadcast_to(spread[0:1], (CROSS, LANES))
        touching.append(jnp.broadcast_to(spread[1:2], (CROSS, LANES)))
    touching = jnp.stack(touching)

    ahead_mask = (cross < CROSS - 1).astype(F32)
    back_mask = jnp.where(cross > 0, 1.0, touching)
    for z in range(ROWS):
        lateral = jnp.where(inside, pick(field[z], table, 1), 0.0)
        a1 = ALONG_RATE * lateral
        a2 = ACROSS_RATE * lateral
        a2b, a2a = a2 * back_mask, a2 * ahead_mask
        keep[z] = (1.0 - 2.0 * a1 - a2b - a2a) * inverse[z]
        along[z], back[z], ahead[z] = a1 * inverse[z], a2b * inverse[z], a2a * inverse[z]
    arrived(LOADING)
    for z in range(ROWS):
        source[z] = source[z] * inverse[z]
    arrived(PRESSURE)

    def solve(_, carry):
        spring_now = springs[...]
        scaled = []
        for z in range(ROWS):
            now = field[z]
            left = jnp.stack([lane_roll(now[2], 1), now[0], now[1]])
            right = jnp.stack([now[1], now[2], lane_roll(now[0], -1)])
            behind = jnp.where(cross == 0, spring_now, cross_roll(now, 1))
            scaled.append(
                source[z] + keep[z] * now + along[z] * (left + right)
                + back[z] * behind + ahead[z] * cross_roll(now, -1)
            )
        for z in range(1, MIDDLE):
            scaled[z] = scaled[z] + chain[z] * scaled[z - 1]
        for z in range(LAST - 2, MIDDLE, -1):
            scaled[z] = scaled[z] + chain[z] * scaled[z + 1]
        scaled[MIDDLE] = (
            scaled[MIDDLE] + chain[MIDDLE] * scaled[MIDDLE - 1] + outward[MIDDLE] * scaled[MIDDLE + 1]
        )
        for z in range(MIDDLE - 1, -1, -1):
            scaled[z] = scaled[z] + outward[z] * scaled[z + 1]
        for z in range(MIDDLE + 1, LAST):
            scaled[z] = scaled[z] + outward[z] * scaled[z - 1]
        end, start = scaled[LAST] + sep_up[...] * scaled[LAST - 1], scaled[0]
        ends, above = jnp.zeros(wide, F32), jnp.zeros(wide, F32)
        for j in range(BLOCKS):
            end_there, start_there = lane_roll(end, OWN * j), lane_roll(start, OWN * j)
            ends = ends + last_end[j] * end_there + last_start[j] * start_there
            above = above + prev_end[j] * end_there + prev_start[j] * start_there
        for z in range(LAST):
            field[z] = scaled[z] + from_prev[z] * above + from_last[z] * ends
        field[LAST] = ends
        return carry

    def outer_step(_, carry):
        lax.fori_loop(0, SUBSTEPS, solve, 0)
        base = ROWS * block.astype(F32) + 0.5
        moment = jnp.zeros(wide, F32)
        for z in range(ROWS):
            moment = moment + (base + float(z)) * field[z]
        row = lax.broadcasted_iota(jnp.int32, (CROSS, LANES), 0)
        face = jnp.where(row == 0, moment[0], 0.0)
        for g in range(1, GROUPS):
            face = jnp.where(row == g, cross_roll(moment[g], g), face)
        total = face
        for j in range(1, BLOCKS):
            total = total + lane_roll(face, OWN * j)
        total = total * (1.0 / (ROWS * BLOCKS) ** 2)
        moment = jnp.stack([cross_roll(total, -g) for g in range(GROUPS)])
        springs[...] = SPRING_KEEP * springs[...] + SPRING_DRIVE * touching * moment
        return carry

    lax.fori_loop(0, OUTER, outer_step, 0)

    spot = lane % OWN

    def own_columns(planes):
        out = jnp.zeros((8, LANES), F32)
        for place_here in range(OWN):
            at, g = divmod(OWN + place_here, GROUPS)
            out = jnp.where(spot == place_here, lane_roll(planes[g], place_here - at), out)
        return out

    mine = jnp.concatenate([own_columns(field[z]) for z in range(ROWS)], 0)
    result[:, 0:OWN] = mine.T.reshape(BLOCKS, OWN, LANES)
    result[:, OWN:] = jnp.broadcast_to(own_columns(springs[...])[None], (BLOCKS, 8, LANES))

    for peer in peers:
        pltpu.make_async_remote_copy(
            src_ref=result.at[peer, pl.ds(0, SENT)], dst_ref=returned.at[me, pl.ds(0, SENT)],
            send_sem=return_send.at[0], recv_sem=return_sem.at[0],
            device_id=(wall, peer), device_id_type=MESH,
        ).start()
    pltpu.make_async_copy(
        result.at[me, pl.ds(0, SENT)], returned.at[me, pl.ds(0, SENT)], return_sem.at[0]
    ).start()

    sent = landed.reshape(3 * BLOCKS * WIDE, LANES).at[pl.ds(0, (BLOCKS - 1) * sum(WIDTHS))]
    pltpu.make_async_copy(sent, sent, send_sem.at[0]).wait()

    @pl.when(has_right)
    def _():
        for which in (LAYER, PRESSURE, LOADING):
            to_right(which).wait_send()

    @pl.when(has_left)
    def _():
        for which in (LAYER, PRESSURE, LOADING):
            to_left(which).wait_send()

    @pl.when(first & has_right)
    def _():
        wall_right.wait_send()

    @pl.when(last & has_left)
    def _():
        wall_left.wait_send()

    given = result.at[pl.ds(0, BLOCKS - 1), pl.ds(0, SENT)]
    pltpu.make_async_copy(given, given, return_send.at[0]).wait()
    back_here = returned.at[:, pl.ds(0, SENT)]
    pltpu.make_async_copy(back_here, back_here, return_sem.at[0]).wait()


def place_rows(returned, pressure_out, spring_out):
    planes = returned[:, 0:OWN].reshape(LANES, LANES).T
    flat = pressure_out.reshape(CROSS * ROWS, LANES)
    for z in range(ROWS):
        flat[pl.ds(z, CROSS, stride=ROWS), :] = planes[z * CROSS:(z + 1) * CROSS]
    owner = lax.broadcasted_iota(jnp.int32, (1, LANES), 1) // OWN
    total = jnp.zeros((1, LANES), F32)
    for d in range(BLOCKS):
        total = jnp.where(owner == d, returned[d, OWN:OWN + 1], total)
    spring_out[...] = total.reshape(spring_out.shape)


def lane_roll_by(x, shift):
    return pltpu.roll(x, shift, x.ndim - 1)


def on_device(pressure, layer, permeability, loading, spring, contact):
    vmem = pl.BlockSpec(memory_space=pltpu.VMEM)
    hbm = pl.BlockSpec(memory_space=pltpu.MemorySpace.HBM)
    planes = pltpu.VMEM((ROWS, GROUPS, CROSS, LANES), F32)
    plane = pltpu.VMEM((GROUPS, CROSS, LANES), F32)
    tile = pltpu.VMEM((8, LANES), F32)
    returned = pl.pallas_call(
        kernel,
        out_shape=jax.ShapeDtypeStruct((BLOCKS, 2 * OWN, LANES), F32),
        in_specs=[hbm] * 6,
        out_specs=hbm,
        scratch_shapes=[
            pltpu.SMEM(permeability.shape, F32),
            pltpu.SMEM(contact.shape, jnp.int32),
            pltpu.VMEM(pressure.shape, F32),
            pltpu.VMEM(layer.shape, jnp.int32),
            pltpu.VMEM(loading.shape, F32),
            pltpu.VMEM(spring.shape, F32),
            pltpu.SemaphoreType.DMA((6,)),
            pltpu.VMEM((3, LANES + 2 * OWN, LANES), F32),
            pltpu.VMEM((3, BLOCKS, WIDE, LANES), F32),
            pltpu.VMEM((3, BLOCKS, OWN, LANES), F32),
            tile, tile,
            planes, planes, planes, planes, planes, planes,
            planes, planes, planes, planes,
            planes, planes, planes, planes, plane, plane,
            pltpu.VMEM((BLOCKS, 2 * OWN, LANES), F32),
            pltpu.SemaphoreType.DMA((1,)),
            pltpu.SemaphoreType.DMA((3,)),
            pltpu.SemaphoreType.DMA((2, 3)),
            pltpu.SemaphoreType.DMA((3,)),
            pltpu.SemaphoreType.DMA((1,)),
            pltpu.SemaphoreType.DMA((2,)),
            pltpu.SemaphoreType.DMA((1,)),
            pltpu.SemaphoreType.DMA((1,)),
        ],
        compiler_params=pltpu.CompilerParams(
            collective_id=0, has_side_effects=True, vmem_limit_bytes=60 << 20
        ),
    )(permeability, contact, pressure, layer, loading, spring)
    return pl.pallas_call(
        place_rows,
        out_shape=(
            jax.ShapeDtypeStruct(pressure.shape, F32),
            jax.ShapeDtypeStruct(spring.shape, F32),
        ),
        in_specs=[vmem],
        out_specs=(vmem, vmem),
    )(returned)


def solution(mesh):
    cells = P(None, "depth", "wall")
    return jax.shard_map(
        on_device,
        mesh=mesh,
        in_specs=(cells, cells, P(), cells, P("wall"), P("wall")),
        out_specs=(cells, P("wall")),
        check_vma=False,
    )
```

```python
import jax
import jax.numpy as jnp
from jax import lax
from jax.experimental import pallas as pl
from jax.experimental.pallas import tpu as pltpu
from jax.sharding import PartitionSpec as P

MESH = pl.DeviceIdType.MESH
F32 = jnp.float32

SOILS = 8
PANEL = 16
SUBSTEPS = 3
OUTER = 2
VNUM = 512.0
ALONG_RATE = 0.1
ACROSS_RATE = 0.06
SPRING_KEEP = 0.5
SPRING_DRIVE = 2.0

CROSS = 8
ROWS = 16
BLOCKS = 16
SOLVERS = 8
OWN = 16
MARGIN = 8
WIDE = OWN + 2 * MARGIN
SPOTS = 8
GROUPS = 4
LANES = 128
LAST = ROWS - 1
MIDDLE = 7
LAYER, PRESSURE, LOADING = 0, 1, 2
HALO = (5, 6, 5)
WIDTHS = tuple(OWN + 2 * halo for halo in HALO)
SIDE = 4
FAR_FIRST = sorted(
    ((dy, dx) for dy in range(SIDE) for dx in range(SIDE) if dy or dx),
    key=lambda at: -sum(min(step, SIDE - step) for step in at),
)
SENT = OWN + 1
ROOM = OWN + 8


def lane_roll(x, shift):
    return pltpu.roll(x, shift % LANES, x.ndim - 1)


def cross_roll(x, shift):
    return pltpu.roll(x, shift % CROSS, x.ndim - 2)


def harmonic(a, b):
    return (2.0 * VNUM) * a * b / (a + b)


def pick(level, table, row):
    value = jnp.full(level.shape, table[row, 0], F32)
    for soil in range(1, SOILS):
        value = jnp.where(level == float(soil), table[row, soil], value)
    return value


def kernel(
    table_in, contact_in, pressure_in, layer_in, loading_in, spring_in,
    returned,
    table, contact, pressure, layer, loading, spring, in_sem,
    packed, landed, beyond, wall_mine, wall_beside,
    field, source, keep, along, back, ahead, chain, outward, from_prev, from_last,
    last_end, last_start, prev_end, prev_start, sep_up, springs,
    turned, result,
    send_sem, land_sem, side_send, side_sem, wall_sem, wall_send, return_send, return_sem,
):
    wall, me = lax.axis_index("wall"), lax.axis_index("depth")
    walls = lax.axis_size("wall")
    has_left, has_right = wall > 0, wall < walls - 1

    def shift_of(wall):
        return SOLVERS * lax.rem(wall, 2)

    def spot_of(device):
        return lax.rem(device + BLOCKS - shift_of(wall), BLOCKS)

    mine = spot_of(me)
    solves, first, last = mine < SOLVERS, mine == 0, mine == SOLVERS - 1
    left_end = (wall - 1, shift_of(wall + 1) + SOLVERS - 1)
    right_end = (wall + 1, shift_of(wall + 1))

    inputs = [
        pltpu.make_async_copy(source_ref, here, in_sem.at[at])
        for at, (source_ref, here) in enumerate((
            (layer_in, layer), (pressure_in, pressure), (loading_in, loading),
            (spring_in, spring), (contact_in, contact), (table_in, table),
        ))
    ]
    for copy in inputs:
        copy.start()

    peers = [
        lax.rem(me // SIDE + dy, SIDE) * SIDE + lax.rem(me % SIDE + dx, SIDE) for dy, dx in FAR_FIRST
    ]

    barrier = pltpu.get_barrier_semaphore()

    @pl.when(solves)
    def _():
        for peer in peers:
            pl.semaphore_signal(barrier, inc=1, device_id=(wall, peer), device_id_type=MESH)

    @pl.when(first & has_left)
    def _():
        def call(k, _):
            pl.semaphore_signal(barrier, inc=1, device_id=(wall - 1, k), device_id_type=MESH)
            return 0

        lax.fori_loop(0, BLOCKS, call, 0)

    @pl.when(last & has_right)
    def _():
        def call(k, _):
            pl.semaphore_signal(barrier, inc=1, device_id=(wall + 1, k), device_id_type=MESH)
            return 0

        lax.fori_loop(0, BLOCKS, call, 0)

    def pack(which, ref):
        inputs[which].wait()
        flat = ref.reshape(CROSS * ROWS, LANES)
        planes = [flat[pl.ds(z, CROSS, stride=ROWS), :] for z in range(ROWS)]
        packed[which, MARGIN:MARGIN + LANES] = jnp.concatenate(planes, 0).astype(F32).T

    def to_peer(which, peer):
        width = OWN + 2 * HALO[which]
        return pltpu.make_async_remote_copy(
            src_ref=packed.at[which, pl.ds(spot_of(peer) * OWN + MARGIN - HALO[which], width)],
            dst_ref=landed.at[which, me, pl.ds(MARGIN - HALO[which], width)],
            send_sem=send_sem.at[0], recv_sem=land_sem.at[which],
            device_id=(wall, peer), device_id_type=MESH,
        )

    def to_self(which):
        width = OWN + 2 * HALO[which]
        return pltpu.make_async_copy(
            packed.at[which, pl.ds(mine * OWN + MARGIN - HALO[which], width)],
            landed.at[which, me, pl.ds(MARGIN - HALO[which], width)],
            land_sem.at[which],
        )

    def to_right(which):
        return pltpu.make_async_remote_copy(
            src_ref=packed.at[which, pl.ds(MARGIN + LANES - HALO[which], HALO[which])],
            dst_ref=beyond.at[which, me, pl.ds(MARGIN - HALO[which], HALO[which])],
            send_sem=side_send.at[0, which], recv_sem=side_sem.at[which],
            device_id=right_end, device_id_type=MESH,
        )

    def to_left(which):
        return pltpu.make_async_remote_copy(
            src_ref=packed.at[which, pl.ds(MARGIN, HALO[which])],
            dst_ref=beyond.at[which, me, pl.ds(0, HALO[which])],
            send_sem=side_send.at[1, which], recv_sem=side_sem.at[which],
            device_id=left_end, device_id_type=MESH,
        )

    for which in (LAYER, PRESSURE, LOADING):
        packed[which, 0:MARGIN] = jnp.zeros((MARGIN, LANES), F32)
        packed[which, MARGIN + LANES:] = jnp.zeros((MARGIN, LANES), F32)
    pack(LAYER, layer)
    pack(PRESSURE, pressure)
    pack(LOADING, loading)
    for copy in inputs[LOADING + 1:]:
        copy.wait()
    lane = lax.broadcasted_iota(jnp.int32, (8, LANES), 1)
    sub = lax.broadcasted_iota(jnp.int32, (8, LANES), 0)
    share = jnp.zeros((8, LANES), F32)
    for panel in range(LANES // PANEL):
        share = jnp.where(lane // PANEL == panel, contact[panel].astype(F32), share)
    own_spring = jnp.broadcast_to(spring[...].reshape(1, LANES), (8, LANES))
    wall_mine[...] = jnp.where(sub == 0, own_spring, share)
    wall_right = pltpu.make_async_remote_copy(
        src_ref=wall_mine, dst_ref=wall_beside, send_sem=wall_send.at[0], recv_sem=wall_sem.at[0],
        device_id=right_end, device_id_type=MESH,
    )
    wall_left = pltpu.make_async_remote_copy(
        src_ref=wall_mine, dst_ref=wall_beside, send_sem=wall_send.at[1], recv_sem=wall_sem.at[0],
        device_id=left_end, device_id_type=MESH,
    )

    sides = has_left.astype(jnp.int32) + has_right.astype(jnp.int32)
    pl.semaphore_wait(barrier, SOLVERS - solves.astype(jnp.int32) + sides)

    @pl.when(first & has_right)
    def _():
        wall_right.start()

    @pl.when(last & has_left)
    def _():
        wall_left.start()

    @pl.when(has_right)
    def _():
        for which in (LAYER, PRESSURE, LOADING):
            to_right(which).start()

    @pl.when(has_left)
    def _():
        for which in (LAYER, PRESSURE, LOADING):
            to_left(which).start()

    def deal(peer, *arrays):
        @pl.when(spot_of(peer) < SOLVERS)
        def _():
            for which in arrays:
                to_peer(which, peer).start()

    for peer in peers:
        deal(peer, LAYER)
    for peer in peers:
        deal(peer, PRESSURE, LOADING)

    @pl.when(solves)
    def _():
        for which in (LAYER, PRESSURE, LOADING):
            to_self(which).start()

    @pl.when(solves)
    def _():
        wide = (GROUPS, CROSS, LANES)
        lanes = lax.broadcasted_iota(jnp.int32, wide, 2)
        block = lanes // SPOTS
        column = GROUPS * (lanes % SPOTS) + lax.broadcasted_iota(jnp.int32, wide, 0)
        cross = lax.broadcasted_iota(jnp.int32, wide, 1)
        place = wall * LANES + mine * OWN - MARGIN + column
        inside = (place >= 0) & (place < walls * LANES)
        top, bottom = block == 0, block == BLOCKS - 1

        def arrived(which):
            valid = landed.at[which, :, pl.ds(MARGIN - HALO[which], OWN + 2 * HALO[which])]
            pltpu.make_async_copy(valid, valid, land_sem.at[which]).wait()

            @pl.when((first & has_left) | (last & has_right))
            def _():
                strip = beyond.at[which, :, pl.ds(0, HALO[which])]
                pltpu.make_async_copy(strip, strip, side_sem.at[which]).wait()

            @pl.when(first)
            def _():
                landed[which, :, 0:MARGIN] = jnp.where(has_left, beyond[which], 0.0)

            @pl.when(last)
            def _():
                landed[which, :, OWN + MARGIN:] = jnp.where(has_right, beyond[which], 0.0)

            for g in range(GROUPS):
                rows = [landed[which, s, pl.ds(g, SPOTS, stride=GROUPS), :] for s in range(BLOCKS)]
                planes = jnp.concatenate(rows, 0).T.reshape(ROWS, CROSS, LANES)
                field_or = source if which == LOADING else field
                field_or[:, g] = planes

        arrived(LAYER)
        perm = [pick(field[z], table, 0) for z in range(ROWS)]
        up = [None] * ROWS
        for z in range(1, ROWS):
            up[z] = harmonic(perm[z - 1], perm[z])
        up[0] = jnp.where(top, VNUM * perm[0], harmonic(lane_roll(perm[LAST], SPOTS), perm[0]))
        down = up[1:] + [jnp.where(bottom, 0.0, lane_roll(up[0], -SPOTS))]
        diagonal = [1.0 + up[z] + down[z] for z in range(ROWS)]

        inverse, toward = [None] * ROWS, [None] * ROWS
        chained = [None] * ROWS
        for z in range(MIDDLE):
            pivot = diagonal[z] if z == 0 else diagonal[z] - up[z] * toward[z - 1]
            inverse[z] = 1.0 / pivot
            toward[z] = down[z] * inverse[z]
            chained[z] = up[z] * inverse[z]
        for z in range(LAST - 1, MIDDLE, -1):
            pivot = diagonal[z] if z == LAST - 1 else diagonal[z] - down[z] * toward[z + 1]
            inverse[z] = 1.0 / pivot
            toward[z] = up[z] * inverse[z]
            chained[z] = down[z] * inverse[z]
        inverse[MIDDLE] = 1.0 / (
            diagonal[MIDDLE] - up[MIDDLE] * toward[MIDDLE - 1] - down[MIDDLE] * toward[MIDDLE + 1]
        )
        chained[MIDDLE] = up[MIDDLE] * inverse[MIDDLE]
        toward[MIDDLE] = down[MIDDLE] * inverse[MIDDLE]
        inverse[LAST] = jnp.ones(wide, F32)

        upper, lower = [None] * LAST, [None] * LAST
        upper[0] = jnp.where(top, 0.0, chained[0])
        for z in range(1, MIDDLE):
            upper[z] = chained[z] * upper[z - 1]
        upper[MIDDLE] = chained[MIDDLE] * upper[MIDDLE - 1]
        for z in range(MIDDLE - 1, -1, -1):
            upper[z] = upper[z] + toward[z] * upper[z + 1]
        for z in range(MIDDLE + 1, LAST):
            upper[z] = toward[z] * upper[z - 1]
        lower[LAST - 1] = chained[LAST - 1]
        for z in range(LAST - 2, MIDDLE, -1):
            lower[z] = chained[z] * lower[z + 1]
        lower[MIDDLE] = toward[MIDDLE] * lower[MIDDLE + 1]
        for z in range(MIDDLE + 1, LAST):
            lower[z] = lower[z] + toward[z] * lower[z - 1]
        for z in range(MIDDLE - 1, -1, -1):
            lower[z] = toward[z] * lower[z + 1]
        for z in range(LAST):
            chain[z], outward[z] = chained[z], toward[z]
            from_prev[z], from_last[z] = upper[z], lower[z]

        a_coef = up[LAST] * upper[LAST - 1]
        c_coef = down[LAST] * lane_roll(lower[0], -SPOTS)
        b_coef = diagonal[LAST] - up[LAST] * lower[LAST - 1] - down[LAST] * lane_roll(upper[0], -SPOTS)
        sep_up[...] = up[LAST]
        coefs = {0: jnp.ones(wide, F32)}
        for level in range(4):
            step = 1 << level
            hop = SPOTS * step
            b_inv = 1.0 / b_coef
            alpha = a_coef * lane_roll(b_inv, hop)
            gamma = c_coef * lane_roll(b_inv, -hop)
            b_coef = b_coef - alpha * lane_roll(c_coef, hop) - gamma * lane_roll(a_coef, -hop)
            a_coef, c_coef = alpha * lane_roll(a_coef, hop), gamma * lane_roll(c_coef, -hop)
            longer = dict(coefs)
            for j, coef in coefs.items():
                if 2 * step == BLOCKS:
                    moved = [((j + step) % BLOCKS, (alpha + gamma) * lane_roll(coef, hop))]
                else:
                    moved = [
                        ((j + step) % BLOCKS, alpha * lane_roll(coef, hop)),
                        ((j - step) % BLOCKS, gamma * lane_roll(coef, -hop)),
                    ]
                for at, term in moved:
                    longer[at] = longer[at] + term if at in longer else term
            coefs = longer
        b_inv = 1.0 / b_coef
        for j in range(BLOCKS):
            by_end = coefs[j] * b_inv
            by_start = by_end * lane_roll(down[LAST], SPOTS * j)
            last_end[j], last_start[(j - 1) % BLOCKS] = by_end, by_start
            prev_end[(j + 1) % BLOCKS], prev_start[j] = lane_roll(by_end, SPOTS), lane_roll(by_start, SPOTS)

        @pl.when((first & has_left) | (last & has_right))
        def _():
            pltpu.make_async_copy(wall_beside, wall_beside, wall_sem.at[0]).wait()

        @pl.when(jnp.logical_not((first & has_left) | (last & has_right)))
        def _():
            wall_beside[...] = jnp.zeros_like(wall_beside)

        beside = (first & (lane >= LANES - MARGIN)) | (last & (lane < MARGIN))
        window = jnp.where(beside, wall_beside[...], wall_mine[...])
        window = lane_roll_by(window, lax.rem(2 * LANES + MARGIN - mine * OWN, LANES))
        touching = []
        for g in range(GROUPS):
            spread = jnp.take_along_axis(window, GROUPS * (lane % SPOTS) + g, axis=1)
            springs[g] = jnp.broadcast_to(spread[0:1], (CROSS, LANES))
            touching.append(jnp.broadcast_to(spread[1:2], (CROSS, LANES)))
        touching = jnp.stack(touching)

        ahead_mask = (cross < CROSS - 1).astype(F32)
        back_mask = jnp.where(cross > 0, 1.0, touching)
        for z in range(ROWS):
            lateral = jnp.where(inside, pick(field[z], table, 1), 0.0)
            a1 = ALONG_RATE * lateral
            a2 = ACROSS_RATE * lateral
            a2b, a2a = a2 * back_mask, a2 * ahead_mask
            keep[z] = (1.0 - 2.0 * a1 - a2b - a2a) * inverse[z]
            along[z], back[z], ahead[z] = a1 * inverse[z], a2b * inverse[z], a2a * inverse[z]
        arrived(LOADING)
        for z in range(ROWS):
            source[z] = source[z] * inverse[z]
        arrived(PRESSURE)

        def solve(_, carry):
            spring_now = springs[...]
            scaled = []
            for z in range(ROWS):
                now = field[z]
                left = jnp.stack([lane_roll(now[3], 1), now[0], now[1], now[2]])
                right = jnp.stack([now[1], now[2], now[3], lane_roll(now[0], -1)])
                behind = jnp.where(cross == 0, spring_now, cross_roll(now, 1))
                scaled.append(
                    source[z] + keep[z] * now + along[z] * (left + right)
                    + back[z] * behind + ahead[z] * cross_roll(now, -1)
                )
            for z in range(1, MIDDLE):
                scaled[z] = scaled[z] + chain[z] * scaled[z - 1]
            for z in range(LAST - 2, MIDDLE, -1):
                scaled[z] = scaled[z] + chain[z] * scaled[z + 1]
            scaled[MIDDLE] = (
                scaled[MIDDLE] + chain[MIDDLE] * scaled[MIDDLE - 1] + outward[MIDDLE] * scaled[MIDDLE + 1]
            )
            for z in range(MIDDLE - 1, -1, -1):
                scaled[z] = scaled[z] + outward[z] * scaled[z + 1]
            for z in range(MIDDLE + 1, LAST):
                scaled[z] = scaled[z] + outward[z] * scaled[z - 1]
            end, start = scaled[LAST] + sep_up[...] * scaled[LAST - 1], scaled[0]
            ends, above = jnp.zeros(wide, F32), jnp.zeros(wide, F32)
            for j in range(BLOCKS):
                end_there, start_there = lane_roll(end, SPOTS * j), lane_roll(start, SPOTS * j)
                ends = ends + last_end[j] * end_there + last_start[j] * start_there
                above = above + prev_end[j] * end_there + prev_start[j] * start_there
            for z in range(LAST):
                field[z] = scaled[z] + from_prev[z] * above + from_last[z] * ends
            field[LAST] = ends
            return carry

        def outer_step(_, carry):
            lax.fori_loop(0, SUBSTEPS, solve, 0)
            base = ROWS * block.astype(F32) + 0.5
            moment = jnp.zeros(wide, F32)
            for z in range(ROWS):
                moment = moment + (base + float(z)) * field[z]
            row = lax.broadcasted_iota(jnp.int32, (CROSS, LANES), 0)
            face = jnp.where(row == 0, moment[0], 0.0)
            for g in range(1, GROUPS):
                face = jnp.where(row == g, cross_roll(moment[g], g), face)
            total = face
            for j in range(1, BLOCKS):
                total = total + lane_roll(face, SPOTS * j)
            total = total * (1.0 / (ROWS * BLOCKS) ** 2)
            moment = jnp.stack([cross_roll(total, -g) for g in range(GROUPS)])
            springs[...] = SPRING_KEEP * springs[...] + SPRING_DRIVE * touching * moment
            return carry

        lax.fori_loop(0, OUTER, outer_step, 0)

        for g in range(GROUPS):
            turned[g] = field[:, g].reshape(LANES, LANES).T
        flat_result = result.reshape(BLOCKS * ROOM, LANES)
        for at in range(OWN):
            i, g = divmod(MARGIN + at, GROUPS)
            for half in range(2):
                flat_result[pl.ds(at + half * 8 * ROOM, 8, stride=ROOM), :] = (
                    turned[g, pl.ds(i + half * 8 * SPOTS, 8, stride=SPOTS), :]
                )
        spring_row = jnp.zeros((8, LANES), F32)
        for g in range(GROUPS):
            spread = jnp.take_along_axis(
                springs[g], (MARGIN + lane % OWN) // GROUPS, axis=1
            )
            spring_row = jnp.where(lane % GROUPS == g, spread, spring_row)
        result[:, OWN:] = jnp.broadcast_to(spring_row[None], (BLOCKS, 8, LANES))

        for peer in peers:
            pltpu.make_async_remote_copy(
                src_ref=result.at[peer, pl.ds(0, SENT)], dst_ref=returned.at[mine, pl.ds(0, SENT)],
                send_sem=return_send.at[0], recv_sem=return_sem.at[0],
                device_id=(wall, peer), device_id_type=MESH,
            ).start()
        pltpu.make_async_copy(
            result.at[me, pl.ds(0, SENT)], returned.at[mine, pl.ds(0, SENT)], return_sem.at[0]
        ).start()

    def wait_dealt(count):
        sent = landed.reshape(3 * BLOCKS * WIDE, LANES).at[pl.ds(0, count * sum(WIDTHS))]
        pltpu.make_async_copy(sent, sent, send_sem.at[0]).wait()

    @pl.when(solves)
    def _():
        wait_dealt(SOLVERS - 1)

    @pl.when(jnp.logical_not(solves))
    def _():
        wait_dealt(SOLVERS)

    @pl.when(has_right)
    def _():
        for which in (LAYER, PRESSURE, LOADING):
            to_right(which).wait_send()

    @pl.when(has_left)
    def _():
        for which in (LAYER, PRESSURE, LOADING):
            to_left(which).wait_send()

    @pl.when(first & has_right)
    def _():
        wall_right.wait_send()

    @pl.when(last & has_left)
    def _():
        wall_left.wait_send()

    @pl.when(solves)
    def _():
        given = result.reshape(BLOCKS * ROOM, LANES).at[pl.ds(0, (BLOCKS - 1) * SENT)]
        pltpu.make_async_copy(given, given, return_send.at[0]).wait()

    back_here = returned.at[:, pl.ds(0, SENT)]
    pltpu.make_async_copy(back_here, back_here, return_sem.at[0]).wait()


def place_rows(returned, pressure_out, spring_out):
    planes = returned[:, 0:OWN].reshape(LANES, LANES).T
    flat = pressure_out.reshape(CROSS * ROWS, LANES)
    for z in range(ROWS):
        flat[pl.ds(z, CROSS, stride=ROWS), :] = planes[z * CROSS:(z + 1) * CROSS]
    owner = lax.broadcasted_iota(jnp.int32, (1, LANES), 1) // OWN
    total = jnp.zeros((1, LANES), F32)
    for d in range(SOLVERS):
        total = jnp.where(owner == d, returned[d, OWN:OWN + 1], total)
    spring_out[...] = total.reshape(spring_out.shape)


def lane_roll_by(x, shift):
    return pltpu.roll(x, shift, x.ndim - 1)


def on_device(pressure, layer, permeability, loading, spring, contact):
    vmem = pl.BlockSpec(memory_space=pltpu.VMEM)
    hbm = pl.BlockSpec(memory_space=pltpu.MemorySpace.HBM)
    planes = pltpu.VMEM((ROWS, GROUPS, CROSS, LANES), F32)
    plane = pltpu.VMEM((GROUPS, CROSS, LANES), F32)
    tile = pltpu.VMEM((8, LANES), F32)
    returned = pl.pallas_call(
        kernel,
        out_shape=jax.ShapeDtypeStruct((SOLVERS, ROOM, LANES), F32),
        in_specs=[hbm] * 6,
        out_specs=hbm,
        scratch_shapes=[
            pltpu.SMEM(permeability.shape, F32),
            pltpu.SMEM(contact.shape, jnp.int32),
            pltpu.VMEM(pressure.shape, F32),
            pltpu.VMEM(layer.shape, jnp.int32),
            pltpu.VMEM(loading.shape, F32),
            pltpu.VMEM(spring.shape, F32),
            pltpu.SemaphoreType.DMA((6,)),
            pltpu.VMEM((3, LANES + 2 * MARGIN, LANES), F32),
            pltpu.VMEM((3, BLOCKS, WIDE, LANES), F32),
            pltpu.VMEM((3, BLOCKS, MARGIN, LANES), F32),
            tile, tile,
            planes, planes, planes, planes, planes, planes,
            planes, planes, planes, planes,
            planes, planes, planes, planes, plane, plane,
            pltpu.VMEM((GROUPS, LANES, LANES), F32),
            pltpu.VMEM((BLOCKS, ROOM, LANES), F32),
            pltpu.SemaphoreType.DMA((1,)),
            pltpu.SemaphoreType.DMA((3,)),
            pltpu.SemaphoreType.DMA((2, 3)),
            pltpu.SemaphoreType.DMA((3,)),
            pltpu.SemaphoreType.DMA((1,)),
            pltpu.SemaphoreType.DMA((2,)),
            pltpu.SemaphoreType.DMA((1,)),
            pltpu.SemaphoreType.DMA((1,)),
        ],
        compiler_params=pltpu.CompilerParams(
            collective_id=0, has_side_effects=True, vmem_limit_bytes=60 << 20
        ),
    )(permeability, contact, pressure, layer, loading, spring)
    return pl.pallas_call(
        place_rows,
        out_shape=(
            jax.ShapeDtypeStruct(pressure.shape, F32),
            jax.ShapeDtypeStruct(spring.shape, F32),
        ),
        in_specs=[vmem],
        out_specs=(vmem, vmem),
    )(returned)


def solution(mesh):
    cells = P(None, "depth", "wall")
    return jax.shard_map(
        on_device,
        mesh=mesh,
        in_specs=(cells, cells, P(), cells, P("wall"), P("wall")),
        out_specs=(cells, P("wall")),
        check_vma=False,
    )
```

```python
import jax
import jax.numpy as jnp
from jax import lax
from jax.experimental import pallas as pl
from jax.experimental.pallas import tpu as pltpu
from jax.sharding import PartitionSpec as P

MESH = pl.DeviceIdType.MESH
F32 = jnp.float32

SOILS = 8
PANEL = 16
SUBSTEPS = 3
OUTER = 2
VNUM = 512.0
ALONG_RATE = 0.1
ACROSS_RATE = 0.06
SPRING_KEEP = 0.5
SPRING_DRIVE = 2.0

CROSS = 8
ROWS = 16
BLOCKS = 16
SOLVERS = 8
MOVED = 5
OWN = 16
MARGIN = 8
WIDE = OWN + 2 * MARGIN
SPOTS = 8
GROUPS = 4
LANES = 128
LAST = ROWS - 1
MIDDLE = 7
LAYER, PRESSURE, LOADING = 0, 1, 2
HALO = (5, 6, 5)
WIDTHS = tuple(OWN + 2 * halo for halo in HALO)
SIDE = 4
FAR_FIRST = sorted(
    ((dy, dx) for dy in range(SIDE) for dx in range(SIDE) if dy or dx),
    key=lambda at: -sum(min(step, SIDE - step) for step in at),
)
SENT = OWN + 1
ROOM = OWN + 8


def lane_roll(x, shift):
    return pltpu.roll(x, shift % LANES, x.ndim - 1)


def cross_roll(x, shift):
    return pltpu.roll(x, shift % CROSS, x.ndim - 2)


def harmonic(a, b):
    return (2.0 * VNUM) * a * b / (a + b)


def pick(level, table, row):
    value = jnp.full(level.shape, table[row, 0], F32)
    for soil in range(1, SOILS):
        value = jnp.where(level == float(soil), table[row, soil], value)
    return value


def kernel(
    table_in, contact_in, pressure_in, layer_in, loading_in, spring_in,
    returned,
    table, contact, pressure, layer, loading, spring, in_sem,
    packed, landed, beyond, wall_mine, wall_beside,
    field, source, keep, along, back, ahead, chain, outward, from_prev, from_last,
    last_end, last_start, prev_end, prev_start, sep_up, springs,
    turned, result,
    send_sem, land_sem, side_send, side_sem, wall_sem, wall_send, return_send, return_sem,
):
    wall, me = lax.axis_index("wall"), lax.axis_index("depth")
    walls = lax.axis_size("wall")
    has_left, has_right = wall > 0, wall < walls - 1

    def shift_of(wall):
        return SOLVERS * lax.rem(wall, 2)

    def spot_of(device):
        at = lax.rem(device + BLOCKS - shift_of(wall), BLOCKS)
        return jnp.where(at < SOLVERS, lax.rem(at + SOLVERS - MOVED, SOLVERS), at)

    mine = spot_of(me)
    solves, first, last = mine < SOLVERS, mine == 0, mine == SOLVERS - 1
    left_end = (wall - 1, shift_of(wall + 1) + (SOLVERS - 1 + MOVED) % SOLVERS)
    right_end = (wall + 1, shift_of(wall + 1) + MOVED)

    inputs = [
        pltpu.make_async_copy(source_ref, here, in_sem.at[at])
        for at, (source_ref, here) in enumerate((
            (layer_in, layer), (pressure_in, pressure), (loading_in, loading),
            (spring_in, spring), (contact_in, contact), (table_in, table),
        ))
    ]
    for copy in inputs:
        copy.start()

    peers = [
        lax.rem(me // SIDE + dy, SIDE) * SIDE + lax.rem(me % SIDE + dx, SIDE) for dy, dx in FAR_FIRST
    ]

    barrier = pltpu.get_barrier_semaphore()

    @pl.when(solves)
    def _():
        for peer in peers:
            pl.semaphore_signal(barrier, inc=1, device_id=(wall, peer), device_id_type=MESH)

    @pl.when(first & has_left)
    def _():
        def call(k, _):
            pl.semaphore_signal(barrier, inc=1, device_id=(wall - 1, k), device_id_type=MESH)
            return 0

        lax.fori_loop(0, BLOCKS, call, 0)

    @pl.when(last & has_right)
    def _():
        def call(k, _):
            pl.semaphore_signal(barrier, inc=1, device_id=(wall + 1, k), device_id_type=MESH)
            return 0

        lax.fori_loop(0, BLOCKS, call, 0)

    def pack(which, ref):
        inputs[which].wait()
        flat = ref.reshape(CROSS * ROWS, LANES)
        planes = [flat[pl.ds(z, CROSS, stride=ROWS), :] for z in range(ROWS)]
        packed[which, MARGIN:MARGIN + LANES] = jnp.concatenate(planes, 0).astype(F32).T

    def to_peer(which, peer):
        width = OWN + 2 * HALO[which]
        return pltpu.make_async_remote_copy(
            src_ref=packed.at[which, pl.ds(spot_of(peer) * OWN + MARGIN - HALO[which], width)],
            dst_ref=landed.at[which, me, pl.ds(MARGIN - HALO[which], width)],
            send_sem=send_sem.at[0], recv_sem=land_sem.at[which],
            device_id=(wall, peer), device_id_type=MESH,
        )

    def to_self(which):
        width = OWN + 2 * HALO[which]
        return pltpu.make_async_copy(
            packed.at[which, pl.ds(mine * OWN + MARGIN - HALO[which], width)],
            landed.at[which, me, pl.ds(MARGIN - HALO[which], width)],
            land_sem.at[which],
        )

    def to_right(which):
        return pltpu.make_async_remote_copy(
            src_ref=packed.at[which, pl.ds(MARGIN + LANES - HALO[which], HALO[which])],
            dst_ref=beyond.at[which, me, pl.ds(MARGIN - HALO[which], HALO[which])],
            send_sem=side_send.at[0, which], recv_sem=side_sem.at[which],
            device_id=right_end, device_id_type=MESH,
        )

    def to_left(which):
        return pltpu.make_async_remote_copy(
            src_ref=packed.at[which, pl.ds(MARGIN, HALO[which])],
            dst_ref=beyond.at[which, me, pl.ds(0, HALO[which])],
            send_sem=side_send.at[1, which], recv_sem=side_sem.at[which],
            device_id=left_end, device_id_type=MESH,
        )

    for which in (LAYER, PRESSURE, LOADING):
        packed[which, 0:MARGIN] = jnp.zeros((MARGIN, LANES), F32)
        packed[which, MARGIN + LANES:] = jnp.zeros((MARGIN, LANES), F32)
    pack(LAYER, layer)
    pack(PRESSURE, pressure)
    pack(LOADING, loading)
    for copy in inputs[LOADING + 1:]:
        copy.wait()
    lane = lax.broadcasted_iota(jnp.int32, (8, LANES), 1)
    sub = lax.broadcasted_iota(jnp.int32, (8, LANES), 0)
    share = jnp.zeros((8, LANES), F32)
    for panel in range(LANES // PANEL):
        share = jnp.where(lane // PANEL == panel, contact[panel].astype(F32), share)
    own_spring = jnp.broadcast_to(spring[...].reshape(1, LANES), (8, LANES))
    wall_mine[...] = jnp.where(sub == 0, own_spring, share)
    wall_right = pltpu.make_async_remote_copy(
        src_ref=wall_mine, dst_ref=wall_beside, send_sem=wall_send.at[0], recv_sem=wall_sem.at[0],
        device_id=right_end, device_id_type=MESH,
    )
    wall_left = pltpu.make_async_remote_copy(
        src_ref=wall_mine, dst_ref=wall_beside, send_sem=wall_send.at[1], recv_sem=wall_sem.at[0],
        device_id=left_end, device_id_type=MESH,
    )

    sides = has_left.astype(jnp.int32) + has_right.astype(jnp.int32)
    pl.semaphore_wait(barrier, SOLVERS - solves.astype(jnp.int32) + sides)

    @pl.when(first & has_right)
    def _():
        wall_right.start()

    @pl.when(last & has_left)
    def _():
        wall_left.start()

    @pl.when(has_right)
    def _():
        for which in (LAYER, PRESSURE, LOADING):
            to_right(which).start()

    @pl.when(has_left)
    def _():
        for which in (LAYER, PRESSURE, LOADING):
            to_left(which).start()

    def deal(peer, *arrays):
        @pl.when(spot_of(peer) < SOLVERS)
        def _():
            for which in arrays:
                to_peer(which, peer).start()

    for peer in peers:
        deal(peer, LAYER)
    for peer in peers:
        deal(peer, PRESSURE, LOADING)

    @pl.when(solves)
    def _():
        for which in (LAYER, PRESSURE, LOADING):
            to_self(which).start()

    @pl.when(solves)
    def _():
        wide = (GROUPS, CROSS, LANES)
        lanes = lax.broadcasted_iota(jnp.int32, wide, 2)
        block = lanes // SPOTS
        column = GROUPS * (lanes % SPOTS) + lax.broadcasted_iota(jnp.int32, wide, 0)
        cross = lax.broadcasted_iota(jnp.int32, wide, 1)
        place = wall * LANES + mine * OWN - MARGIN + column
        inside = (place >= 0) & (place < walls * LANES)
        top, bottom = block == 0, block == BLOCKS - 1

        def arrived(which):
            valid = landed.at[which, :, pl.ds(MARGIN - HALO[which], OWN + 2 * HALO[which])]
            pltpu.make_async_copy(valid, valid, land_sem.at[which]).wait()

            @pl.when((first & has_left) | (last & has_right))
            def _():
                strip = beyond.at[which, :, pl.ds(0, HALO[which])]
                pltpu.make_async_copy(strip, strip, side_sem.at[which]).wait()

            @pl.when(first)
            def _():
                landed[which, :, 0:MARGIN] = jnp.where(has_left, beyond[which], 0.0)

            @pl.when(last)
            def _():
                landed[which, :, OWN + MARGIN:] = jnp.where(has_right, beyond[which], 0.0)

            for g in range(GROUPS):
                rows = [landed[which, s, pl.ds(g, SPOTS, stride=GROUPS), :] for s in range(BLOCKS)]
                planes = jnp.concatenate(rows, 0).T.reshape(ROWS, CROSS, LANES)
                field_or = source if which == LOADING else field
                field_or[:, g] = planes

        arrived(LAYER)
        perm = [pick(field[z], table, 0) for z in range(ROWS)]
        up = [None] * ROWS
        for z in range(1, ROWS):
            up[z] = harmonic(perm[z - 1], perm[z])
        up[0] = jnp.where(top, VNUM * perm[0], harmonic(lane_roll(perm[LAST], SPOTS), perm[0]))
        down = up[1:] + [jnp.where(bottom, 0.0, lane_roll(up[0], -SPOTS))]
        diagonal = [1.0 + up[z] + down[z] for z in range(ROWS)]

        inverse, toward = [None] * ROWS, [None] * ROWS
        chained = [None] * ROWS
        for z in range(MIDDLE):
            pivot = diagonal[z] if z == 0 else diagonal[z] - up[z] * toward[z - 1]
            inverse[z] = 1.0 / pivot
            toward[z] = down[z] * inverse[z]
            chained[z] = up[z] * inverse[z]
        for z in range(LAST - 1, MIDDLE, -1):
            pivot = diagonal[z] if z == LAST - 1 else diagonal[z] - down[z] * toward[z + 1]
            inverse[z] = 1.0 / pivot
            toward[z] = up[z] * inverse[z]
            chained[z] = down[z] * inverse[z]
        inverse[MIDDLE] = 1.0 / (
            diagonal[MIDDLE] - up[MIDDLE] * toward[MIDDLE - 1] - down[MIDDLE] * toward[MIDDLE + 1]
        )
        chained[MIDDLE] = up[MIDDLE] * inverse[MIDDLE]
        toward[MIDDLE] = down[MIDDLE] * inverse[MIDDLE]
        inverse[LAST] = jnp.ones(wide, F32)

        upper, lower = [None] * LAST, [None] * LAST
        upper[0] = jnp.where(top, 0.0, chained[0])
        for z in range(1, MIDDLE):
            upper[z] = chained[z] * upper[z - 1]
        upper[MIDDLE] = chained[MIDDLE] * upper[MIDDLE - 1]
        for z in range(MIDDLE - 1, -1, -1):
            upper[z] = upper[z] + toward[z] * upper[z + 1]
        for z in range(MIDDLE + 1, LAST):
            upper[z] = toward[z] * upper[z - 1]
        lower[LAST - 1] = chained[LAST - 1]
        for z in range(LAST - 2, MIDDLE, -1):
            lower[z] = chained[z] * lower[z + 1]
        lower[MIDDLE] = toward[MIDDLE] * lower[MIDDLE + 1]
        for z in range(MIDDLE + 1, LAST):
            lower[z] = lower[z] + toward[z] * lower[z - 1]
        for z in range(MIDDLE - 1, -1, -1):
            lower[z] = toward[z] * lower[z + 1]
        for z in range(LAST):
            chain[z], outward[z] = chained[z], toward[z]
            from_prev[z], from_last[z] = upper[z], lower[z]

        a_coef = up[LAST] * upper[LAST - 1]
        c_coef = down[LAST] * lane_roll(lower[0], -SPOTS)
        b_coef = diagonal[LAST] - up[LAST] * lower[LAST - 1] - down[LAST] * lane_roll(upper[0], -SPOTS)
        sep_up[...] = up[LAST]
        coefs = {0: jnp.ones(wide, F32)}
        for level in range(4):
            step = 1 << level
            hop = SPOTS * step
            b_inv = 1.0 / b_coef
            alpha = a_coef * lane_roll(b_inv, hop)
            gamma = c_coef * lane_roll(b_inv, -hop)
            b_coef = b_coef - alpha * lane_roll(c_coef, hop) - gamma * lane_roll(a_coef, -hop)
            a_coef, c_coef = alpha * lane_roll(a_coef, hop), gamma * lane_roll(c_coef, -hop)
            longer = dict(coefs)
            for j, coef in coefs.items():
                if 2 * step == BLOCKS:
                    moved = [((j + step) % BLOCKS, (alpha + gamma) * lane_roll(coef, hop))]
                else:
                    moved = [
                        ((j + step) % BLOCKS, alpha * lane_roll(coef, hop)),
                        ((j - step) % BLOCKS, gamma * lane_roll(coef, -hop)),
                    ]
                for at, term in moved:
                    longer[at] = longer[at] + term if at in longer else term
            coefs = longer
        b_inv = 1.0 / b_coef
        for j in range(BLOCKS):
            by_end = coefs[j] * b_inv
            by_start = by_end * lane_roll(down[LAST], SPOTS * j)
            last_end[j], last_start[(j - 1) % BLOCKS] = by_end, by_start
            prev_end[(j + 1) % BLOCKS], prev_start[j] = lane_roll(by_end, SPOTS), lane_roll(by_start, SPOTS)

        @pl.when((first & has_left) | (last & has_right))
        def _():
            pltpu.make_async_copy(wall_beside, wall_beside, wall_sem.at[0]).wait()

        @pl.when(jnp.logical_not((first & has_left) | (last & has_right)))
        def _():
            wall_beside[...] = jnp.zeros_like(wall_beside)

        beside = (first & (lane >= LANES - MARGIN)) | (last & (lane < MARGIN))
        window = jnp.where(beside, wall_beside[...], wall_mine[...])
        window = lane_roll_by(window, lax.rem(2 * LANES + MARGIN - mine * OWN, LANES))
        touching = []
        for g in range(GROUPS):
            spread = jnp.take_along_axis(window, GROUPS * (lane % SPOTS) + g, axis=1)
            springs[g] = jnp.broadcast_to(spread[0:1], (CROSS, LANES))
            touching.append(jnp.broadcast_to(spread[1:2], (CROSS, LANES)))
        touching = jnp.stack(touching)

        ahead_mask = (cross < CROSS - 1).astype(F32)
        back_mask = jnp.where(cross > 0, 1.0, touching)
        for z in range(ROWS):
            lateral = jnp.where(inside, pick(field[z], table, 1), 0.0)
            a1 = ALONG_RATE * lateral
            a2 = ACROSS_RATE * lateral
            a2b, a2a = a2 * back_mask, a2 * ahead_mask
            keep[z] = (1.0 - 2.0 * a1 - a2b - a2a) * inverse[z]
            along[z], back[z], ahead[z] = a1 * inverse[z], a2b * inverse[z], a2a * inverse[z]
        arrived(LOADING)
        for z in range(ROWS):
            source[z] = source[z] * inverse[z]
        arrived(PRESSURE)

        def solve(_, carry):
            spring_now = springs[...]
            scaled = []
            for z in range(ROWS):
                now = field[z]
                left = jnp.stack([lane_roll(now[3], 1), now[0], now[1], now[2]])
                right = jnp.stack([now[1], now[2], now[3], lane_roll(now[0], -1)])
                behind = jnp.where(cross == 0, spring_now, cross_roll(now, 1))
                scaled.append(
                    source[z] + keep[z] * now + along[z] * (left + right)
                    + back[z] * behind + ahead[z] * cross_roll(now, -1)
                )
            for z in range(1, MIDDLE):
                scaled[z] = scaled[z] + chain[z] * scaled[z - 1]
            for z in range(LAST - 2, MIDDLE, -1):
                scaled[z] = scaled[z] + chain[z] * scaled[z + 1]
            scaled[MIDDLE] = (
                scaled[MIDDLE] + chain[MIDDLE] * scaled[MIDDLE - 1] + outward[MIDDLE] * scaled[MIDDLE + 1]
            )
            for z in range(MIDDLE - 1, -1, -1):
                scaled[z] = scaled[z] + outward[z] * scaled[z + 1]
            for z in range(MIDDLE + 1, LAST):
                scaled[z] = scaled[z] + outward[z] * scaled[z - 1]
            end, start = scaled[LAST] + sep_up[...] * scaled[LAST - 1], scaled[0]
            ends, above = jnp.zeros(wide, F32), jnp.zeros(wide, F32)
            for j in range(BLOCKS):
                end_there, start_there = lane_roll(end, SPOTS * j), lane_roll(start, SPOTS * j)
                ends = ends + last_end[j] * end_there + last_start[j] * start_there
                above = above + prev_end[j] * end_there + prev_start[j] * start_there
            for z in range(LAST):
                field[z] = scaled[z] + from_prev[z] * above + from_last[z] * ends
            field[LAST] = ends
            return carry

        def outer_step(_, carry):
            lax.fori_loop(0, SUBSTEPS, solve, 0)
            base = ROWS * block.astype(F32) + 0.5
            moment = jnp.zeros(wide, F32)
            for z in range(ROWS):
                moment = moment + (base + float(z)) * field[z]
            row = lax.broadcasted_iota(jnp.int32, (CROSS, LANES), 0)
            face = jnp.where(row == 0, moment[0], 0.0)
            for g in range(1, GROUPS):
                face = jnp.where(row == g, cross_roll(moment[g], g), face)
            total = face
            for j in range(1, BLOCKS):
                total = total + lane_roll(face, SPOTS * j)
            total = total * (1.0 / (ROWS * BLOCKS) ** 2)
            moment = jnp.stack([cross_roll(total, -g) for g in range(GROUPS)])
            springs[...] = SPRING_KEEP * springs[...] + SPRING_DRIVE * touching * moment
            return carry

        lax.fori_loop(0, OUTER, outer_step, 0)

        for g in range(GROUPS):
            turned[g] = field[:, g].reshape(LANES, LANES).T
        flat_result = result.reshape(BLOCKS * ROOM, LANES)
        for at in range(OWN):
            i, g = divmod(MARGIN + at, GROUPS)
            for half in range(2):
                flat_result[pl.ds(at + half * 8 * ROOM, 8, stride=ROOM), :] = (
                    turned[g, pl.ds(i + half * 8 * SPOTS, 8, stride=SPOTS), :]
                )
        spring_row = jnp.zeros((8, LANES), F32)
        for g in range(GROUPS):
            spread = jnp.take_along_axis(
                springs[g], (MARGIN + lane % OWN) // GROUPS, axis=1
            )
            spring_row = jnp.where(lane % GROUPS == g, spread, spring_row)
        result[:, OWN:] = jnp.broadcast_to(spring_row[None], (BLOCKS, 8, LANES))

        for peer in peers:
            pltpu.make_async_remote_copy(
                src_ref=result.at[peer, pl.ds(0, SENT)], dst_ref=returned.at[mine, pl.ds(0, SENT)],
                send_sem=return_send.at[0], recv_sem=return_sem.at[0],
                device_id=(wall, peer), device_id_type=MESH,
            ).start()
        pltpu.make_async_copy(
            result.at[me, pl.ds(0, SENT)], returned.at[mine, pl.ds(0, SENT)], return_sem.at[0]
        ).start()

    def wait_dealt(count):
        sent = landed.reshape(3 * BLOCKS * WIDE, LANES).at[pl.ds(0, count * sum(WIDTHS))]
        pltpu.make_async_copy(sent, sent, send_sem.at[0]).wait()

    @pl.when(solves)
    def _():
        wait_dealt(SOLVERS - 1)

    @pl.when(jnp.logical_not(solves))
    def _():
        wait_dealt(SOLVERS)

    @pl.when(has_right)
    def _():
        for which in (LAYER, PRESSURE, LOADING):
            to_right(which).wait_send()

    @pl.when(has_left)
    def _():
        for which in (LAYER, PRESSURE, LOADING):
            to_left(which).wait_send()

    @pl.when(first & has_right)
    def _():
        wall_right.wait_send()

    @pl.when(last & has_left)
    def _():
        wall_left.wait_send()

    @pl.when(solves)
    def _():
        given = result.reshape(BLOCKS * ROOM, LANES).at[pl.ds(0, (BLOCKS - 1) * SENT)]
        pltpu.make_async_copy(given, given, return_send.at[0]).wait()

    back_here = returned.at[:, pl.ds(0, SENT)]
    pltpu.make_async_copy(back_here, back_here, return_sem.at[0]).wait()


def place_rows(returned, pressure_out, spring_out):
    planes = returned[:, 0:OWN].reshape(LANES, LANES).T
    flat = pressure_out.reshape(CROSS * ROWS, LANES)
    for z in range(ROWS):
        flat[pl.ds(z, CROSS, stride=ROWS), :] = planes[z * CROSS:(z + 1) * CROSS]
    owner = lax.broadcasted_iota(jnp.int32, (1, LANES), 1) // OWN
    total = jnp.zeros((1, LANES), F32)
    for d in range(SOLVERS):
        total = jnp.where(owner == d, returned[d, OWN:OWN + 1], total)
    spring_out[...] = total.reshape(spring_out.shape)


def lane_roll_by(x, shift):
    return pltpu.roll(x, shift, x.ndim - 1)


def on_device(pressure, layer, permeability, loading, spring, contact):
    vmem = pl.BlockSpec(memory_space=pltpu.VMEM)
    hbm = pl.BlockSpec(memory_space=pltpu.MemorySpace.HBM)
    planes = pltpu.VMEM((ROWS, GROUPS, CROSS, LANES), F32)
    plane = pltpu.VMEM((GROUPS, CROSS, LANES), F32)
    tile = pltpu.VMEM((8, LANES), F32)
    returned = pl.pallas_call(
        kernel,
        out_shape=jax.ShapeDtypeStruct((SOLVERS, ROOM, LANES), F32),
        in_specs=[hbm] * 6,
        out_specs=hbm,
        scratch_shapes=[
            pltpu.SMEM(permeability.shape, F32),
            pltpu.SMEM(contact.shape, jnp.int32),
            pltpu.VMEM(pressure.shape, F32),
            pltpu.VMEM(layer.shape, jnp.int32),
            pltpu.VMEM(loading.shape, F32),
            pltpu.VMEM(spring.shape, F32),
            pltpu.SemaphoreType.DMA((6,)),
            pltpu.VMEM((3, LANES + 2 * MARGIN, LANES), F32),
            pltpu.VMEM((3, BLOCKS, WIDE, LANES), F32),
            pltpu.VMEM((3, BLOCKS, MARGIN, LANES), F32),
            tile, tile,
            planes, planes, planes, planes, planes, planes,
            planes, planes, planes, planes,
            planes, planes, planes, planes, plane, plane,
            pltpu.VMEM((GROUPS, LANES, LANES), F32),
            pltpu.VMEM((BLOCKS, ROOM, LANES), F32),
            pltpu.SemaphoreType.DMA((1,)),
            pltpu.SemaphoreType.DMA((3,)),
            pltpu.SemaphoreType.DMA((2, 3)),
            pltpu.SemaphoreType.DMA((3,)),
            pltpu.SemaphoreType.DMA((1,)),
            pltpu.SemaphoreType.DMA((2,)),
            pltpu.SemaphoreType.DMA((1,)),
            pltpu.SemaphoreType.DMA((1,)),
        ],
        compiler_params=pltpu.CompilerParams(
            collective_id=0, has_side_effects=True, vmem_limit_bytes=60 << 20
        ),
    )(permeability, contact, pressure, layer, loading, spring)
    return pl.pallas_call(
        place_rows,
        out_shape=(
            jax.ShapeDtypeStruct(pressure.shape, F32),
            jax.ShapeDtypeStruct(spring.shape, F32),
        ),
        in_specs=[vmem],
        out_specs=(vmem, vmem),
    )(returned)


def solution(mesh):
    cells = P(None, "depth", "wall")
    return jax.shard_map(
        on_device,
        mesh=mesh,
        in_specs=(cells, cells, P(), cells, P("wall"), P("wall")),
        out_specs=(cells, P("wall")),
        check_vma=False,
    )
```

```python
import functools

import jax
import jax.numpy as jnp
from jax import lax
from jax.experimental import pallas as pl
from jax.experimental.pallas import tpu as pltpu
from jax.sharding import PartitionSpec as P

MESH = pl.DeviceIdType.MESH
F32 = jnp.float32

SOILS = 8
PANEL = 16
SUBSTEPS = 3
OUTER = 2
VNUM = 512.0
ALONG_RATE = 0.1
ACROSS_RATE = 0.06
SPRING_KEEP = 0.5
SPRING_DRIVE = 2.0

CROSS = 8
ROWS = 16
BLOCKS = 16
SOLVERS = 8
MOVED = 1
OWN = 16
MARGIN = 8
WIDE = OWN + 2 * MARGIN
SPOTS = 8
GROUPS = 4
LANES = 128
LAST = ROWS - 1
MIDDLE = 7
LAYER, PRESSURE, LOADING = 0, 1, 2
HALO = (5, 6, 5)
WIDTHS = tuple(OWN + 2 * halo for halo in HALO)
SIDE = 4
FAR_FIRST = sorted(
    ((dy, dx) for dy in range(SIDE) for dx in range(SIDE) if dy or dx),
    key=lambda at: -sum(min(step, SIDE - step) for step in at),
)
EARLY_FIRST = sorted(range(BLOCKS), key=lambda device: device // SIDE + device % SIDE)
SENT = OWN + 1
ROOM = OWN + 8


def lane_roll(x, shift):
    return pltpu.roll(x, shift % LANES, x.ndim - 1)


def cross_roll(x, shift):
    return pltpu.roll(x, shift % CROSS, x.ndim - 2)


def harmonic(a, b):
    return (2.0 * VNUM) * a * b / (a + b)


def pick(level, table, row):
    value = jnp.full(level.shape, table[row, 0], F32)
    for soil in range(1, SOILS):
        value = jnp.where(level == float(soil), table[row, soil], value)
    return value


def kernel(
    table_in, contact_in, pressure_in, layer_in, loading_in, spring_in,
    returned,
    table, contact, pressure, layer, loading, spring, in_sem,
    packed, landed, beyond, wall_mine, wall_beside,
    field, source, keep, along, back, ahead, chain, outward, from_prev, from_last,
    last_end, last_start, prev_end, prev_start, sep_up, springs,
    turned, result,
    send_sem, land_sem, side_send, side_sem, wall_sem, wall_send, return_send, return_sem,
):
    wall, me = lax.axis_index("wall"), lax.axis_index("depth")
    walls = lax.axis_size("wall")
    has_left, has_right = wall > 0, wall < walls - 1

    def shift_of(wall):
        return SOLVERS * lax.rem(wall, 2)

    def spot_of(device):
        at = lax.rem(device + BLOCKS - shift_of(wall), BLOCKS)
        return jnp.where(at < SOLVERS, lax.rem(at + SOLVERS - MOVED, SOLVERS), at)

    mine = spot_of(me)
    solves, first, last = mine < SOLVERS, mine == 0, mine == SOLVERS - 1
    left_end = (wall - 1, shift_of(wall + 1) + (SOLVERS - 1 + MOVED) % SOLVERS)
    right_end = (wall + 1, shift_of(wall + 1) + MOVED)

    inputs = [
        pltpu.make_async_copy(source_ref, here, in_sem.at[at])
        for at, (source_ref, here) in enumerate((
            (layer_in, layer), (pressure_in, pressure), (loading_in, loading),
            (spring_in, spring), (contact_in, contact), (table_in, table),
        ))
    ]
    for copy in inputs:
        copy.start()

    peers = [
        lax.rem(me // SIDE + dy, SIDE) * SIDE + lax.rem(me % SIDE + dx, SIDE) for dy, dx in FAR_FIRST
    ]

    barrier = pltpu.get_barrier_semaphore()

    @pl.when(solves)
    def _():
        for peer in peers:
            pl.semaphore_signal(barrier, inc=1, device_id=(wall, peer), device_id_type=MESH)

    @pl.when(first & has_left)
    def _():
        def call(k, _):
            pl.semaphore_signal(barrier, inc=1, device_id=(wall - 1, k), device_id_type=MESH)
            return 0

        lax.fori_loop(0, BLOCKS, call, 0)

    @pl.when(last & has_right)
    def _():
        def call(k, _):
            pl.semaphore_signal(barrier, inc=1, device_id=(wall + 1, k), device_id_type=MESH)
            return 0

        lax.fori_loop(0, BLOCKS, call, 0)

    def pack(which, ref):
        inputs[which].wait()
        flat = ref.reshape(CROSS * ROWS, LANES)
        planes = [flat[pl.ds(z, CROSS, stride=ROWS), :] for z in range(ROWS)]
        packed[which, MARGIN:MARGIN + LANES] = jnp.concatenate(planes, 0).astype(F32).T

    def to_peer(which, peer):
        width = OWN + 2 * HALO[which]
        return pltpu.make_async_remote_copy(
            src_ref=packed.at[which, pl.ds(spot_of(peer) * OWN + MARGIN - HALO[which], width)],
            dst_ref=landed.at[which, me, pl.ds(MARGIN - HALO[which], width)],
            send_sem=send_sem.at[0], recv_sem=land_sem.at[which],
            device_id=(wall, peer), device_id_type=MESH,
        )

    def to_self(which):
        width = OWN + 2 * HALO[which]
        return pltpu.make_async_copy(
            packed.at[which, pl.ds(mine * OWN + MARGIN - HALO[which], width)],
            landed.at[which, me, pl.ds(MARGIN - HALO[which], width)],
            land_sem.at[which],
        )

    def to_right(which):
        return pltpu.make_async_remote_copy(
            src_ref=packed.at[which, pl.ds(MARGIN + LANES - HALO[which], HALO[which])],
            dst_ref=beyond.at[which, me, pl.ds(MARGIN - HALO[which], HALO[which])],
            send_sem=side_send.at[0, which], recv_sem=side_sem.at[which],
            device_id=right_end, device_id_type=MESH,
        )

    def to_left(which):
        return pltpu.make_async_remote_copy(
            src_ref=packed.at[which, pl.ds(MARGIN, HALO[which])],
            dst_ref=beyond.at[which, me, pl.ds(0, HALO[which])],
            send_sem=side_send.at[1, which], recv_sem=side_sem.at[which],
            device_id=left_end, device_id_type=MESH,
        )

    for which in (LAYER, PRESSURE, LOADING):
        packed[which, 0:MARGIN] = jnp.zeros((MARGIN, LANES), F32)
        packed[which, MARGIN + LANES:] = jnp.zeros((MARGIN, LANES), F32)
    pack(LAYER, layer)
    pack(PRESSURE, pressure)
    pack(LOADING, loading)
    for copy in inputs[LOADING + 1:]:
        copy.wait()
    lane = lax.broadcasted_iota(jnp.int32, (8, LANES), 1)
    sub = lax.broadcasted_iota(jnp.int32, (8, LANES), 0)
    share = jnp.zeros((8, LANES), F32)
    for panel in range(LANES // PANEL):
        share = jnp.where(lane // PANEL == panel, contact[panel].astype(F32), share)
    own_spring = jnp.broadcast_to(spring[...].reshape(1, LANES), (8, LANES))
    wall_mine[...] = jnp.where(sub == 0, own_spring, share)
    wall_right = pltpu.make_async_remote_copy(
        src_ref=wall_mine, dst_ref=wall_beside, send_sem=wall_send.at[0], recv_sem=wall_sem.at[0],
        device_id=right_end, device_id_type=MESH,
    )
    wall_left = pltpu.make_async_remote_copy(
        src_ref=wall_mine, dst_ref=wall_beside, send_sem=wall_send.at[1], recv_sem=wall_sem.at[0],
        device_id=left_end, device_id_type=MESH,
    )

    sides = has_left.astype(jnp.int32) + has_right.astype(jnp.int32)
    pl.semaphore_wait(barrier, SOLVERS - solves.astype(jnp.int32) + sides)

    @pl.when(first & has_right)
    def _():
        wall_right.start()

    @pl.when(last & has_left)
    def _():
        wall_left.start()

    @pl.when(has_right)
    def _():
        for which in (LAYER, PRESSURE, LOADING):
            to_right(which).start()

    @pl.when(has_left)
    def _():
        for which in (LAYER, PRESSURE, LOADING):
            to_left(which).start()

    def deal(peer, *arrays):
        @pl.when(spot_of(peer) < SOLVERS)
        def _():
            for which in arrays:
                to_peer(which, peer).start()

    for peer in peers:
        deal(peer, LAYER)
    for peer in peers:
        deal(peer, PRESSURE, LOADING)

    @pl.when(solves)
    def _():
        for which in (LAYER, PRESSURE, LOADING):
            to_self(which).start()

    @pl.when(solves)
    def _():
        wide = (GROUPS, CROSS, LANES)
        lanes = lax.broadcasted_iota(jnp.int32, wide, 2)
        block = lanes // SPOTS
        column = GROUPS * (lanes % SPOTS) + lax.broadcasted_iota(jnp.int32, wide, 0)
        cross = lax.broadcasted_iota(jnp.int32, wide, 1)
        place = wall * LANES + mine * OWN - MARGIN + column
        inside = (place >= 0) & (place < walls * LANES)
        top, bottom = block == 0, block == BLOCKS - 1

        def arrived(which):
            valid = landed.at[which, :, pl.ds(MARGIN - HALO[which], OWN + 2 * HALO[which])]
            pltpu.make_async_copy(valid, valid, land_sem.at[which]).wait()

            @pl.when((first & has_left) | (last & has_right))
            def _():
                strip = beyond.at[which, :, pl.ds(0, HALO[which])]
                pltpu.make_async_copy(strip, strip, side_sem.at[which]).wait()

            @pl.when(first)
            def _():
                landed[which, :, 0:MARGIN] = jnp.where(has_left, beyond[which], 0.0)

            @pl.when(last)
            def _():
                landed[which, :, OWN + MARGIN:] = jnp.where(has_right, beyond[which], 0.0)

            for g in range(GROUPS):
                rows = [landed[which, s, pl.ds(g, SPOTS, stride=GROUPS), :] for s in range(BLOCKS)]
                planes = jnp.concatenate(rows, 0).T.reshape(ROWS, CROSS, LANES)
                field_or = source if which == LOADING else field
                field_or[:, g] = planes

        arrived(LAYER)
        perm = [pick(field[z], table, 0) for z in range(ROWS)]
        up = [None] * ROWS
        for z in range(1, ROWS):
            up[z] = harmonic(perm[z - 1], perm[z])
        up[0] = jnp.where(top, VNUM * perm[0], harmonic(lane_roll(perm[LAST], SPOTS), perm[0]))
        down = up[1:] + [jnp.where(bottom, 0.0, lane_roll(up[0], -SPOTS))]
        diagonal = [1.0 + up[z] + down[z] for z in range(ROWS)]

        inverse, toward = [None] * ROWS, [None] * ROWS
        chained = [None] * ROWS
        for z in range(MIDDLE):
            pivot = diagonal[z] if z == 0 else diagonal[z] - up[z] * toward[z - 1]
            inverse[z] = 1.0 / pivot
            toward[z] = down[z] * inverse[z]
            chained[z] = up[z] * inverse[z]
        for z in range(LAST - 1, MIDDLE, -1):
            pivot = diagonal[z] if z == LAST - 1 else diagonal[z] - down[z] * toward[z + 1]
            inverse[z] = 1.0 / pivot
            toward[z] = up[z] * inverse[z]
            chained[z] = down[z] * inverse[z]
        inverse[MIDDLE] = 1.0 / (
            diagonal[MIDDLE] - up[MIDDLE] * toward[MIDDLE - 1] - down[MIDDLE] * toward[MIDDLE + 1]
        )
        chained[MIDDLE] = up[MIDDLE] * inverse[MIDDLE]
        toward[MIDDLE] = down[MIDDLE] * inverse[MIDDLE]
        inverse[LAST] = jnp.ones(wide, F32)

        upper, lower = [None] * LAST, [None] * LAST
        upper[0] = jnp.where(top, 0.0, chained[0])
        for z in range(1, MIDDLE):
            upper[z] = chained[z] * upper[z - 1]
        upper[MIDDLE] = chained[MIDDLE] * upper[MIDDLE - 1]
        for z in range(MIDDLE - 1, -1, -1):
            upper[z] = upper[z] + toward[z] * upper[z + 1]
        for z in range(MIDDLE + 1, LAST):
            upper[z] = toward[z] * upper[z - 1]
        lower[LAST - 1] = chained[LAST - 1]
        for z in range(LAST - 2, MIDDLE, -1):
            lower[z] = chained[z] * lower[z + 1]
        lower[MIDDLE] = toward[MIDDLE] * lower[MIDDLE + 1]
        for z in range(MIDDLE + 1, LAST):
            lower[z] = lower[z] + toward[z] * lower[z - 1]
        for z in range(MIDDLE - 1, -1, -1):
            lower[z] = toward[z] * lower[z + 1]
        for z in range(LAST):
            chain[z], outward[z] = chained[z], toward[z]
            from_prev[z], from_last[z] = upper[z], lower[z]

        a_coef = up[LAST] * upper[LAST - 1]
        c_coef = down[LAST] * lane_roll(lower[0], -SPOTS)
        b_coef = diagonal[LAST] - up[LAST] * lower[LAST - 1] - down[LAST] * lane_roll(upper[0], -SPOTS)
        sep_up[...] = up[LAST]
        coefs = {0: jnp.ones(wide, F32)}
        for level in range(4):
            step = 1 << level
            hop = SPOTS * step
            b_inv = 1.0 / b_coef
            alpha = a_coef * lane_roll(b_inv, hop)
            gamma = c_coef * lane_roll(b_inv, -hop)
            b_coef = b_coef - alpha * lane_roll(c_coef, hop) - gamma * lane_roll(a_coef, -hop)
            a_coef, c_coef = alpha * lane_roll(a_coef, hop), gamma * lane_roll(c_coef, -hop)
            longer = dict(coefs)
            for j, coef in coefs.items():
                if 2 * step == BLOCKS:
                    moved = [((j + step) % BLOCKS, (alpha + gamma) * lane_roll(coef, hop))]
                else:
                    moved = [
                        ((j + step) % BLOCKS, alpha * lane_roll(coef, hop)),
                        ((j - step) % BLOCKS, gamma * lane_roll(coef, -hop)),
                    ]
                for at, term in moved:
                    longer[at] = longer[at] + term if at in longer else term
            coefs = longer
        b_inv = 1.0 / b_coef
        for j in range(BLOCKS):
            by_end = coefs[j] * b_inv
            by_start = by_end * lane_roll(down[LAST], SPOTS * j)
            last_end[j], last_start[(j - 1) % BLOCKS] = by_end, by_start
            prev_end[(j + 1) % BLOCKS], prev_start[j] = lane_roll(by_end, SPOTS), lane_roll(by_start, SPOTS)

        @pl.when((first & has_left) | (last & has_right))
        def _():
            pltpu.make_async_copy(wall_beside, wall_beside, wall_sem.at[0]).wait()

        @pl.when(jnp.logical_not((first & has_left) | (last & has_right)))
        def _():
            wall_beside[...] = jnp.zeros_like(wall_beside)

        beside = (first & (lane >= LANES - MARGIN)) | (last & (lane < MARGIN))
        window = jnp.where(beside, wall_beside[...], wall_mine[...])
        window = lane_roll_by(window, lax.rem(2 * LANES + MARGIN - mine * OWN, LANES))
        touching = []
        for g in range(GROUPS):
            spread = jnp.take_along_axis(window, GROUPS * (lane % SPOTS) + g, axis=1)
            springs[g] = jnp.broadcast_to(spread[0:1], (CROSS, LANES))
            touching.append(jnp.broadcast_to(spread[1:2], (CROSS, LANES)))
        touching = jnp.stack(touching)

        ahead_mask = (cross < CROSS - 1).astype(F32)
        back_mask = jnp.where(cross > 0, 1.0, touching)
        for z in range(ROWS):
            lateral = jnp.where(inside, pick(field[z], table, 1), 0.0)
            a1 = ALONG_RATE * lateral
            a2 = ACROSS_RATE * lateral
            a2b, a2a = a2 * back_mask, a2 * ahead_mask
            keep[z] = (1.0 - 2.0 * a1 - a2b - a2a) * inverse[z]
            along[z], back[z], ahead[z] = a1 * inverse[z], a2b * inverse[z], a2a * inverse[z]
        arrived(LOADING)
        for z in range(ROWS):
            source[z] = source[z] * inverse[z]
        arrived(PRESSURE)

        def solve(_, carry):
            spring_now = springs[...]
            scaled = []
            for z in range(ROWS):
                now = field[z]
                left = jnp.stack([lane_roll(now[3], 1), now[0], now[1], now[2]])
                right = jnp.stack([now[1], now[2], now[3], lane_roll(now[0], -1)])
                behind = jnp.where(cross == 0, spring_now, cross_roll(now, 1))
                scaled.append(
                    source[z] + keep[z] * now + along[z] * (left + right)
                    + back[z] * behind + ahead[z] * cross_roll(now, -1)
                )
            for z in range(1, MIDDLE):
                scaled[z] = scaled[z] + chain[z] * scaled[z - 1]
            for z in range(LAST - 2, MIDDLE, -1):
                scaled[z] = scaled[z] + chain[z] * scaled[z + 1]
            scaled[MIDDLE] = (
                scaled[MIDDLE] + chain[MIDDLE] * scaled[MIDDLE - 1] + outward[MIDDLE] * scaled[MIDDLE + 1]
            )
            for z in range(MIDDLE - 1, -1, -1):
                scaled[z] = scaled[z] + outward[z] * scaled[z + 1]
            for z in range(MIDDLE + 1, LAST):
                scaled[z] = scaled[z] + outward[z] * scaled[z - 1]
            end, start = scaled[LAST] + sep_up[...] * scaled[LAST - 1], scaled[0]
            ends, above = jnp.zeros(wide, F32), jnp.zeros(wide, F32)
            for j in range(BLOCKS):
                end_there, start_there = lane_roll(end, SPOTS * j), lane_roll(start, SPOTS * j)
                ends = ends + last_end[j] * end_there + last_start[j] * start_there
                above = above + prev_end[j] * end_there + prev_start[j] * start_there
            for z in range(LAST):
                field[z] = scaled[z] + from_prev[z] * above + from_last[z] * ends
            field[LAST] = ends
            return carry

        def outer_step(_, carry):
            lax.fori_loop(0, SUBSTEPS, solve, 0, unroll=True)
            base = ROWS * block.astype(F32) + 0.5
            moment = jnp.zeros(wide, F32)
            for z in range(ROWS):
                moment = moment + (base + float(z)) * field[z]
            row = lax.broadcasted_iota(jnp.int32, (CROSS, LANES), 0)
            face = jnp.where(row == 0, moment[0], 0.0)
            for g in range(1, GROUPS):
                face = jnp.where(row == g, cross_roll(moment[g], g), face)
            total = face
            for j in range(1, BLOCKS):
                total = total + lane_roll(face, SPOTS * j)
            total = total * (1.0 / (ROWS * BLOCKS) ** 2)
            moment = jnp.stack([cross_roll(total, -g) for g in range(GROUPS)])
            springs[...] = SPRING_KEEP * springs[...] + SPRING_DRIVE * touching * moment
            return carry

        for step in range(OUTER):
            outer_step(step, 0)

        for g in range(GROUPS):
            turned[g] = field[:, g].reshape(LANES, LANES).T
        flat_result = result.reshape(BLOCKS * ROOM, LANES)
        for at in range(OWN):
            i, g = divmod(MARGIN + at, GROUPS)
            for half in range(2):
                flat_result[pl.ds(at + half * 8 * ROOM, 8, stride=ROOM), :] = (
                    turned[g, pl.ds(i + half * 8 * SPOTS, 8, stride=SPOTS), :]
                )
        spring_row = jnp.zeros((8, LANES), F32)
        for g in range(GROUPS):
            spread = jnp.take_along_axis(
                springs[g], (MARGIN + lane % OWN) // GROUPS, axis=1
            )
            spring_row = jnp.where(lane % GROUPS == g, spread, spring_row)
        result[:, OWN:] = jnp.broadcast_to(spring_row[None], (BLOCKS, 8, LANES))

        def give_back(device):
            pltpu.make_async_remote_copy(
                src_ref=result.at[device, pl.ds(0, SENT)], dst_ref=returned.at[mine, pl.ds(0, SENT)],
                send_sem=return_send.at[0], recv_sem=return_sem.at[0],
                device_id=(wall, device), device_id_type=MESH,
            ).start()

        for device in EARLY_FIRST:
            pl.when(me != device)(functools.partial(give_back, device))
        pltpu.make_async_copy(
            result.at[me, pl.ds(0, SENT)], returned.at[mine, pl.ds(0, SENT)], return_sem.at[0]
        ).start()

    def wait_dealt(count):
        sent = landed.reshape(3 * BLOCKS * WIDE, LANES).at[pl.ds(0, count * sum(WIDTHS))]
        pltpu.make_async_copy(sent, sent, send_sem.at[0]).wait()

    @pl.when(solves)
    def _():
        wait_dealt(SOLVERS - 1)

    @pl.when(jnp.logical_not(solves))
    def _():
        wait_dealt(SOLVERS)

    @pl.when(has_right)
    def _():
        for which in (LAYER, PRESSURE, LOADING):
            to_right(which).wait_send()

    @pl.when(has_left)
    def _():
        for which in (LAYER, PRESSURE, LOADING):
            to_left(which).wait_send()

    @pl.when(first & has_right)
    def _():
        wall_right.wait_send()

    @pl.when(last & has_left)
    def _():
        wall_left.wait_send()

    @pl.when(solves)
    def _():
        given = result.reshape(BLOCKS * ROOM, LANES).at[pl.ds(0, (BLOCKS - 1) * SENT)]
        pltpu.make_async_copy(given, given, return_send.at[0]).wait()

    back_here = returned.at[:, pl.ds(0, SENT)]
    pltpu.make_async_copy(back_here, back_here, return_sem.at[0]).wait()


def place_rows(returned, pressure_out, spring_out):
    planes = returned[:, 0:OWN].reshape(LANES, LANES).T
    flat = pressure_out.reshape(CROSS * ROWS, LANES)
    for z in range(ROWS):
        flat[pl.ds(z, CROSS, stride=ROWS), :] = planes[z * CROSS:(z + 1) * CROSS]
    owner = lax.broadcasted_iota(jnp.int32, (1, LANES), 1) // OWN
    total = jnp.zeros((1, LANES), F32)
    for d in range(SOLVERS):
        total = jnp.where(owner == d, returned[d, OWN:OWN + 1], total)
    spring_out[...] = total.reshape(spring_out.shape)


def lane_roll_by(x, shift):
    return pltpu.roll(x, shift, x.ndim - 1)


def on_device(pressure, layer, permeability, loading, spring, contact):
    vmem = pl.BlockSpec(memory_space=pltpu.VMEM)
    hbm = pl.BlockSpec(memory_space=pltpu.MemorySpace.HBM)
    planes = pltpu.VMEM((ROWS, GROUPS, CROSS, LANES), F32)
    plane = pltpu.VMEM((GROUPS, CROSS, LANES), F32)
    tile = pltpu.VMEM((8, LANES), F32)
    returned = pl.pallas_call(
        kernel,
        out_shape=jax.ShapeDtypeStruct((SOLVERS, ROOM, LANES), F32),
        in_specs=[hbm] * 6,
        out_specs=hbm,
        scratch_shapes=[
            pltpu.SMEM(permeability.shape, F32),
            pltpu.SMEM(contact.shape, jnp.int32),
            pltpu.VMEM(pressure.shape, F32),
            pltpu.VMEM(layer.shape, jnp.int32),
            pltpu.VMEM(loading.shape, F32),
            pltpu.VMEM(spring.shape, F32),
            pltpu.SemaphoreType.DMA((6,)),
            pltpu.VMEM((3, LANES + 2 * MARGIN, LANES), F32),
            pltpu.VMEM((3, BLOCKS, WIDE, LANES), F32),
            pltpu.VMEM((3, BLOCKS, MARGIN, LANES), F32),
            tile, tile,
            planes, planes, planes, planes, planes, planes,
            planes, planes, planes, planes,
            planes, planes, planes, planes, plane, plane,
            pltpu.VMEM((GROUPS, LANES, LANES), F32),
            pltpu.VMEM((BLOCKS, ROOM, LANES), F32),
            pltpu.SemaphoreType.DMA((1,)),
            pltpu.SemaphoreType.DMA((3,)),
            pltpu.SemaphoreType.DMA((2, 3)),
            pltpu.SemaphoreType.DMA((3,)),
            pltpu.SemaphoreType.DMA((1,)),
            pltpu.SemaphoreType.DMA((2,)),
            pltpu.SemaphoreType.DMA((1,)),
            pltpu.SemaphoreType.DMA((1,)),
        ],
        compiler_params=pltpu.CompilerParams(
            collective_id=0, has_side_effects=True, vmem_limit_bytes=60 << 20
        ),
    )(permeability, contact, pressure, layer, loading, spring)
    return pl.pallas_call(
        place_rows,
        out_shape=(
            jax.ShapeDtypeStruct(pressure.shape, F32),
            jax.ShapeDtypeStruct(spring.shape, F32),
        ),
        in_specs=[vmem],
        out_specs=(vmem, vmem),
    )(returned)


def solution(mesh):
    cells = P(None, "depth", "wall")
    return jax.shard_map(
        on_device,
        mesh=mesh,
        in_specs=(cells, cells, P(), cells, P("wall"), P("wall")),
        out_specs=(cells, P("wall")),
        check_vma=False,
    )
```

```python
import functools

import jax
import jax.numpy as jnp
from jax import lax
from jax.experimental import pallas as pl
from jax.experimental.pallas import tpu as pltpu
from jax.sharding import PartitionSpec as P

MESH = pl.DeviceIdType.MESH
F32 = jnp.float32

SOILS = 8
PANEL = 16
SUBSTEPS = 3
OUTER = 2
VNUM = 512.0
ALONG_RATE = 0.1
ACROSS_RATE = 0.06
SPRING_KEEP = 0.5
SPRING_DRIVE = 2.0

CROSS = 8
ROWS = 16
BLOCKS = 16
SOLVERS = 8
MOVED = 1
OWN = 16
MARGIN = 8
WIDE = OWN + 2 * MARGIN
SPOTS = 8
GROUPS = 4
LANES = 128
LAST = ROWS - 1
MIDDLE = 7
LAYER, PRESSURE, LOADING = 0, 1, 2
HALO = (5, 6, 5)
WIDTHS = tuple(OWN + 2 * halo for halo in HALO)
SIDE = 4
FAR_FIRST = sorted(
    ((dy, dx) for dy in range(SIDE) for dx in range(SIDE) if dy or dx),
    key=lambda at: -sum(min(step, SIDE - step) for step in at),
)
EARLY_FIRST = sorted(range(BLOCKS), key=lambda device: device // SIDE + device % SIDE)
SENT = OWN + 1
ROOM = OWN + 8


def lane_roll(x, shift):
    return pltpu.roll(x, shift % LANES, x.ndim - 1)


def cross_roll(x, shift):
    return pltpu.roll(x, shift % CROSS, x.ndim - 2)


def harmonic(a, b):
    return (2.0 * VNUM) * a * b / (a + b)


def pick(level, table, row):
    value = jnp.full(level.shape, table[row, 0], F32)
    for soil in range(1, SOILS):
        value = jnp.where(level == float(soil), table[row, soil], value)
    return value


def kernel(
    table_in, contact_in, pressure_in, layer_in, loading_in, spring_in,
    returned,
    table, contact, pressure, layer, loading, spring, in_sem,
    packed, landed, beyond, wall_mine, wall_beside,
    field, source, keep, along, back, ahead, chain, outward, from_prev, from_last,
    last_end, last_start, prev_end, prev_start, sep_up, springs,
    turned, result,
    send_sem, land_sem, side_send, side_sem, wall_sem, wall_send, return_send, return_sem,
):
    wall, me = lax.axis_index("wall"), lax.axis_index("depth")
    walls = lax.axis_size("wall")
    has_left, has_right = wall > 0, wall < walls - 1

    def spot_of(device):
        row, at = device // SIDE, device % SIDE
        place = lax.rem(2 * row + at % 2 + SOLVERS - MOVED, SOLVERS)
        return jnp.where(at // 2 == lax.rem(wall, 2), place, SOLVERS)

    def device_of(spot, wall):
        place = (spot + MOVED) % SOLVERS
        return place // 2 * SIDE + 2 * lax.rem(wall, 2) + place % 2

    mine = spot_of(me)
    solves, first, last = mine < SOLVERS, mine == 0, mine == SOLVERS - 1
    left_end = (wall - 1, device_of(SOLVERS - 1, wall + 1))
    right_end = (wall + 1, device_of(0, wall + 1))

    inputs = [
        pltpu.make_async_copy(source_ref, here, in_sem.at[at])
        for at, (source_ref, here) in enumerate((
            (layer_in, layer), (pressure_in, pressure), (loading_in, loading),
            (spring_in, spring), (contact_in, contact), (table_in, table),
        ))
    ]
    for copy in inputs:
        copy.start()

    peers = [
        lax.rem(me // SIDE + dy, SIDE) * SIDE + lax.rem(me % SIDE + dx, SIDE) for dy, dx in FAR_FIRST
    ]

    barrier = pltpu.get_barrier_semaphore()

    @pl.when(solves)
    def _():
        for peer in peers:
            pl.semaphore_signal(barrier, inc=1, device_id=(wall, peer), device_id_type=MESH)

    @pl.when(first & has_left)
    def _():
        for k in reversed(range(BLOCKS)):
            pl.semaphore_signal(barrier, inc=1, device_id=(wall - 1, k), device_id_type=MESH)

    @pl.when(last & has_right)
    def _():
        for k in reversed(range(BLOCKS)):
            pl.semaphore_signal(barrier, inc=1, device_id=(wall + 1, k), device_id_type=MESH)

    def pack(which, ref):
        inputs[which].wait()
        flat = ref.reshape(CROSS * ROWS, LANES)
        planes = [flat[pl.ds(z, CROSS, stride=ROWS), :] for z in range(ROWS)]
        packed[which, MARGIN:MARGIN + LANES] = jnp.concatenate(planes, 0).astype(F32).T

    def to_peer(which, peer):
        width = OWN + 2 * HALO[which]
        return pltpu.make_async_remote_copy(
            src_ref=packed.at[which, pl.ds(spot_of(peer) * OWN + MARGIN - HALO[which], width)],
            dst_ref=landed.at[which, me, pl.ds(MARGIN - HALO[which], width)],
            send_sem=send_sem.at[0], recv_sem=land_sem.at[which],
            device_id=(wall, peer), device_id_type=MESH,
        )

    def to_self(which):
        width = OWN + 2 * HALO[which]
        return pltpu.make_async_copy(
            packed.at[which, pl.ds(mine * OWN + MARGIN - HALO[which], width)],
            landed.at[which, me, pl.ds(MARGIN - HALO[which], width)],
            land_sem.at[which],
        )

    def to_right(which):
        return pltpu.make_async_remote_copy(
            src_ref=packed.at[which, pl.ds(MARGIN + LANES - HALO[which], HALO[which])],
            dst_ref=beyond.at[which, me, pl.ds(MARGIN - HALO[which], HALO[which])],
            send_sem=side_send.at[0, which], recv_sem=side_sem.at[which],
            device_id=right_end, device_id_type=MESH,
        )

    def to_left(which):
        return pltpu.make_async_remote_copy(
            src_ref=packed.at[which, pl.ds(MARGIN, HALO[which])],
            dst_ref=beyond.at[which, me, pl.ds(0, HALO[which])],
            send_sem=side_send.at[1, which], recv_sem=side_sem.at[which],
            device_id=left_end, device_id_type=MESH,
        )

    for which in (LAYER, PRESSURE, LOADING):
        packed[which, 0:MARGIN] = jnp.zeros((MARGIN, LANES), F32)
        packed[which, MARGIN + LANES:] = jnp.zeros((MARGIN, LANES), F32)
    pack(LAYER, layer)
    pack(PRESSURE, pressure)
    pack(LOADING, loading)
    for copy in inputs[LOADING + 1:]:
        copy.wait()
    lane = lax.broadcasted_iota(jnp.int32, (8, LANES), 1)
    sub = lax.broadcasted_iota(jnp.int32, (8, LANES), 0)
    share = jnp.zeros((8, LANES), F32)
    for panel in range(LANES // PANEL):
        share = jnp.where(lane // PANEL == panel, contact[panel].astype(F32), share)
    own_spring = jnp.broadcast_to(spring[...].reshape(1, LANES), (8, LANES))
    wall_mine[...] = jnp.where(sub == 0, own_spring, share)
    wall_right = pltpu.make_async_remote_copy(
        src_ref=wall_mine, dst_ref=wall_beside, send_sem=wall_send.at[0], recv_sem=wall_sem.at[0],
        device_id=right_end, device_id_type=MESH,
    )
    wall_left = pltpu.make_async_remote_copy(
        src_ref=wall_mine, dst_ref=wall_beside, send_sem=wall_send.at[1], recv_sem=wall_sem.at[0],
        device_id=left_end, device_id_type=MESH,
    )

    sides = has_left.astype(jnp.int32) + has_right.astype(jnp.int32)
    pl.semaphore_wait(barrier, SOLVERS - solves.astype(jnp.int32) + sides)

    @pl.when(first & has_right)
    def _():
        wall_right.start()

    @pl.when(last & has_left)
    def _():
        wall_left.start()

    @pl.when(has_right)
    def _():
        for which in (LAYER, PRESSURE, LOADING):
            to_right(which).start()

    @pl.when(has_left)
    def _():
        for which in (LAYER, PRESSURE, LOADING):
            to_left(which).start()

    def deal(peer, *arrays):
        @pl.when(spot_of(peer) < SOLVERS)
        def _():
            for which in arrays:
                to_peer(which, peer).start()

    for peer in peers:
        deal(peer, LAYER)
    for peer in peers:
        deal(peer, PRESSURE, LOADING)

    @pl.when(solves)
    def _():
        for which in (LAYER, PRESSURE, LOADING):
            to_self(which).start()

    @pl.when(solves)
    def _():
        wide = (GROUPS, CROSS, LANES)
        lanes = lax.broadcasted_iota(jnp.int32, wide, 2)
        block = lanes // SPOTS
        column = GROUPS * (lanes % SPOTS) + lax.broadcasted_iota(jnp.int32, wide, 0)
        cross = lax.broadcasted_iota(jnp.int32, wide, 1)
        place = wall * LANES + mine * OWN - MARGIN + column
        inside = (place >= 0) & (place < walls * LANES)
        top, bottom = block == 0, block == BLOCKS - 1

        def arrived(which):
            valid = landed.at[which, :, pl.ds(MARGIN - HALO[which], OWN + 2 * HALO[which])]
            pltpu.make_async_copy(valid, valid, land_sem.at[which]).wait()

            @pl.when((first & has_left) | (last & has_right))
            def _():
                strip = beyond.at[which, :, pl.ds(0, HALO[which])]
                pltpu.make_async_copy(strip, strip, side_sem.at[which]).wait()

            @pl.when(first)
            def _():
                landed[which, :, 0:MARGIN] = jnp.where(has_left, beyond[which], 0.0)

            @pl.when(last)
            def _():
                landed[which, :, OWN + MARGIN:] = jnp.where(has_right, beyond[which], 0.0)

            for g in range(GROUPS):
                rows = [landed[which, s, pl.ds(g, SPOTS, stride=GROUPS), :] for s in range(BLOCKS)]
                planes = jnp.concatenate(rows, 0).T.reshape(ROWS, CROSS, LANES)
                field_or = source if which == LOADING else field
                field_or[:, g] = planes

        arrived(LAYER)
        perm = [pick(field[z], table, 0) for z in range(ROWS)]
        up = [None] * ROWS
        for z in range(1, ROWS):
            up[z] = harmonic(perm[z - 1], perm[z])
        up[0] = jnp.where(top, VNUM * perm[0], harmonic(lane_roll(perm[LAST], SPOTS), perm[0]))
        down = up[1:] + [jnp.where(bottom, 0.0, lane_roll(up[0], -SPOTS))]
        diagonal = [1.0 + up[z] + down[z] for z in range(ROWS)]

        inverse, toward = [None] * ROWS, [None] * ROWS
        chained = [None] * ROWS
        for z in range(MIDDLE):
            pivot = diagonal[z] if z == 0 else diagonal[z] - up[z] * toward[z - 1]
            inverse[z] = 1.0 / pivot
            toward[z] = down[z] * inverse[z]
            chained[z] = up[z] * inverse[z]
        for z in range(LAST - 1, MIDDLE, -1):
            pivot = diagonal[z] if z == LAST - 1 else diagonal[z] - down[z] * toward[z + 1]
            inverse[z] = 1.0 / pivot
            toward[z] = up[z] * inverse[z]
            chained[z] = down[z] * inverse[z]
        inverse[MIDDLE] = 1.0 / (
            diagonal[MIDDLE] - up[MIDDLE] * toward[MIDDLE - 1] - down[MIDDLE] * toward[MIDDLE + 1]
        )
        chained[MIDDLE] = up[MIDDLE] * inverse[MIDDLE]
        toward[MIDDLE] = down[MIDDLE] * inverse[MIDDLE]
        inverse[LAST] = jnp.ones(wide, F32)

        upper, lower = [None] * LAST, [None] * LAST
        upper[0] = jnp.where(top, 0.0, chained[0])
        for z in range(1, MIDDLE):
            upper[z] = chained[z] * upper[z - 1]
        upper[MIDDLE] = chained[MIDDLE] * upper[MIDDLE - 1]
        for z in range(MIDDLE - 1, -1, -1):
            upper[z] = upper[z] + toward[z] * upper[z + 1]
        for z in range(MIDDLE + 1, LAST):
            upper[z] = toward[z] * upper[z - 1]
        lower[LAST - 1] = chained[LAST - 1]
        for z in range(LAST - 2, MIDDLE, -1):
            lower[z] = chained[z] * lower[z + 1]
        lower[MIDDLE] = toward[MIDDLE] * lower[MIDDLE + 1]
        for z in range(MIDDLE + 1, LAST):
            lower[z] = lower[z] + toward[z] * lower[z - 1]
        for z in range(MIDDLE - 1, -1, -1):
            lower[z] = toward[z] * lower[z + 1]
        for z in range(LAST):
            chain[z], outward[z] = chained[z], toward[z]
            from_prev[z], from_last[z] = upper[z], lower[z]

        a_coef = up[LAST] * upper[LAST - 1]
        c_coef = down[LAST] * lane_roll(lower[0], -SPOTS)
        b_coef = diagonal[LAST] - up[LAST] * lower[LAST - 1] - down[LAST] * lane_roll(upper[0], -SPOTS)
        sep_up[...] = up[LAST]
        coefs = {0: jnp.ones(wide, F32)}
        for level in range(4):
            step = 1 << level
            hop = SPOTS * step
            b_inv = 1.0 / b_coef
            alpha = a_coef * lane_roll(b_inv, hop)
            gamma = c_coef * lane_roll(b_inv, -hop)
            b_coef = b_coef - alpha * lane_roll(c_coef, hop) - gamma * lane_roll(a_coef, -hop)
            a_coef, c_coef = alpha * lane_roll(a_coef, hop), gamma * lane_roll(c_coef, -hop)
            longer = dict(coefs)
            for j, coef in coefs.items():
                if 2 * step == BLOCKS:
                    moved = [((j + step) % BLOCKS, (alpha + gamma) * lane_roll(coef, hop))]
                else:
                    moved = [
                        ((j + step) % BLOCKS, alpha * lane_roll(coef, hop)),
                        ((j - step) % BLOCKS, gamma * lane_roll(coef, -hop)),
                    ]
                for at, term in moved:
                    longer[at] = longer[at] + term if at in longer else term
            coefs = longer
        b_inv = 1.0 / b_coef
        for j in range(BLOCKS):
            by_end = coefs[j] * b_inv
            by_start = by_end * lane_roll(down[LAST], SPOTS * j)
            last_end[j], last_start[(j - 1) % BLOCKS] = by_end, by_start
            prev_end[(j + 1) % BLOCKS], prev_start[j] = lane_roll(by_end, SPOTS), lane_roll(by_start, SPOTS)

        @pl.when((first & has_left) | (last & has_right))
        def _():
            pltpu.make_async_copy(wall_beside, wall_beside, wall_sem.at[0]).wait()

        @pl.when(jnp.logical_not((first & has_left) | (last & has_right)))
        def _():
            wall_beside[...] = jnp.zeros_like(wall_beside)

        beside = (first & (lane >= LANES - MARGIN)) | (last & (lane < MARGIN))
        window = jnp.where(beside, wall_beside[...], wall_mine[...])
        window = lane_roll_by(window, lax.rem(2 * LANES + MARGIN - mine * OWN, LANES))
        touching = []
        for g in range(GROUPS):
            spread = jnp.take_along_axis(window, GROUPS * (lane % SPOTS) + g, axis=1)
            springs[g] = jnp.broadcast_to(spread[0:1], (CROSS, LANES))
            touching.append(jnp.broadcast_to(spread[1:2], (CROSS, LANES)))
        touching = jnp.stack(touching)

        ahead_mask = (cross < CROSS - 1).astype(F32)
        back_mask = jnp.where(cross > 0, 1.0, touching)
        for z in range(ROWS):
            lateral = jnp.where(inside, pick(field[z], table, 1), 0.0)
            a1 = ALONG_RATE * lateral
            a2 = ACROSS_RATE * lateral
            a2b, a2a = a2 * back_mask, a2 * ahead_mask
            keep[z] = (1.0 - 2.0 * a1 - a2b - a2a) * inverse[z]
            along[z], back[z], ahead[z] = a1 * inverse[z], a2b * inverse[z], a2a * inverse[z]
        arrived(PRESSURE)
        arrived(LOADING)
        for z in range(ROWS):
            source[z] = source[z] * inverse[z]

        def solve(_, carry):
            spring_now = springs[...]
            scaled = []
            for z in range(ROWS):
                now = field[z]
                left = jnp.stack([lane_roll(now[3], 1), now[0], now[1], now[2]])
                right = jnp.stack([now[1], now[2], now[3], lane_roll(now[0], -1)])
                behind = jnp.where(cross == 0, spring_now, cross_roll(now, 1))
                scaled.append(
                    source[z] + keep[z] * now + along[z] * (left + right)
                    + back[z] * behind + ahead[z] * cross_roll(now, -1)
                )
            for z in range(1, MIDDLE):
                scaled[z] = scaled[z] + chain[z] * scaled[z - 1]
            for z in range(LAST - 2, MIDDLE, -1):
                scaled[z] = scaled[z] + chain[z] * scaled[z + 1]
            scaled[MIDDLE] = (
                scaled[MIDDLE] + chain[MIDDLE] * scaled[MIDDLE - 1] + outward[MIDDLE] * scaled[MIDDLE + 1]
            )
            for z in range(MIDDLE - 1, -1, -1):
                scaled[z] = scaled[z] + outward[z] * scaled[z + 1]
            for z in range(MIDDLE + 1, LAST):
                scaled[z] = scaled[z] + outward[z] * scaled[z - 1]
            end, start = scaled[LAST] + sep_up[...] * scaled[LAST - 1], scaled[0]
            ends, above = jnp.zeros(wide, F32), jnp.zeros(wide, F32)
            for j in range(BLOCKS):
                end_there, start_there = lane_roll(end, SPOTS * j), lane_roll(start, SPOTS * j)
                ends = ends + last_end[j] * end_there + last_start[j] * start_there
                above = above + prev_end[j] * end_there + prev_start[j] * start_there
            for z in range(LAST):
                field[z] = scaled[z] + from_prev[z] * above + from_last[z] * ends
            field[LAST] = ends
            return carry

        def outer_step(_, carry):
            lax.fori_loop(0, SUBSTEPS, solve, 0, unroll=True)
            base = ROWS * block.astype(F32) + 0.5
            moment = jnp.zeros(wide, F32)
            for z in range(ROWS):
                moment = moment + (base + float(z)) * field[z]
            row = lax.broadcasted_iota(jnp.int32, (CROSS, LANES), 0)
            face = jnp.where(row == 0, moment[0], 0.0)
            for g in range(1, GROUPS):
                face = jnp.where(row == g, cross_roll(moment[g], g), face)
            total = face
            for j in range(1, BLOCKS):
                total = total + lane_roll(face, SPOTS * j)
            total = total * (1.0 / (ROWS * BLOCKS) ** 2)
            moment = jnp.stack([cross_roll(total, -g) for g in range(GROUPS)])
            springs[...] = SPRING_KEEP * springs[...] + SPRING_DRIVE * touching * moment
            return carry

        for step in range(OUTER):
            outer_step(step, 0)

        for g in range(GROUPS):
            turned[g] = field[:, g].reshape(LANES, LANES).T
        flat_result = result.reshape(BLOCKS * ROOM, LANES)
        for at in range(OWN):
            i, g = divmod(MARGIN + at, GROUPS)
            for half in range(2):
                flat_result[pl.ds(at + half * 8 * ROOM, 8, stride=ROOM), :] = (
                    turned[g, pl.ds(i + half * 8 * SPOTS, 8, stride=SPOTS), :]
                )
        spring_row = jnp.zeros((8, LANES), F32)
        for g in range(GROUPS):
            spread = jnp.take_along_axis(
                springs[g], (MARGIN + lane % OWN) // GROUPS, axis=1
            )
            spring_row = jnp.where(lane % GROUPS == g, spread, spring_row)
        result[:, OWN:] = jnp.broadcast_to(spring_row[None], (BLOCKS, 8, LANES))

        def give_back(device):
            pltpu.make_async_remote_copy(
                src_ref=result.at[device, pl.ds(0, SENT)], dst_ref=returned.at[mine, pl.ds(0, SENT)],
                send_sem=return_send.at[0], recv_sem=return_sem.at[0],
                device_id=(wall, device), device_id_type=MESH,
            ).start()

        for device in EARLY_FIRST:
            pl.when(me != device)(functools.partial(give_back, device))
        pltpu.make_async_copy(
            result.at[me, pl.ds(0, SENT)], returned.at[mine, pl.ds(0, SENT)], return_sem.at[0]
        ).start()

    def wait_dealt(count):
        sent = landed.reshape(3 * BLOCKS * WIDE, LANES).at[pl.ds(0, count * sum(WIDTHS))]
        pltpu.make_async_copy(sent, sent, send_sem.at[0]).wait()

    @pl.when(solves)
    def _():
        wait_dealt(SOLVERS - 1)

    @pl.when(jnp.logical_not(solves))
    def _():
        wait_dealt(SOLVERS)

    @pl.when(has_right)
    def _():
        for which in (LAYER, PRESSURE, LOADING):
            to_right(which).wait_send()

    @pl.when(has_left)
    def _():
        for which in (LAYER, PRESSURE, LOADING):
            to_left(which).wait_send()

    @pl.when(first & has_right)
    def _():
        wall_right.wait_send()

    @pl.when(last & has_left)
    def _():
        wall_left.wait_send()

    @pl.when(solves)
    def _():
        given = result.reshape(BLOCKS * ROOM, LANES).at[pl.ds(0, (BLOCKS - 1) * SENT)]
        pltpu.make_async_copy(given, given, return_send.at[0]).wait()

    back_here = returned.at[:, pl.ds(0, SENT)]
    pltpu.make_async_copy(back_here, back_here, return_sem.at[0]).wait()


def place_rows(returned, pressure_out, spring_out):
    planes = returned[:, 0:OWN].reshape(LANES, LANES).T
    flat = pressure_out.reshape(CROSS * ROWS, LANES)
    for z in range(ROWS):
        flat[pl.ds(z, CROSS, stride=ROWS), :] = planes[z * CROSS:(z + 1) * CROSS]
    owner = lax.broadcasted_iota(jnp.int32, (1, LANES), 1) // OWN
    total = jnp.zeros((1, LANES), F32)
    for d in range(SOLVERS):
        total = jnp.where(owner == d, returned[d, OWN:OWN + 1], total)
    spring_out[...] = total.reshape(spring_out.shape)


def lane_roll_by(x, shift):
    return pltpu.roll(x, shift, x.ndim - 1)


def on_device(pressure, layer, permeability, loading, spring, contact):
    vmem = pl.BlockSpec(memory_space=pltpu.VMEM)
    hbm = pl.BlockSpec(memory_space=pltpu.MemorySpace.HBM)
    planes = pltpu.VMEM((ROWS, GROUPS, CROSS, LANES), F32)
    plane = pltpu.VMEM((GROUPS, CROSS, LANES), F32)
    tile = pltpu.VMEM((8, LANES), F32)
    returned = pl.pallas_call(
        kernel,
        out_shape=jax.ShapeDtypeStruct((SOLVERS, ROOM, LANES), F32),
        in_specs=[hbm] * 6,
        out_specs=hbm,
        scratch_shapes=[
            pltpu.SMEM(permeability.shape, F32),
            pltpu.SMEM(contact.shape, jnp.int32),
            pltpu.VMEM(pressure.shape, F32),
            pltpu.VMEM(layer.shape, jnp.int32),
            pltpu.VMEM(loading.shape, F32),
            pltpu.VMEM(spring.shape, F32),
            pltpu.SemaphoreType.DMA((6,)),
            pltpu.VMEM((3, LANES + 2 * MARGIN, LANES), F32),
            pltpu.VMEM((3, BLOCKS, WIDE, LANES), F32),
            pltpu.VMEM((3, BLOCKS, MARGIN, LANES), F32),
            tile, tile,
            planes, planes, planes, planes, planes, planes,
            planes, planes, planes, planes,
            planes, planes, planes, planes, plane, plane,
            pltpu.VMEM((GROUPS, LANES, LANES), F32),
            pltpu.VMEM((BLOCKS, ROOM, LANES), F32),
            pltpu.SemaphoreType.DMA((1,)),
            pltpu.SemaphoreType.DMA((3,)),
            pltpu.SemaphoreType.DMA((2, 3)),
            pltpu.SemaphoreType.DMA((3,)),
            pltpu.SemaphoreType.DMA((1,)),
            pltpu.SemaphoreType.DMA((2,)),
            pltpu.SemaphoreType.DMA((1,)),
            pltpu.SemaphoreType.DMA((1,)),
        ],
        compiler_params=pltpu.CompilerParams(
            collective_id=0, has_side_effects=True, vmem_limit_bytes=60 << 20
        ),
    )(permeability, contact, pressure, layer, loading, spring)
    return pl.pallas_call(
        place_rows,
        out_shape=(
            jax.ShapeDtypeStruct(pressure.shape, F32),
            jax.ShapeDtypeStruct(spring.shape, F32),
        ),
        in_specs=[vmem],
        out_specs=(vmem, vmem),
    )(returned)


def solution(mesh):
    cells = P(None, "depth", "wall")
    return jax.shard_map(
        on_device,
        mesh=mesh,
        in_specs=(cells, cells, P(), cells, P("wall"), P("wall")),
        out_specs=(cells, P("wall")),
        check_vma=False,
    )
```

```python
import functools

import jax
import jax.numpy as jnp
from jax import lax
from jax.experimental import pallas as pl
from jax.experimental.pallas import tpu as pltpu
from jax.sharding import PartitionSpec as P

MESH = pl.DeviceIdType.MESH
F32 = jnp.float32

SOILS = 8
PANEL = 16
SUBSTEPS = 3
OUTER = 2
VNUM = 512.0
ALONG_RATE = 0.1
ACROSS_RATE = 0.06
SPRING_KEEP = 0.5
SPRING_DRIVE = 2.0

CROSS = 8
ROWS = 16
BLOCKS = 16
SOLVERS = 8
MOVED = 1
OWN = 16
MARGIN = 8
WIDE = OWN + 2 * MARGIN
SPOTS = 8
GROUPS = 4
LANES = 128
LAST = ROWS - 1
MIDDLE = 7
LAYER, PRESSURE, LOADING = 0, 1, 2
HALO = (5, 6, 5)
WIDTHS = tuple(OWN + 2 * halo for halo in HALO)
SIDE = 4
FAR_FIRST = sorted(
    ((dy, dx) for dy in range(SIDE) for dx in range(SIDE) if dy or dx),
    key=lambda at: -sum(min(step, SIDE - step) for step in at),
)
EARLY_FIRST = sorted(range(BLOCKS), key=lambda device: device // SIDE + device % SIDE)
SENT = OWN + 1
ROOM = OWN + 8


def lane_roll(x, shift):
    return pltpu.roll(x, shift % LANES, x.ndim - 1)


def cross_roll(x, shift):
    return pltpu.roll(x, shift % CROSS, x.ndim - 2)


def harmonic(a, b):
    return (2.0 * VNUM) * a * b / (a + b)


def pick(level, table, row):
    value = jnp.full(level.shape, table[row, 0], F32)
    for soil in range(1, SOILS):
        value = jnp.where(level == float(soil), table[row, soil], value)
    return value


def kernel(
    table_in, contact_in, pressure_in, layer_in, loading_in, spring_in,
    returned,
    table, contact, pressure, layer, loading, spring, in_sem,
    packed, landed, beyond, wall_mine, wall_beside,
    field, source, keep, along, back, ahead, chain, outward, from_prev, from_last,
    last_end, last_start, prev_end, prev_start, sep_up, springs,
    turned, result,
    send_sem, land_sem, side_send, side_sem, wall_sem, wall_send, return_send, return_sem,
):
    wall, me = lax.axis_index("wall"), lax.axis_index("depth")
    walls = lax.axis_size("wall")
    has_left, has_right = wall > 0, wall < walls - 1

    def spot_of(device):
        row, at = device // SIDE, device % SIDE
        place = lax.rem(2 * row + at % 2 + SOLVERS - MOVED, SOLVERS)
        return jnp.where(at // 2 == lax.rem(wall, 2), place, SOLVERS)

    def device_of(spot, wall):
        place = (spot + MOVED) % SOLVERS
        return place // 2 * SIDE + 2 * lax.rem(wall, 2) + place % 2

    mine = spot_of(me)
    solves, first, last = mine < SOLVERS, mine == 0, mine == SOLVERS - 1
    left_end = (wall - 1, device_of(SOLVERS - 1, wall + 1))
    right_end = (wall + 1, device_of(0, wall + 1))

    inputs = [
        pltpu.make_async_copy(source_ref, here, in_sem.at[at])
        for at, (source_ref, here) in enumerate((
            (layer_in, layer), (pressure_in, pressure), (loading_in, loading),
            (spring_in, spring), (contact_in, contact), (table_in, table),
        ))
    ]
    for copy in inputs:
        copy.start()

    peers = [
        lax.rem(me // SIDE + dy, SIDE) * SIDE + lax.rem(me % SIDE + dx, SIDE) for dy, dx in FAR_FIRST
    ]

    barrier = pltpu.get_barrier_semaphore()

    @pl.when(solves)
    def _():
        for peer in peers:
            pl.semaphore_signal(barrier, inc=1, device_id=(wall, peer), device_id_type=MESH)

    @pl.when(first & has_left)
    def _():
        for k in reversed(range(BLOCKS)):
            pl.semaphore_signal(barrier, inc=1, device_id=(wall - 1, k), device_id_type=MESH)

    @pl.when(last & has_right)
    def _():
        for k in reversed(range(BLOCKS)):
            pl.semaphore_signal(barrier, inc=1, device_id=(wall + 1, k), device_id_type=MESH)

    def pack(which, ref):
        inputs[which].wait()
        flat = ref.reshape(CROSS * ROWS, LANES)
        planes = [flat[pl.ds(z, CROSS, stride=ROWS), :] for z in range(ROWS)]
        packed[which, MARGIN:MARGIN + LANES] = jnp.concatenate(planes, 0).astype(F32).T

    def to_peer(which, peer):
        width = OWN + 2 * HALO[which]
        return pltpu.make_async_remote_copy(
            src_ref=packed.at[which, pl.ds(spot_of(peer) * OWN + MARGIN - HALO[which], width)],
            dst_ref=landed.at[which, me, pl.ds(MARGIN - HALO[which], width)],
            send_sem=send_sem.at[0], recv_sem=land_sem.at[which],
            device_id=(wall, peer), device_id_type=MESH,
        )

    def to_self(which):
        width = OWN + 2 * HALO[which]
        return pltpu.make_async_copy(
            packed.at[which, pl.ds(mine * OWN + MARGIN - HALO[which], width)],
            landed.at[which, me, pl.ds(MARGIN - HALO[which], width)],
            land_sem.at[which],
        )

    def to_right(which):
        return pltpu.make_async_remote_copy(
            src_ref=packed.at[which, pl.ds(MARGIN + LANES - HALO[which], HALO[which])],
            dst_ref=beyond.at[which, me, pl.ds(MARGIN - HALO[which], HALO[which])],
            send_sem=side_send.at[0, which], recv_sem=side_sem.at[which],
            device_id=right_end, device_id_type=MESH,
        )

    def to_left(which):
        return pltpu.make_async_remote_copy(
            src_ref=packed.at[which, pl.ds(MARGIN, HALO[which])],
            dst_ref=beyond.at[which, me, pl.ds(0, HALO[which])],
            send_sem=side_send.at[1, which], recv_sem=side_sem.at[which],
            device_id=left_end, device_id_type=MESH,
        )

    for which in (LAYER, PRESSURE, LOADING):
        packed[which, 0:MARGIN] = jnp.zeros((MARGIN, LANES), F32)
        packed[which, MARGIN + LANES:] = jnp.zeros((MARGIN, LANES), F32)
    pack(LAYER, layer)
    pack(PRESSURE, pressure)
    pack(LOADING, loading)
    sides = has_left.astype(jnp.int32) + has_right.astype(jnp.int32)
    pl.semaphore_wait(barrier, SOLVERS - solves.astype(jnp.int32) + sides)

    @pl.when(has_right)
    def _():
        for which in (LAYER, PRESSURE, LOADING):
            to_right(which).start()

    @pl.when(has_left)
    def _():
        for which in (LAYER, PRESSURE, LOADING):
            to_left(which).start()

    def deal(peer, *arrays):
        @pl.when(spot_of(peer) < SOLVERS)
        def _():
            for which in arrays:
                to_peer(which, peer).start()

    for peer in peers:
        deal(peer, LAYER)
    for copy in inputs[LOADING + 1:]:
        copy.wait()
    lane = lax.broadcasted_iota(jnp.int32, (8, LANES), 1)
    sub = lax.broadcasted_iota(jnp.int32, (8, LANES), 0)
    share = jnp.zeros((8, LANES), F32)
    for panel in range(LANES // PANEL):
        share = jnp.where(lane // PANEL == panel, contact[panel].astype(F32), share)
    own_spring = jnp.broadcast_to(spring[...].reshape(1, LANES), (8, LANES))
    wall_mine[...] = jnp.where(sub == 0, own_spring, share)
    wall_right = pltpu.make_async_remote_copy(
        src_ref=wall_mine, dst_ref=wall_beside, send_sem=wall_send.at[0], recv_sem=wall_sem.at[0],
        device_id=right_end, device_id_type=MESH,
    )
    wall_left = pltpu.make_async_remote_copy(
        src_ref=wall_mine, dst_ref=wall_beside, send_sem=wall_send.at[1], recv_sem=wall_sem.at[0],
        device_id=left_end, device_id_type=MESH,
    )

    @pl.when(first & has_right)
    def _():
        wall_right.start()

    @pl.when(last & has_left)
    def _():
        wall_left.start()

    for peer in peers:
        deal(peer, PRESSURE, LOADING)

    @pl.when(solves)
    def _():
        for which in (LAYER, PRESSURE, LOADING):
            to_self(which).start()

    @pl.when(solves)
    def _():
        wide = (GROUPS, CROSS, LANES)
        lanes = lax.broadcasted_iota(jnp.int32, wide, 2)
        block = lanes // SPOTS
        column = GROUPS * (lanes % SPOTS) + lax.broadcasted_iota(jnp.int32, wide, 0)
        cross = lax.broadcasted_iota(jnp.int32, wide, 1)
        place = wall * LANES + mine * OWN - MARGIN + column
        inside = (place >= 0) & (place < walls * LANES)
        top, bottom = block == 0, block == BLOCKS - 1

        def arrived(which):
            valid = landed.at[which, :, pl.ds(MARGIN - HALO[which], OWN + 2 * HALO[which])]
            pltpu.make_async_copy(valid, valid, land_sem.at[which]).wait()

            @pl.when((first & has_left) | (last & has_right))
            def _():
                strip = beyond.at[which, :, pl.ds(0, HALO[which])]
                pltpu.make_async_copy(strip, strip, side_sem.at[which]).wait()

            @pl.when(first)
            def _():
                landed[which, :, 0:MARGIN] = jnp.where(has_left, beyond[which], 0.0)

            @pl.when(last)
            def _():
                landed[which, :, OWN + MARGIN:] = jnp.where(has_right, beyond[which], 0.0)

            for g in range(GROUPS):
                rows = [landed[which, s, pl.ds(g, SPOTS, stride=GROUPS), :] for s in range(BLOCKS)]
                planes = jnp.concatenate(rows, 0).T.reshape(ROWS, CROSS, LANES)
                field_or = source if which == LOADING else field
                field_or[:, g] = planes

        arrived(LAYER)
        perm = [pick(field[z], table, 0) for z in range(ROWS)]
        up = [None] * ROWS
        for z in range(1, ROWS):
            up[z] = harmonic(perm[z - 1], perm[z])
        up[0] = jnp.where(top, VNUM * perm[0], harmonic(lane_roll(perm[LAST], SPOTS), perm[0]))
        down = up[1:] + [jnp.where(bottom, 0.0, lane_roll(up[0], -SPOTS))]
        diagonal = [1.0 + up[z] + down[z] for z in range(ROWS)]

        inverse, toward = [None] * ROWS, [None] * ROWS
        chained = [None] * ROWS
        for z in range(MIDDLE):
            pivot = diagonal[z] if z == 0 else diagonal[z] - up[z] * toward[z - 1]
            inverse[z] = 1.0 / pivot
            toward[z] = down[z] * inverse[z]
            chained[z] = up[z] * inverse[z]
        for z in range(LAST - 1, MIDDLE, -1):
            pivot = diagonal[z] if z == LAST - 1 else diagonal[z] - down[z] * toward[z + 1]
            inverse[z] = 1.0 / pivot
            toward[z] = up[z] * inverse[z]
            chained[z] = down[z] * inverse[z]
        inverse[MIDDLE] = 1.0 / (
            diagonal[MIDDLE] - up[MIDDLE] * toward[MIDDLE - 1] - down[MIDDLE] * toward[MIDDLE + 1]
        )
        chained[MIDDLE] = up[MIDDLE] * inverse[MIDDLE]
        toward[MIDDLE] = down[MIDDLE] * inverse[MIDDLE]
        inverse[LAST] = jnp.ones(wide, F32)

        upper, lower = [None] * LAST, [None] * LAST
        upper[0] = jnp.where(top, 0.0, chained[0])
        for z in range(1, MIDDLE):
            upper[z] = chained[z] * upper[z - 1]
        upper[MIDDLE] = chained[MIDDLE] * upper[MIDDLE - 1]
        for z in range(MIDDLE - 1, -1, -1):
            upper[z] = upper[z] + toward[z] * upper[z + 1]
        for z in range(MIDDLE + 1, LAST):
            upper[z] = toward[z] * upper[z - 1]
        lower[LAST - 1] = chained[LAST - 1]
        for z in range(LAST - 2, MIDDLE, -1):
            lower[z] = chained[z] * lower[z + 1]
        lower[MIDDLE] = toward[MIDDLE] * lower[MIDDLE + 1]
        for z in range(MIDDLE + 1, LAST):
            lower[z] = lower[z] + toward[z] * lower[z - 1]
        for z in range(MIDDLE - 1, -1, -1):
            lower[z] = toward[z] * lower[z + 1]
        for z in range(LAST):
            chain[z], outward[z] = chained[z], toward[z]
            from_prev[z], from_last[z] = upper[z], lower[z]

        a_coef = up[LAST] * upper[LAST - 1]
        c_coef = down[LAST] * lane_roll(lower[0], -SPOTS)
        b_coef = diagonal[LAST] - up[LAST] * lower[LAST - 1] - down[LAST] * lane_roll(upper[0], -SPOTS)
        sep_up[...] = up[LAST]
        coefs = {0: jnp.ones(wide, F32)}
        for level in range(4):
            step = 1 << level
            hop = SPOTS * step
            b_inv = 1.0 / b_coef
            alpha = a_coef * lane_roll(b_inv, hop)
            gamma = c_coef * lane_roll(b_inv, -hop)
            b_coef = b_coef - alpha * lane_roll(c_coef, hop) - gamma * lane_roll(a_coef, -hop)
            a_coef, c_coef = alpha * lane_roll(a_coef, hop), gamma * lane_roll(c_coef, -hop)
            longer = dict(coefs)
            for j, coef in coefs.items():
                if 2 * step == BLOCKS:
                    moved = [((j + step) % BLOCKS, (alpha + gamma) * lane_roll(coef, hop))]
                else:
                    moved = [
                        ((j + step) % BLOCKS, alpha * lane_roll(coef, hop)),
                        ((j - step) % BLOCKS, gamma * lane_roll(coef, -hop)),
                    ]
                for at, term in moved:
                    longer[at] = longer[at] + term if at in longer else term
            coefs = longer
        b_inv = 1.0 / b_coef
        for j in range(BLOCKS):
            by_end = coefs[j] * b_inv
            by_start = by_end * lane_roll(down[LAST], SPOTS * j)
            last_end[j], last_start[(j - 1) % BLOCKS] = by_end, by_start
            prev_end[(j + 1) % BLOCKS], prev_start[j] = lane_roll(by_end, SPOTS), lane_roll(by_start, SPOTS)

        @pl.when((first & has_left) | (last & has_right))
        def _():
            pltpu.make_async_copy(wall_beside, wall_beside, wall_sem.at[0]).wait()

        @pl.when(jnp.logical_not((first & has_left) | (last & has_right)))
        def _():
            wall_beside[...] = jnp.zeros_like(wall_beside)

        beside = (first & (lane >= LANES - MARGIN)) | (last & (lane < MARGIN))
        window = jnp.where(beside, wall_beside[...], wall_mine[...])
        window = lane_roll_by(window, lax.rem(2 * LANES + MARGIN - mine * OWN, LANES))
        touching = []
        for g in range(GROUPS):
            spread = jnp.take_along_axis(window, GROUPS * (lane % SPOTS) + g, axis=1)
            springs[g] = jnp.broadcast_to(spread[0:1], (CROSS, LANES))
            touching.append(jnp.broadcast_to(spread[1:2], (CROSS, LANES)))
        touching = jnp.stack(touching)

        ahead_mask = (cross < CROSS - 1).astype(F32)
        back_mask = jnp.where(cross > 0, 1.0, touching)
        for z in range(ROWS):
            lateral = jnp.where(inside, pick(field[z], table, 1), 0.0)
            a1 = ALONG_RATE * lateral
            a2 = ACROSS_RATE * lateral
            a2b, a2a = a2 * back_mask, a2 * ahead_mask
            keep[z] = (1.0 - 2.0 * a1 - a2b - a2a) * inverse[z]
            along[z], back[z], ahead[z] = a1 * inverse[z], a2b * inverse[z], a2a * inverse[z]
        arrived(PRESSURE)
        arrived(LOADING)
        for z in range(ROWS):
            source[z] = source[z] * inverse[z]

        def solve(_, carry):
            spring_now = springs[...]
            scaled = []
            for z in range(ROWS):
                now = field[z]
                left = jnp.stack([lane_roll(now[3], 1), now[0], now[1], now[2]])
                right = jnp.stack([now[1], now[2], now[3], lane_roll(now[0], -1)])
                behind = jnp.where(cross == 0, spring_now, cross_roll(now, 1))
                scaled.append(
                    source[z] + keep[z] * now + along[z] * (left + right)
                    + back[z] * behind + ahead[z] * cross_roll(now, -1)
                )
            for z in range(1, MIDDLE):
                scaled[z] = scaled[z] + chain[z] * scaled[z - 1]
            for z in range(LAST - 2, MIDDLE, -1):
                scaled[z] = scaled[z] + chain[z] * scaled[z + 1]
            scaled[MIDDLE] = (
                scaled[MIDDLE] + chain[MIDDLE] * scaled[MIDDLE - 1] + outward[MIDDLE] * scaled[MIDDLE + 1]
            )
            for z in range(MIDDLE - 1, -1, -1):
                scaled[z] = scaled[z] + outward[z] * scaled[z + 1]
            for z in range(MIDDLE + 1, LAST):
                scaled[z] = scaled[z] + outward[z] * scaled[z - 1]
            end, start = scaled[LAST] + sep_up[...] * scaled[LAST - 1], scaled[0]
            ends, above = jnp.zeros(wide, F32), jnp.zeros(wide, F32)
            for j in range(BLOCKS):
                end_there, start_there = lane_roll(end, SPOTS * j), lane_roll(start, SPOTS * j)
                ends = ends + last_end[j] * end_there + last_start[j] * start_there
                above = above + prev_end[j] * end_there + prev_start[j] * start_there
            for z in range(LAST):
                field[z] = scaled[z] + from_prev[z] * above + from_last[z] * ends
            field[LAST] = ends
            return carry

        def outer_step(_, carry):
            lax.fori_loop(0, SUBSTEPS, solve, 0, unroll=True)
            base = ROWS * block.astype(F32) + 0.5
            moment = jnp.zeros(wide, F32)
            for z in range(ROWS):
                moment = moment + (base + float(z)) * field[z]
            row = lax.broadcasted_iota(jnp.int32, (CROSS, LANES), 0)
            face = jnp.where(row == 0, moment[0], 0.0)
            for g in range(1, GROUPS):
                face = jnp.where(row == g, cross_roll(moment[g], g), face)
            total = face
            for j in range(1, BLOCKS):
                total = total + lane_roll(face, SPOTS * j)
            total = total * (1.0 / (ROWS * BLOCKS) ** 2)
            moment = jnp.stack([cross_roll(total, -g) for g in range(GROUPS)])
            springs[...] = SPRING_KEEP * springs[...] + SPRING_DRIVE * touching * moment
            return carry

        for step in range(OUTER):
            outer_step(step, 0)

        for g in range(GROUPS):
            turned[g] = field[:, g].reshape(LANES, LANES).T
        flat_result = result.reshape(BLOCKS * ROOM, LANES)
        for at in range(OWN):
            i, g = divmod(MARGIN + at, GROUPS)
            for half in range(2):
                flat_result[pl.ds(at + half * 8 * ROOM, 8, stride=ROOM), :] = (
                    turned[g, pl.ds(i + half * 8 * SPOTS, 8, stride=SPOTS), :]
                )
        spring_row = jnp.zeros((8, LANES), F32)
        for g in range(GROUPS):
            spread = jnp.take_along_axis(
                springs[g], (MARGIN + lane % OWN) // GROUPS, axis=1
            )
            spring_row = jnp.where(lane % GROUPS == g, spread, spring_row)
        result[:, OWN:] = jnp.broadcast_to(spring_row[None], (BLOCKS, 8, LANES))

        def give_back(device):
            pltpu.make_async_remote_copy(
                src_ref=result.at[device, pl.ds(0, SENT)], dst_ref=returned.at[mine, pl.ds(0, SENT)],
                send_sem=return_send.at[0], recv_sem=return_sem.at[0],
                device_id=(wall, device), device_id_type=MESH,
            ).start()

        for device in EARLY_FIRST:
            pl.when(me != device)(functools.partial(give_back, device))
        pltpu.make_async_copy(
            result.at[me, pl.ds(0, SENT)], returned.at[mine, pl.ds(0, SENT)], return_sem.at[0]
        ).start()

    def wait_dealt(count):
        sent = landed.reshape(3 * BLOCKS * WIDE, LANES).at[pl.ds(0, count * sum(WIDTHS))]
        pltpu.make_async_copy(sent, sent, send_sem.at[0]).wait()

    @pl.when(solves)
    def _():
        wait_dealt(SOLVERS - 1)

    @pl.when(jnp.logical_not(solves))
    def _():
        wait_dealt(SOLVERS)

    @pl.when(has_right)
    def _():
        for which in (LAYER, PRESSURE, LOADING):
            to_right(which).wait_send()

    @pl.when(has_left)
    def _():
        for which in (LAYER, PRESSURE, LOADING):
            to_left(which).wait_send()

    @pl.when(first & has_right)
    def _():
        wall_right.wait_send()

    @pl.when(last & has_left)
    def _():
        wall_left.wait_send()

    @pl.when(solves)
    def _():
        given = result.reshape(BLOCKS * ROOM, LANES).at[pl.ds(0, (BLOCKS - 1) * SENT)]
        pltpu.make_async_copy(given, given, return_send.at[0]).wait()

    back_here = returned.at[:, pl.ds(0, SENT)]
    pltpu.make_async_copy(back_here, back_here, return_sem.at[0]).wait()


def place_rows(returned, pressure_out, spring_out):
    planes = returned[:, 0:OWN].reshape(LANES, LANES).T
    flat = pressure_out.reshape(CROSS * ROWS, LANES)
    for z in range(ROWS):
        flat[pl.ds(z, CROSS, stride=ROWS), :] = planes[z * CROSS:(z + 1) * CROSS]
    owner = lax.broadcasted_iota(jnp.int32, (1, LANES), 1) // OWN
    total = jnp.zeros((1, LANES), F32)
    for d in range(SOLVERS):
        total = jnp.where(owner == d, returned[d, OWN:OWN + 1], total)
    spring_out[...] = total.reshape(spring_out.shape)


def lane_roll_by(x, shift):
    return pltpu.roll(x, shift, x.ndim - 1)


def on_device(pressure, layer, permeability, loading, spring, contact):
    vmem = pl.BlockSpec(memory_space=pltpu.VMEM)
    hbm = pl.BlockSpec(memory_space=pltpu.MemorySpace.HBM)
    planes = pltpu.VMEM((ROWS, GROUPS, CROSS, LANES), F32)
    plane = pltpu.VMEM((GROUPS, CROSS, LANES), F32)
    tile = pltpu.VMEM((8, LANES), F32)
    returned = pl.pallas_call(
        kernel,
        out_shape=jax.ShapeDtypeStruct((SOLVERS, ROOM, LANES), F32),
        in_specs=[hbm] * 6,
        out_specs=hbm,
        scratch_shapes=[
            pltpu.SMEM(permeability.shape, F32),
            pltpu.SMEM(contact.shape, jnp.int32),
            pltpu.VMEM(pressure.shape, F32),
            pltpu.VMEM(layer.shape, jnp.int32),
            pltpu.VMEM(loading.shape, F32),
            pltpu.VMEM(spring.shape, F32),
            pltpu.SemaphoreType.DMA((6,)),
            pltpu.VMEM((3, LANES + 2 * MARGIN, LANES), F32),
            pltpu.VMEM((3, BLOCKS, WIDE, LANES), F32),
            pltpu.VMEM((3, BLOCKS, MARGIN, LANES), F32),
            tile, tile,
            planes, planes, planes, planes, planes, planes,
            planes, planes, planes, planes,
            planes, planes, planes, planes, plane, plane,
            pltpu.VMEM((GROUPS, LANES, LANES), F32),
            pltpu.VMEM((BLOCKS, ROOM, LANES), F32),
            pltpu.SemaphoreType.DMA((1,)),
            pltpu.SemaphoreType.DMA((3,)),
            pltpu.SemaphoreType.DMA((2, 3)),
            pltpu.SemaphoreType.DMA((3,)),
            pltpu.SemaphoreType.DMA((1,)),
            pltpu.SemaphoreType.DMA((2,)),
            pltpu.SemaphoreType.DMA((1,)),
            pltpu.SemaphoreType.DMA((1,)),
        ],
        compiler_params=pltpu.CompilerParams(
            collective_id=0, has_side_effects=True, vmem_limit_bytes=60 << 20
        ),
    )(permeability, contact, pressure, layer, loading, spring)
    return pl.pallas_call(
        place_rows,
        out_shape=(
            jax.ShapeDtypeStruct(pressure.shape, F32),
            jax.ShapeDtypeStruct(spring.shape, F32),
        ),
        in_specs=[vmem],
        out_specs=(vmem, vmem),
    )(returned)


def solution(mesh):
    cells = P(None, "depth", "wall")
    return jax.shard_map(
        on_device,
        mesh=mesh,
        in_specs=(cells, cells, P(), cells, P("wall"), P("wall")),
        out_specs=(cells, P("wall")),
        check_vma=False,
    )
```
